128 devices in a mesh: row: 8 (over y_lo, x), col: 16 (over z, y_hi, core).
Axes of the slice: x: 4, y: 4 (y_hi: 2, y_lo: 2; y = y_hi * 2 + y_lo), z: 4, core: 2. Of those that a mesh axis runs over, the one named last changes fastest.
Arguments:
- tokens: bfloat16 [128, 512, 256], P('row', 'col'), may hold values from -6 to 6
- target: bfloat16 [128, 512, 256], P('row', 'col'), may hold values from -6 to 6
- block_qkv: bfloat16 [256, 768], replicated, may hold values from -0.375 to 0.375
- block_out: bfloat16 [256, 256], replicated, may hold values from -0.375 to 0.375
- grid_qkv: bfloat16 [256, 768], replicated, may hold values from -0.375 to 0.375
- grid_out: bfloat16 [256, 256], replicated, may hold values from -0.375 to 0.375
- mlp_in: bfloat16 [256, 1024], replicated, may hold values from -0.375 to 0.375
- mlp_out: bfloat16 [1024, 256], replicated, may hold values from -0.1875 to 0.1875
- probe_block_qkv: int32 [9, 768], replicated, may hold values from 0 to 1073741823
- probe_block_out: int32 [9, 256], replicated, may hold values from 0 to 1073741823
- probe_grid_qkv: int32 [9, 768], replicated, may hold values from 0 to 1073741823
- probe_grid_out: int32 [9, 256], replicated, may hold values from 0 to 1073741823
- probe_mlp_in: int32 [9, 1024], replicated, may hold values from 0 to 1073741823
- probe_mlp_out: int32 [35, 256], replicated, may hold values from 0 to 1073741823
Outputs:
- hv_block_qkv: float32 [256, 768], replicated
- hv_block_out: float32 [256, 256], replicated
- hv_grid_qkv: float32 [256, 768], replicated
- hv_grid_out: float32 [256, 256], replicated
- hv_mlp_in: float32 [256, 1024], replicated
- hv_mlp_out: float32 [1024, 256], replicated
- trace_terms: float32 [6], replicated
The draws below stay inside these ranges and needn't reach their ends.
All inputs are finite; a program needn't handle non-finite values.
Results may differ from the reference program's by a relative error of at most 0.035.
Values may be sent and summed in bfloat16 or wider, within the bound.
No kernel may reach another device: no remote copies, remote signals or barrier semaphores. Data moves between devices by JAX's collectives and lax.ppermute only.
A program may use at most 128 MiB of HBM per device.

```python
import math
import jax
import jax.numpy as jnp
from jax import lax

D = 256
FF = 1024
HEADS = 8
HD = 32
SLAB_ROWS = 128
SLAB_COLS = 512
D_WORDS = 9
FF_WORDS = 35


def set_ends(array, own_key, smallest, high):
    extent = array.shape
    spot = [jax.random.randint(jax.random.fold_in(own_key, axis), (), 0, extent[axis]) for axis in range(len(extent))]
    array = array.at[tuple(spot)].set(smallest)
    longest = extent.index(max(extent))
    spot[longest] = (spot[longest] + 1) % extent[longest]
    return array.at[tuple(spot)].set(high)


def levels(key, extent, pieces, least, high):
    def one(position, shards_of):
        heights = jax.random.uniform(jax.random.fold_in(jax.random.fold_in(key, 6), position), (shards_of,), jnp.float32, least / len(pieces), high / len(pieces))
        return jnp.repeat(jnp.exp(heights), extent[position] // shards_of).reshape((-1,) + (1,) * (len(extent) - position - 1))

    loudness = one(*pieces[0])
    for cut in pieces[1:]:
        loudness = loudness * one(*cut)
    return loudness


def normal_values(rng, dims, scale, most, pieces=(), held_as=jnp.bfloat16):
    array = jax.random.normal(rng, dims, jnp.float32) * scale
    if len(pieces) > 0:
        array = levels(rng, dims, pieces, -0.22, 0.18) * array
    return jnp.clip(array, min=-most, max=most).astype(held_as)


def setup_inputs(seed: int = 0) -> dict:
    seeds = jax.random.split(jax.random.key(seed), 15)
    return {
        "tokens": normal_values(seeds[0], (SLAB_ROWS, SLAB_COLS, D), 1.0, 6.0, ((0, 8), (1, 16))),
        "target": normal_values(seeds[1], (SLAB_ROWS, SLAB_COLS, D), 1.0, 6.0, ((0, 8), (1, 16))),
        "block_qkv": normal_values(seeds[2], (D, 3 * D), D ** -0.5, 0.375),
        "block_out": normal_values(seeds[3], (D, D), D ** -0.5, 0.375),
        "grid_qkv": normal_values(seeds[4], (D, 3 * D), D ** -0.5, 0.375),
        "grid_out": normal_values(seeds[5], (D, D), D ** -0.5, 0.375),
        "mlp_in": normal_values(seeds[6], (D, FF), D ** -0.5, 0.375),
        "mlp_out": normal_values(seeds[7], (FF, D), FF ** -0.5, 0.1875),
        "probe_block_qkv": set_ends(jax.random.randint(seeds[8], (D_WORDS, 3 * D), 0, 1073741824), jax.random.fold_in(seeds[8], 1), 0, 1073741823).astype(jnp.int32),
        "probe_block_out": set_ends(jax.random.randint(seeds[9], (D_WORDS, D), 0, 1073741824), jax.random.fold_in(seeds[9], 1), 0, 1073741823).astype(jnp.int32),
        "probe_grid_qkv": set_ends(jax.random.randint(seeds[10], (D_WORDS, 3 * D), 0, 1073741824), jax.random.fold_in(seeds[10], 1), 0, 1073741823).astype(jnp.int32),
        "probe_grid_out": set_ends(jax.random.randint(seeds[11], (D_WORDS, D), 0, 1073741824), jax.random.fold_in(seeds[11], 1), 0, 1073741823).astype(jnp.int32),
        "probe_mlp_in": set_ends(jax.random.randint(seeds[12], (D_WORDS, FF), 0, 1073741824), jax.random.fold_in(seeds[12], 1), 0, 1073741823).astype(jnp.int32),
        "probe_mlp_out": set_ends(jax.random.randint(seeds[13], (FF_WORDS, D), 0, 1073741824), jax.random.fold_in(seeds[13], 1), 0, 1073741823).astype(jnp.int32),
    }


EPSILON = 1e-05

def normalize(values):
    center = values - lax.optimization_barrier(jnp.mean(values, axis=-1, keepdims=True))
    spread = lax.optimization_barrier(jnp.mean(center * center, axis=-1, keepdims=True))
    return center * lax.rsqrt(spread + EPSILON)

def unpack_signs(words, row_total):
    shifts = jnp.arange(30, dtype=jnp.int32)
    flags = jnp.right_shift(words[:, None, :], shifts[None, :, None]) & 1
    flags = flags.reshape(-1, words.shape[1])[:row_total]
    return (1 - 2 * flags).astype(jnp.bfloat16)

def window_attention(features, qkv_weight, out_weight, dilated):
    height, breadth, channels = features.shape
    if dilated:
        windows = features.reshape(8, height // 8, 8, breadth // 8, channels).transpose(1, 3, 0, 2, 4)
    else:
        windows = features.reshape(height // 8, 8, breadth // 8, 8, channels).transpose(0, 2, 1, 3, 4)
    windows = windows.reshape(-1, 64, channels).astype(jnp.float32)
    project = jnp.einsum('wtd,de->wte', windows, qkv_weight.astype(jnp.float32)).astype(jnp.bfloat16)
    project = project.reshape(project.shape[0], 64, 3, HEADS, HD).astype(jnp.float32)
    scores = jnp.einsum('wqhe,wkhe->whqk', project[:, :, 0], project[:, :, 1]) * HD ** (-0.5)
    raised = jnp.exp(scores)
    weights = (raised / lax.optimization_barrier(jnp.sum(raised, axis=-1, keepdims=True))).astype(jnp.bfloat16)
    blended = jnp.einsum('whqk,wkhe->wqhe', weights.astype(jnp.float32), project[:, :, 2]).astype(jnp.bfloat16)
    blended = blended.reshape(blended.shape[0], 64, channels).astype(jnp.float32)
    result = jnp.einsum('wtd,de->wte', blended, out_weight.astype(jnp.float32))
    result = result.reshape(height // 8, breadth // 8, 8, 8, channels)
    if dilated:
        return result.transpose(2, 0, 3, 1, 4).reshape(height, breadth, channels)
    return result.transpose(0, 2, 1, 3, 4).reshape(height, breadth, channels)

def first_section(block_pair, tokens):
    inputs = tokens.astype(jnp.float32)
    normed = normalize(inputs).astype(jnp.bfloat16)
    residual = inputs + window_attention(normed, block_pair[0], block_pair[1], False)
    return (residual, normalize(residual).astype(jnp.bfloat16))

def grid_section(grid_pair, normed):
    return window_attention(normed, grid_pair[0], grid_pair[1], True).astype(jnp.bfloat16)

def last_section(mlp_pair, residual, branch, target, factor):
    summed = residual + branch.astype(jnp.float32)
    normed = normalize(summed).astype(jnp.bfloat16)
    flattened = normed.reshape(-1, normed.shape[-1])
    hidden = jax.nn.gelu(jnp.dot(flattened, mlp_pair[0], preferred_element_type=jnp.float32)).astype(jnp.bfloat16)
    output = summed + jnp.dot(hidden, mlp_pair[1], preferred_element_type=jnp.float32).reshape(summed.shape)
    return jnp.sum(target.astype(jnp.float32) * output) * factor

def reference(tokens, target, block_qkv, block_out, grid_qkv, grid_out, mlp_in, mlp_out, probe_block_qkv, probe_block_out, probe_grid_qkv, probe_grid_out, probe_mlp_in, probe_mlp_out):
    weight_list = (block_qkv, block_out, grid_qkv, grid_out, mlp_in, mlp_out)
    word_list = (probe_block_qkv, probe_block_out, probe_grid_qkv, probe_grid_out, probe_mlp_in, probe_mlp_out)
    signs = tuple((unpack_signs(words, weight.shape[0]) for words, weight in zip(word_list, weight_list)))
    factor = 1.0 / math.sqrt(SLAB_ROWS * SLAB_COLS)

    def total_loss(params):
        residual, normed = first_section(params[0:2], tokens)
        branch = grid_section(params[2:4], normed)
        return last_section(params[4:6], residual, branch, target, factor)
    curvature = jax.jvp(jax.grad(total_loss), (weight_list,), (signs,))[1]
    curvature = tuple((term.astype(jnp.float32) for term in curvature))
    traces = jnp.stack([jnp.sum(sign.astype(jnp.float32) * term) / math.sqrt(term.size) for sign, term in zip(signs, curvature)])
    return (curvature[0], curvature[1], curvature[2], curvature[3], curvature[4], curvature[5], traces)
```

```python
import functools
import math

import jax
import jax.numpy as jnp
from jax import lax
from jax.experimental import pallas as pl
from jax.experimental.pallas import tpu as pltpu
from jax.sharding import Mesh, PartitionSpec as P

F32 = jnp.float32
BF16 = jnp.bfloat16
HD = 32
WINDOW = 64
GROUP = 128
EPSILON = 1e-05
SCALE = HD ** (-0.5)
GELU_K = math.sqrt(2.0 / math.pi)
GELU_C = 0.044715
PEERS = ("y_lo", "x", "z", "y_hi")


def nn(a, b):
    return lax.dot_general(a, b, (((1,), (0,)), ((), ())), preferred_element_type=F32)


def nt(a, b):
    return lax.dot_general(a, b, (((1,), (1,)), ((), ())), preferred_element_type=F32)


def tn(a, b):
    return lax.dot_general(a, b, (((0,), (0,)), ((), ())), preferred_element_type=F32)


def lanes(*parts):
    return jnp.concatenate(parts, axis=1)


def rows(*parts):
    return jnp.concatenate(parts, axis=0)


def mean(values):
    return jnp.mean(values, axis=-1, keepdims=True)


def norm_pair(x, xd):
    center = x - mean(x)
    inverse = lax.rsqrt(mean(center * center) + EPSILON)
    h = center * inverse
    cd = xd - mean(xd)
    along = mean(h * cd)
    return h, inverse * (cd - h * along), inverse, -inverse * along


def norm_back_pair(h, hd, inverse, slope, dy, dyd):
    second = mean(dy * h)
    dx = inverse * (dy - mean(dy) - h * second)
    second_dot = mean(dyd * h + dy * hd)
    dxd = slope * dx + inverse * (dyd - mean(dyd) - hd * second - h * second_dot)
    return dx, dxd


def unpack_signs(words_ref, out_ref):
    total, width = out_ref.shape
    for start in range(0, total, 16):
        row = start + lax.broadcasted_iota(jnp.int32, (16, 1), 0)
        first = start // 30
        edge = 30 * (first + 1)
        word = jnp.broadcast_to(words_ref[first : first + 1, :], (16, width))
        shift = row - 30 * first
        if edge < start + 16:
            later = jnp.broadcast_to(words_ref[first + 1 : first + 2, :], (16, width))
            word = jnp.where(row < edge, word, later)
            shift = jnp.where(row < edge, shift, row - edge)
        bit = jnp.right_shift(word, jnp.broadcast_to(shift, (16, width))) & 1
        out_ref[start : start + 16, :] = (1 - 2 * bit).astype(F32).astype(BF16)


def fill_masks(ones_ref, mask_ref):
    head_row = lax.broadcasted_iota(jnp.int32, (256, 256), 0) // WINDOW
    head_col = lax.broadcasted_iota(jnp.int32, (256, 256), 1) // WINDOW
    ones_ref[...] = (head_row == head_col).astype(F32).astype(BF16)
    head_row = lax.broadcasted_iota(jnp.int32, (256, GROUP), 0) // WINDOW
    head_col = lax.broadcasted_iota(jnp.int32, (256, GROUP), 1) // HD
    mask_ref[...] = (head_row == head_col).astype(F32).astype(BF16)


def spread(values, mask):
    return rows(values, values, values, values) * mask


def collect(values):
    lane = lax.broadcasted_iota(jnp.int32, (WINDOW, GROUP), 1)
    parts = [values[WINDOW * i : WINDOW * (i + 1), :] for i in range(4)]
    low = jnp.where(lane < HD, parts[0], parts[1])
    high = jnp.where(lane < 3 * HD, parts[2], parts[3])
    return jnp.where(lane < 2 * HD, low, high)


def attend(qkv_ref, qkvd_ref, a_ref, ad_ref, o_ref, od_ref, ones_ref, mask_ref):
    windows = qkv_ref.shape[0] // WINDOW

    def step(w, carry):
        at = pl.ds(pl.multiple_of(w * WINDOW, WINDOW), WINDOW)
        ones = ones_ref[...]
        mask = mask_ref[...]
        for g in range(2):
            qs, ks, vs = (pl.ds(256 * i + GROUP * g, GROUP) for i in range(3))
            q, qd = qkv_ref[at, qs], qkvd_ref[at, qs]
            kb, kdb = spread(qkv_ref[at, ks], mask), spread(qkvd_ref[at, ks], mask)
            vb, vdb = spread(qkv_ref[at, vs], mask), spread(qkvd_ref[at, vs], mask)
            raised = jnp.exp(nt(q, kb) * SCALE)
            scores_dot = nt(lanes(qd, q), lanes(kb, kdb)) * SCALE
            weights = raised / nn(raised.astype(BF16), ones)
            moved = weights * scores_dot
            weights_dot = moved - weights * nn(moved.astype(BF16), ones)
            a, ad = weights.astype(BF16), weights_dot.astype(BF16)
            spot = pl.ds(256 * g, 256)
            a_ref[at, spot] = a
            ad_ref[at, spot] = ad
            here = pl.ds(GROUP * g, GROUP)
            o_ref[at, here] = nn(a, vb).astype(BF16)
            od_ref[at, here] = nn(lanes(ad, a), rows(vb, vdb)).astype(BF16)
        return carry

    lax.fori_loop(0, windows, step, 0)


def attend_back(
    qkv_ref, qkvd_ref, a_ref, ad_ref, do_ref, dod_ref, dqkv_ref, dqkvd_ref, ones_ref, mask_ref
):
    windows = qkv_ref.shape[0] // WINDOW

    def step(w, carry):
        at = pl.ds(pl.multiple_of(w * WINDOW, WINDOW), WINDOW)
        ones = ones_ref[...]
        mask = mask_ref[...]
        for g in range(2):
            qs, ks, vs = (pl.ds(256 * i + GROUP * g, GROUP) for i in range(3))
            q, qd = qkv_ref[at, qs], qkvd_ref[at, qs]
            kb, kdb = spread(qkv_ref[at, ks], mask), spread(qkvd_ref[at, ks], mask)
            vb, vdb = spread(qkv_ref[at, vs], mask), spread(qkvd_ref[at, vs], mask)
            here = pl.ds(GROUP * g, GROUP)
            do, dod = do_ref[at, here], dod_ref[at, here]
            spot = pl.ds(256 * g, 256)
            ab, adb = a_ref[at, spot], ad_ref[at, spot]
            a, ad = ab.astype(F32), adb.astype(F32)
            da = nt(do, vb)
            dad = nt(lanes(dod, do), lanes(vb, vdb))
            rest = da - nn((a * da).astype(BF16), ones)
            rest_dot = dad - nn((ad * da + a * dad).astype(BF16), ones)
            ds = (a * rest * SCALE).astype(BF16)
            dsd = ((ad * rest + a * rest_dot) * SCALE).astype(BF16)
            dqkvd_ref[at, qs] = nn(lanes(dsd, ds), rows(kb, kdb)).astype(BF16)
            dqkvd_ref[at, ks] = collect(tn(rows(dsd, ds), rows(q, qd))).astype(BF16)
            dqkvd_ref[at, vs] = collect(tn(rows(adb, ab), rows(do, dod))).astype(BF16)
            if dqkv_ref is not None:
                dqkv_ref[at, qs] = nn(ds, kb).astype(BF16)
                dqkv_ref[at, ks] = collect(tn(ds, q)).astype(BF16)
                dqkv_ref[at, vs] = collect(tn(ab, do)).astype(BF16)
        return carry

    lax.fori_loop(0, windows, step, 0)


def block_forward_kernel(
    tok_ref, tgt_ref, wq_ref, wo_ref, pq_ref, po_ref,
    pack_ref, h_ref, qkv_ref, qkvd_ref, a_ref, ad_ref, o_ref, od_ref, so_ref,
    sq_ref, x_ref, ones_ref, mask_ref,
):
    fill_masks(ones_ref, mask_ref)
    unpack_signs(pq_ref, sq_ref)
    unpack_signs(po_ref, so_ref)
    for half in range(2):
        at = pl.ds(256 * half, 256)
        slab = tok_ref[8 * half : 8 * half + 8].astype(F32)
        x = rows(*[slab[:, 8 * i : 8 * i + 8, :].reshape(WINDOW, 256) for i in range(4)])
        x_ref[at, :] = x
        center = x - mean(x)
        h = (center * lax.rsqrt(mean(center * center) + EPSILON)).astype(BF16)
        h_ref[at, :] = h
        qkv_ref[at, :] = nn(h, wq_ref[...]).astype(BF16)
        qkvd_ref[at, :] = nn(h, sq_ref[...]).astype(BF16)
    attend(qkv_ref, qkvd_ref, a_ref, ad_ref, o_ref, od_ref, ones_ref, mask_ref)
    for half in range(2):
        at = pl.ds(256 * half, 256)
        out = pl.ds(32 * half, 32)
        o, od = o_ref[at, :], od_ref[at, :]
        x = x_ref[at, :] + nn(o, wo_ref[...])
        xd = nn(lanes(od, o), rows(wo_ref[...], so_ref[...]))
        both = jnp.concatenate([x.reshape(32, 8, 256), xd.reshape(32, 8, 256)], axis=1)
        pack_ref[out, :, 0:256] = both.astype(BF16)
        slab = tgt_ref[8 * half : 8 * half + 8].astype(F32)
        t = jnp.concatenate([slab[:, 8 * i : 8 * i + 8, :] for i in range(4)], axis=0)
        both = jnp.concatenate([t[:, :, 0:128], t[:, :, 128:256]], axis=1)
        pack_ref[out, :, 256:384] = both.astype(BF16)


def middle_kernel(
    factor,
    core_ref, pack_ref, wq_ref, wo_ref, wi_ref, wf_ref, pq_ref, po_ref, pi_ref, pf_ref,
    back_ref, keep_ref, send_ref,
    sq_ref, so_ref, si_ref, sf_ref, ones_ref, mask_ref, mix_ref, mixd_ref, mixt_ref,
    x_ref, xd_ref, t_ref, h1_ref, h2_ref, qkv_ref, qkvd_ref, a_ref, ad_ref, o_ref,
    ud_ref, dz_ref, dx_ref, dxd_ref, dg_ref, do_ref, dod_ref, dqkv_ref, hv_ref,
):
    tokens = x_ref.shape[0]
    fill_masks(ones_ref, mask_ref)
    unpack_signs(pq_ref, sq_ref)
    unpack_signs(po_ref, so_ref)
    unpack_signs(pi_ref, si_ref)
    unpack_signs(pf_ref, sf_ref)
    arrived = pack_ref[:, :, 0:256].astype(F32)
    for c in range(2):
        mix_ref[c] = arrived[:, 0:8, 128 * c : 128 * c + 128].reshape(tokens, 128)
        mixd_ref[c] = arrived[:, 8:16, 128 * c : 128 * c + 128].reshape(tokens, 128)
    arrived = pack_ref[:, :, 256:384].astype(F32) * factor
    for c in range(2):
        mixt_ref[c] = arrived[:, 8 * c : 8 * c + 8, :].reshape(tokens, 128)
    for w in range(8):
        at = pl.ds(WINDOW * w, WINDOW)
        for c in range(2):
            cols = pl.ds(128 * c, 128)
            x_ref[at, cols] = mix_ref[c, pl.ds(w, WINDOW, stride=8), :]
            xd_ref[at, cols] = mixd_ref[c, pl.ds(w, WINDOW, stride=8), :]
            t_ref[at, cols] = mixt_ref[c, pl.ds(w, WINDOW, stride=8), :].astype(BF16)

    def first(i, carry):
        at = pl.ds(pl.multiple_of(i * 256, 256), 256)
        low = pl.ds(pl.multiple_of(i * 256 + tokens, 256), 256)
        h, hd, _, _ = norm_pair(x_ref[at, :], xd_ref[at, :])
        h, hd = h.astype(BF16), hd.astype(BF16)
        h1_ref[at, :] = hd
        h1_ref[low, :] = h
        qkv_ref[at, :] = nn(h, wq_ref[...]).astype(BF16)
        qkvd_ref[at, :] = nn(lanes(hd, h), rows(wq_ref[...], sq_ref[...])).astype(BF16)
        return carry

    lax.fori_loop(0, tokens // 256, first, 0)
    o_part, od_part = o_ref.at[pl.ds(tokens, tokens), :], o_ref.at[pl.ds(0, tokens), :]
    attend(qkv_ref, qkvd_ref, a_ref, ad_ref, o_part, od_part, ones_ref, mask_ref)

    def second(i, carry):
        at = pl.ds(pl.multiple_of(i * 256, 256), 256)
        low = pl.ds(pl.multiple_of(i * 256 + tokens, 256), 256)
        od, o = o_ref[at, :], o_ref[low, :]
        g = nn(o, wo_ref[...]).astype(BF16).astype(F32)
        gd = nn(lanes(od, o), rows(wo_ref[...], so_ref[...])).astype(BF16).astype(F32)
        h, hd, inverse, slope = norm_pair(x_ref[at, :] + g, xd_ref[at, :] + gd)
        hb, hdb = h.astype(BF16), hd.astype(BF16)
        h2_ref[at, :] = hdb
        h2_ref[low, :] = hb
        t = t_ref[at, :]
        dh = jnp.zeros((256, 256), F32)
        dhd = jnp.zeros((256, 256), F32)
        for c in range(4):
            cols = pl.ds(256 * c, 256)
            wi, si = wi_ref[:, cols], si_ref[:, cols]
            z = nn(hb, wi)
            zd = nn(lanes(hdb, hb), rows(wi, si))
            du = nt(t, wf_ref[cols, :])
            dud = nt(t, sf_ref[cols, :])
            square = z * z
            bend = jnp.tanh(z * (GELU_K + GELU_K * GELU_C * square))
            inner = GELU_K + (3.0 * GELU_K * GELU_C) * square
            flat = (1.0 - bend * bend) * inner
            half = 0.5 * z
            slope1 = 0.5 + 0.5 * bend + half * flat
            slope2 = flat * (1.0 - z * bend * inner) + (1.0 - bend * bend) * (
                3.0 * GELU_K * GELU_C
            ) * square
            ud_ref[at, cols] = (slope1 * zd).astype(BF16)
            dz = (du * slope1).astype(BF16)
            dzd = (dud * slope1 + du * slope2 * zd).astype(BF16)
            dz_ref[at, cols] = dz
            dz_ref[low, cols] = dzd
            dh = dh + nt(dz, wi)
            dhd = dhd + nt(lanes(dzd, dz), lanes(wi, si))
        dx, dxd = norm_back_pair(h, hd, inverse, slope, dh, dhd)
        dx = dx + t.astype(F32)
        dx_ref[at, :] = dx
        dxd_ref[at, :] = dxd
        dg, dgd = dx.astype(BF16), dxd.astype(BF16)
        dg_ref[at, :] = dg
        dg_ref[low, :] = dgd
        do_ref[at, :] = nt(dg, wo_ref[...]).astype(BF16)
        dod_ref[at, :] = nt(lanes(dgd, dg), lanes(wo_ref[...], so_ref[...])).astype(BF16)
        return carry

    lax.fori_loop(0, tokens // 256, second, 0)
    dqkv, dqkvd = dqkv_ref.at[pl.ds(0, tokens), :], dqkv_ref.at[pl.ds(tokens, tokens), :]
    attend_back(
        qkv_ref, qkvd_ref, a_ref, ad_ref, do_ref, dod_ref, dqkv, dqkvd, ones_ref, mask_ref
    )

    for i in range(tokens // 256):
        at = pl.ds(i * 256, 256)
        low = pl.ds(i * 256 + tokens, 256)
        dqkv, dqkvd = dqkv_ref[at, :], dqkv_ref[low, :]
        dh = nt(dqkv, wq_ref[...])
        dhd = nt(lanes(dqkvd, dqkv), lanes(wq_ref[...], sq_ref[...]))
        h, hd, inverse, slope = norm_pair(x_ref[at, :], xd_ref[at, :])
        dx, dxd = norm_back_pair(h, hd, inverse, slope, dh, dhd)
        dx_ref[at, :] += dx
        dxd_ref[at, :] += dxd
    for w in range(8):
        at = pl.ds(WINDOW * w, WINDOW)
        for c in range(2):
            cols = pl.ds(128 * c, 128)
            mix_ref[c, pl.ds(w, WINDOW, stride=8), :] = dx_ref[at, cols]
            mixd_ref[c, pl.ds(w, WINDOW, stride=8), :] = dxd_ref[at, cols]
    for c in range(2):
        dx = mix_ref[c].reshape(tokens // 8, 8, 128)
        dxd = mixd_ref[c].reshape(tokens // 8, 8, 128)
        both = jnp.concatenate([dx, dxd], axis=1)
        back_ref[:, :, 128 * c : 128 * c + 128] = both.astype(BF16)

    def put(block, value):
        hv_ref[block] = value.astype(BF16)

    h1 = h1_ref[...]
    for c in range(3):
        put(c, tn(h1, dqkv_ref[:, 256 * c : 256 * c + 256]))
    put(3, tn(o_ref[...], dg_ref[...]))
    h2 = h2_ref[...]
    for c in range(4):
        put(4 + c, tn(h2, dz_ref[:, 256 * c : 256 * c + 256]))
    t = t_ref[...]
    for c in range(4):
        put(8 + c, tn(ud_ref[:, 256 * c : 256 * c + 256], t))
    split_halves(core_ref, hv_ref, keep_ref, send_ref)


def split_halves(core_ref, hv_ref, keep_ref, send_ref):
    core = core_ref[0]
    mine = pl.ds(pl.multiple_of(core * 128, 128), 128)
    other = pl.ds(pl.multiple_of((1 - core) * 128, 128), 128)
    for block in range(hv_ref.shape[0]):
        keep_ref[128 * block : 128 * block + 128, :] = hv_ref[block, mine, :]
        send_ref[128 * block : 128 * block + 128, :] = hv_ref[block, other, :]


def block_back_kernel(
    core_ref, back_ref, h_ref, qkv_ref, qkvd_ref, a_ref, ad_ref, o_ref, od_ref, wo_ref, so_ref,
    keep_ref, send_ref,
    ones_ref, mask_ref, do_ref, dod_ref, dqkvd_ref, hv_ref,
):
    tokens = h_ref.shape[0]
    fill_masks(ones_ref, mask_ref)
    arrived = back_ref[...].astype(F32)
    dx = arrived[:, 0:8, :].reshape(tokens, 256).astype(BF16)
    dxd = arrived[:, 8:16, :].reshape(tokens, 256).astype(BF16)
    do_ref[...] = nt(dx, wo_ref[...]).astype(BF16)
    dod_ref[...] = nt(lanes(dxd, dx), lanes(wo_ref[...], so_ref[...])).astype(BF16)
    hv_ref[3] = tn(rows(od_ref[...], o_ref[...]), rows(dx, dxd)).astype(BF16)
    attend_back(
        qkv_ref, qkvd_ref, a_ref, ad_ref, do_ref, dod_ref, None, dqkvd_ref, ones_ref, mask_ref
    )
    h = h_ref[...]
    for c in range(3):
        hv_ref[c] = tn(h, dqkvd_ref[:, 256 * c : 256 * c + 256]).astype(BF16)
    split_halves(core_ref, hv_ref, keep_ref, send_ref)


def pair_sum_kernel(mid_keep_ref, mid_got_ref, keep_ref, got_ref, out_ref):
    count = mid_keep_ref.shape[0]
    out_ref[0:count, :] = (mid_keep_ref[...].astype(F32) + mid_got_ref[...].astype(F32)).astype(BF16)
    out_ref[count:, :] = (keep_ref[...].astype(F32) + got_ref[...].astype(F32)).astype(BF16)


def peer_sum_kernel(parts_ref, out_ref):
    total = parts_ref[0].astype(F32)
    for i in range(1, parts_ref.shape[0]):
        total = total + parts_ref[i].astype(F32)
    total = total.astype(BF16)
    for i in range(parts_ref.shape[0]):
        out_ref[i] = total


def finish_kernel(
    core_ref, mine_ref, other_ref, pbq_ref, pbo_ref, pgq_ref, pgo_ref, pmi_ref, pmo_ref,
    bq_ref, bo_ref, gq_ref, go_ref, mi_ref, mo_ref, trace_ref,
    sign_ref,
):
    core = core_ref[0]
    lane = lax.broadcasted_iota(jnp.int32, (1, 128), 1)
    traces = jnp.zeros((1, 128), F32)
    plan = (
        (bq_ref, pbq_ref, 12, 0),
        (bo_ref, pbo_ref, 15, 1),
        (gq_ref, pgq_ref, 0, 2),
        (go_ref, pgo_ref, 3, 3),
        (mi_ref, pmi_ref, 4, 4),
        (mo_ref, pmo_ref, 8, 5),
    )
    for out_ref, words_ref, base, place in plan:
        height, width = out_ref.shape
        across = width // 256
        for block in range(height * width // 65536):
            cols = pl.ds(256 * (block % across), 256)
            down = 256 * (block // across)
            for source_ref, who in ((mine_ref, core), (other_ref, 1 - core)):
                start = pl.multiple_of(down + who * 128, 128)
                value = source_ref[128 * (base + block) : 128 * (base + block) + 128, :]
                out_ref[pl.ds(start, 128), cols] = value.astype(F32)
        signs = sign_ref.at[0:height, 0:width]
        unpack_signs(words_ref, signs)
        total = jnp.sum(out_ref[...] * signs[...].astype(F32), axis=0, keepdims=True)
        total = jnp.sum(total, axis=1, keepdims=True) / math.sqrt(height * width)
        traces = jnp.where(lane == place, total, traces)
    trace_ref[...] = traces


def shaped(dtype, *shape):
    return jax.ShapeDtypeStruct(shape, dtype)


def call(kernel, outs, scratch, smem_first, operands, name, limit):
    spaces = [pltpu.SMEM if (smem_first and i == 0) else pltpu.VMEM for i in range(len(operands))]
    return pl.pallas_call(
        kernel,
        out_shape=outs,
        in_specs=[pl.BlockSpec(memory_space=space) for space in spaces],
        out_specs=[pl.BlockSpec(memory_space=pltpu.VMEM) for _ in outs],
        scratch_shapes=scratch,
        compiler_params=pltpu.CompilerParams(vmem_limit_bytes=limit * 2**20),
        name=name,
    )(*operands)


def body(
    tokens, target, block_qkv, block_out, grid_qkv, grid_out, mlp_in, mlp_out,
    probe_block_qkv, probe_block_out, probe_grid_qkv, probe_grid_out, probe_mlp_in, probe_mlp_out,
):
    count = tokens.shape[0] * tokens.shape[1]
    peers = lax.axis_size(PEERS)
    factor = 1.0 / math.sqrt(count * peers * lax.axis_size("core"))
    core = lax.axis_index("core").astype(jnp.int32).reshape(1)
    swap = [(0, 1), (1, 0)]
    masks = [pltpu.VMEM((256, 256), BF16), pltpu.VMEM((256, GROUP), BF16)]

    def exchange(values):
        return lax.all_to_all(values, PEERS, 0, 0, tiled=True)

    pack, h0, qkv, qkvd, a, ad, o, od, so = call(
        block_forward_kernel,
        [
            shaped(BF16, peers, 16, 384),
            shaped(BF16, count, 256),
            shaped(BF16, count, 768),
            shaped(BF16, count, 768),
            shaped(BF16, count, 512),
            shaped(BF16, count, 512),
            shaped(BF16, count, 256),
            shaped(BF16, count, 256),
            shaped(BF16, 256, 256),
        ],
        [pltpu.VMEM((256, 768), BF16), pltpu.VMEM((count, 256), F32)] + masks,
        False,
        (tokens, target, block_qkv, block_out, probe_block_qkv, probe_block_out),
        "block_forward",
        32,
    )
    pack = exchange(pack)
    back, mid_keep, mid_send = call(
        functools.partial(middle_kernel, factor),
        [shaped(BF16, peers, 16, 256), shaped(BF16, 1536, 256), shaped(BF16, 1536, 256)],
        [
            pltpu.VMEM((256, 768), BF16),
            pltpu.VMEM((256, 256), BF16),
            pltpu.VMEM((256, 1024), BF16),
            pltpu.VMEM((1024, 256), BF16),
        ]
        + masks
        + [pltpu.VMEM((2, count, 128), F32)] * 3
        + [pltpu.VMEM((count, 256), F32)] * 2
        + [
            pltpu.VMEM((count, 256), BF16),
            pltpu.VMEM((2 * count, 256), BF16),
            pltpu.VMEM((2 * count, 256), BF16),
            pltpu.VMEM((count, 768), BF16),
            pltpu.VMEM((count, 768), BF16),
            pltpu.VMEM((count, 512), BF16),
            pltpu.VMEM((count, 512), BF16),
            pltpu.VMEM((2 * count, 256), BF16),
            pltpu.VMEM((count, 1024), BF16),
            pltpu.VMEM((2 * count, 1024), BF16),
            pltpu.VMEM((count, 256), F32),
            pltpu.VMEM((count, 256), F32),
            pltpu.VMEM((2 * count, 256), BF16),
            pltpu.VMEM((count, 256), BF16),
            pltpu.VMEM((count, 256), BF16),
            pltpu.VMEM((2 * count, 768), BF16),
            pltpu.VMEM((12, 256, 256), BF16),
        ],
        True,
        (
            core, pack, grid_qkv, grid_out, mlp_in, mlp_out,
            probe_grid_qkv, probe_grid_out, probe_mlp_in, probe_mlp_out,
        ),
        "middle",
        48,
    )
    mid_got = lax.ppermute(mid_send, "core", swap)
    back = exchange(back)
    keep, send = call(
        block_back_kernel,
        [shaped(BF16, 512, 256), shaped(BF16, 512, 256)],
        masks
        + [
            pltpu.VMEM((count, 256), BF16),
            pltpu.VMEM((count, 256), BF16),
            pltpu.VMEM((count, 768), BF16),
            pltpu.VMEM((4, 256, 256), BF16),
        ],
        True,
        (core, back, h0, qkv, qkvd, a, ad, o, od, block_out, so),
        "block_back",
        32,
    )
    got = lax.ppermute(send, "core", swap)
    (parts,) = call(
        pair_sum_kernel,
        [shaped(BF16, 2048, 256)],
        [],
        False,
        (mid_keep, mid_got, keep, got),
        "pair_sum",
        32,
    )
    parts = exchange(parts.reshape(peers, 2048 // peers, 256))
    (copies,) = call(
        peer_sum_kernel,
        [shaped(BF16, peers, 2048 // peers, 256)],
        [],
        False,
        (parts,),
        "peer_sum",
        32,
    )
    mine = exchange(copies).reshape(2048, 256)
    other = lax.ppermute(mine, "core", swap)
    results = call(
        finish_kernel,
        [
            shaped(F32, 256, 768),
            shaped(F32, 256, 256),
            shaped(F32, 256, 768),
            shaped(F32, 256, 256),
            shaped(F32, 256, 1024),
            shaped(F32, 1024, 256),
            shaped(F32, 1, 128),
        ],
        [pltpu.VMEM((1024, 1024), BF16)],
        True,
        (
            core, mine, other, probe_block_qkv, probe_block_out, probe_grid_qkv,
            probe_grid_out, probe_mlp_in, probe_mlp_out,
        ),
        "finish",
        32,
    )
    return (*results[:6], results[6][0, :6])


def solution(mesh):
    fine = Mesh(mesh.devices.reshape(2, 4, 4, 2, 2), ("y_lo", "x", "z", "y_hi", "core"))
    placed = P(("y_lo", "x"), ("z", "y_hi", "core"), None)
    return jax.shard_map(
        body,
        mesh=fine,
        in_specs=(placed, placed) + (P(),) * 12,
        out_specs=(P(),) * 7,
        check_vma=False,
    )
```

```python
import functools
import math

import jax
import jax.numpy as jnp
from jax import lax
from jax.experimental import pallas as pl
from jax.experimental.pallas import tpu as pltpu
from jax.sharding import Mesh, PartitionSpec as P

F32 = jnp.float32
BF16 = jnp.bfloat16
HD = 32
WINDOW = 64
GROUP = 128
EPSILON = 1e-05
SCALE = HD ** (-0.5)
GELU_K = math.sqrt(2.0 / math.pi)
GELU_C = 0.044715
PEERS = ("y_lo", "x", "z", "y_hi")


def nn(a, b):
    return lax.dot_general(a, b, (((1,), (0,)), ((), ())), preferred_element_type=F32)


def nt(a, b):
    return lax.dot_general(a, b, (((1,), (1,)), ((), ())), preferred_element_type=F32)


def tn(a, b):
    return lax.dot_general(a, b, (((0,), (0,)), ((), ())), preferred_element_type=F32)


def lanes(*parts):
    return jnp.concatenate(parts, axis=1)


def rows(*parts):
    return jnp.concatenate(parts, axis=0)


def mean(values):
    return jnp.mean(values, axis=-1, keepdims=True)


def norm_pair(x, xd):
    center = x - mean(x)
    inverse = lax.rsqrt(mean(center * center) + EPSILON)
    h = center * inverse
    cd = xd - mean(xd)
    along = mean(h * cd)
    return h, inverse * (cd - h * along), inverse, -inverse * along


def norm_back_pair(h, hd, inverse, slope, dy, dyd):
    second = mean(dy * h)
    dx = inverse * (dy - mean(dy) - h * second)
    second_dot = mean(dyd * h + dy * hd)
    dxd = slope * dx + inverse * (dyd - mean(dyd) - hd * second - h * second_dot)
    return dx, dxd


def fetch(sources, buffers, sems):
    copies = [
        pltpu.make_async_copy(source, buffer, sems.at[i])
        for i, (source, buffer) in enumerate(zip(sources, buffers))
    ]
    for copy in copies:
        copy.start()
    return lambda *places: [copies[place].wait() for place in places]


def unpack_signs(words_ref, out_ref):
    total, width = out_ref.shape
    for start in range(0, total, 16):
        row = start + lax.broadcasted_iota(jnp.int32, (16, 1), 0)
        first = start // 30
        edge = 30 * (first + 1)
        word = jnp.broadcast_to(words_ref[first : first + 1, :], (16, width))
        shift = row - 30 * first
        if edge < start + 16:
            later = jnp.broadcast_to(words_ref[first + 1 : first + 2, :], (16, width))
            word = jnp.where(row < edge, word, later)
            shift = jnp.where(row < edge, shift, row - edge)
        bit = jnp.right_shift(word, jnp.broadcast_to(shift, (16, width))) & 1
        out_ref[start : start + 16, :] = (1 - 2 * bit).astype(F32).astype(BF16)


def fill_masks(ones_ref, mask_ref):
    head_row = lax.broadcasted_iota(jnp.int32, (256, 256), 0) // WINDOW
    head_col = lax.broadcasted_iota(jnp.int32, (256, 256), 1) // WINDOW
    ones_ref[...] = (head_row == head_col).astype(F32).astype(BF16)
    head_row = lax.broadcasted_iota(jnp.int32, (256, GROUP), 0) // WINDOW
    head_col = lax.broadcasted_iota(jnp.int32, (256, GROUP), 1) // HD
    mask_ref[...] = (head_row == head_col).astype(F32).astype(BF16)


def spread(values, mask):
    return rows(values, values, values, values) * mask


def collect(values):
    lane = lax.broadcasted_iota(jnp.int32, (WINDOW, GROUP), 1)
    parts = [values[WINDOW * i : WINDOW * (i + 1), :] for i in range(4)]
    low = jnp.where(lane < HD, parts[0], parts[1])
    high = jnp.where(lane < 3 * HD, parts[2], parts[3])
    return jnp.where(lane < 2 * HD, low, high)


def attend(qkv_ref, qkvd_ref, a_ref, ad_ref, o_ref, od_ref, ones_ref, mask_ref):
    windows = qkv_ref.shape[0] // WINDOW

    def step(w, carry):
        at = pl.ds(pl.multiple_of(w * WINDOW, WINDOW), WINDOW)
        ones = ones_ref[...]
        mask = mask_ref[...]
        for g in range(2):
            qs, ks, vs = (pl.ds(256 * i + GROUP * g, GROUP) for i in range(3))
            q, qd = qkv_ref[at, qs], qkvd_ref[at, qs]
            kb, kdb = spread(qkv_ref[at, ks], mask), spread(qkvd_ref[at, ks], mask)
            vb, vdb = spread(qkv_ref[at, vs], mask), spread(qkvd_ref[at, vs], mask)
            raised = jnp.exp(nt(q, kb) * SCALE)
            scores_dot = nt(lanes(qd, q), lanes(kb, kdb)) * SCALE
            weights = raised / nn(raised.astype(BF16), ones)
            moved = weights * scores_dot
            weights_dot = moved - weights * nn(moved.astype(BF16), ones)
            a, ad = weights.astype(BF16), weights_dot.astype(BF16)
            spot = pl.ds(256 * g, 256)
            a_ref[at, spot] = a
            ad_ref[at, spot] = ad
            here = pl.ds(GROUP * g, GROUP)
            o_ref[at, here] = nn(a, vb).astype(BF16)
            od_ref[at, here] = nn(lanes(ad, a), rows(vb, vdb)).astype(BF16)
        return carry

    lax.fori_loop(0, windows, step, 0)


def attend_back(
    qkv_ref, qkvd_ref, a_ref, ad_ref, do_ref, dod_ref, dqkv_ref, dqkvd_ref, ones_ref, mask_ref
):
    windows = qkv_ref.shape[0] // WINDOW

    def step(w, carry):
        at = pl.ds(pl.multiple_of(w * WINDOW, WINDOW), WINDOW)
        ones = ones_ref[...]
        mask = mask_ref[...]
        for g in range(2):
            qs, ks, vs = (pl.ds(256 * i + GROUP * g, GROUP) for i in range(3))
            q, qd = qkv_ref[at, qs], qkvd_ref[at, qs]
            kb, kdb = spread(qkv_ref[at, ks], mask), spread(qkvd_ref[at, ks], mask)
            vb, vdb = spread(qkv_ref[at, vs], mask), spread(qkvd_ref[at, vs], mask)
            here = pl.ds(GROUP * g, GROUP)
            do, dod = do_ref[at, here], dod_ref[at, here]
            spot = pl.ds(256 * g, 256)
            ab, adb = a_ref[at, spot], ad_ref[at, spot]
            a, ad = ab.astype(F32), adb.astype(F32)
            da = nt(do, vb)
            dad = nt(lanes(dod, do), lanes(vb, vdb))
            rest = da - nn((a * da).astype(BF16), ones)
            rest_dot = dad - nn((ad * da + a * dad).astype(BF16), ones)
            ds = (a * rest * SCALE).astype(BF16)
            dsd = ((ad * rest + a * rest_dot) * SCALE).astype(BF16)
            dqkvd_ref[at, qs] = nn(lanes(dsd, ds), rows(kb, kdb)).astype(BF16)
            dqkvd_ref[at, ks] = collect(tn(rows(dsd, ds), rows(q, qd))).astype(BF16)
            dqkvd_ref[at, vs] = collect(tn(rows(adb, ab), rows(do, dod))).astype(BF16)
            if dqkv_ref is not None:
                dqkv_ref[at, qs] = nn(ds, kb).astype(BF16)
                dqkv_ref[at, ks] = collect(tn(ds, q)).astype(BF16)
                dqkv_ref[at, vs] = collect(tn(ab, do)).astype(BF16)
        return carry

    lax.fori_loop(0, windows, step, 0)


def block_forward_kernel(
    pq_hbm, tok_hbm, wq_hbm, po_hbm, wo_hbm, tgt_hbm,
    pack_ref, h_ref, qkv_ref, qkvd_ref, a_ref, ad_ref, o_ref, od_ref, sq_ref, so_ref,
    pq_ref, tok_ref, wq_ref, po_ref, wo_ref, tgt_ref, sems, x_ref, ones_ref, mask_ref,
):
    wait = fetch(
        (pq_hbm, tok_hbm, wq_hbm, po_hbm, wo_hbm, tgt_hbm),
        (pq_ref, tok_ref, wq_ref, po_ref, wo_ref, tgt_ref),
        sems,
    )
    fill_masks(ones_ref, mask_ref)
    wait(0)
    unpack_signs(pq_ref, sq_ref)
    wait(1, 2)
    for half in range(2):
        at = pl.ds(256 * half, 256)
        slab = tok_ref[8 * half : 8 * half + 8].astype(F32)
        x = rows(*[slab[:, 8 * i : 8 * i + 8, :].reshape(WINDOW, 256) for i in range(4)])
        x_ref[at, :] = x
        center = x - mean(x)
        h = (center * lax.rsqrt(mean(center * center) + EPSILON)).astype(BF16)
        h_ref[at, :] = h
        qkv_ref[at, :] = nn(h, wq_ref[...]).astype(BF16)
        qkvd_ref[at, :] = nn(h, sq_ref[...]).astype(BF16)
    attend(qkv_ref, qkvd_ref, a_ref, ad_ref, o_ref, od_ref, ones_ref, mask_ref)
    wait(3, 4, 5)
    unpack_signs(po_ref, so_ref)
    for half in range(2):
        at = pl.ds(256 * half, 256)
        out = pl.ds(32 * half, 32)
        o, od = o_ref[at, :], od_ref[at, :]
        x = x_ref[at, :] + nn(o, wo_ref[...])
        xd = nn(lanes(od, o), rows(wo_ref[...], so_ref[...]))
        both = jnp.concatenate([x.reshape(32, 8, 256), xd.reshape(32, 8, 256)], axis=1)
        pack_ref[out, :, 0:256] = both.astype(BF16)
        slab = tgt_ref[8 * half : 8 * half + 8].astype(F32)
        t = jnp.concatenate([slab[:, 8 * i : 8 * i + 8, :] for i in range(4)], axis=0)
        both = jnp.concatenate([t[:, :, 0:128], t[:, :, 128:256]], axis=1)
        pack_ref[out, :, 256:384] = both.astype(BF16)


def middle_kernel(
    factor,
    core_ref, pack_ref, pq_ref, wq_ref, po_ref, wo_ref, pi_ref, wi_ref, pf_ref, wf_ref,
    back_ref, keep_ref, send_ref, sq_ref, so_ref, si_ref, sf_ref,
    ones_ref, mask_ref, mix_ref, mixd_ref, mixt_ref,
    x_ref, xd_ref, t_ref, h1_ref, h2_ref, qkv_ref, qkvd_ref, a_ref, ad_ref, o_ref,
    ud_ref, dz_ref, dx_ref, dxd_ref, dg_ref, do_ref, dod_ref, dqkv_ref, hv_ref,
):
    tokens = x_ref.shape[0]
    fill_masks(ones_ref, mask_ref)
    arrived = pack_ref[:, :, 0:256].astype(F32)
    for c in range(2):
        mix_ref[c] = arrived[:, 0:8, 128 * c : 128 * c + 128].reshape(tokens, 128)
        mixd_ref[c] = arrived[:, 8:16, 128 * c : 128 * c + 128].reshape(tokens, 128)
    arrived = pack_ref[:, :, 256:384].astype(F32) * factor
    for c in range(2):
        mixt_ref[c] = arrived[:, 8 * c : 8 * c + 8, :].reshape(tokens, 128)
    for w in range(8):
        at = pl.ds(WINDOW * w, WINDOW)
        for c in range(2):
            cols = pl.ds(128 * c, 128)
            x_ref[at, cols] = mix_ref[c, pl.ds(w, WINDOW, stride=8), :]
            xd_ref[at, cols] = mixd_ref[c, pl.ds(w, WINDOW, stride=8), :]
            t_ref[at, cols] = mixt_ref[c, pl.ds(w, WINDOW, stride=8), :].astype(BF16)
    unpack_signs(pq_ref, sq_ref)
    unpack_signs(po_ref, so_ref)
    unpack_signs(pi_ref, si_ref)
    unpack_signs(pf_ref, sf_ref)

    def first(i, carry):
        at = pl.ds(pl.multiple_of(i * 256, 256), 256)
        low = pl.ds(pl.multiple_of(i * 256 + tokens, 256), 256)
        h, hd, _, _ = norm_pair(x_ref[at, :], xd_ref[at, :])
        h, hd = h.astype(BF16), hd.astype(BF16)
        h1_ref[at, :] = hd
        h1_ref[low, :] = h
        qkv_ref[at, :] = nn(h, wq_ref[...]).astype(BF16)
        qkvd_ref[at, :] = nn(lanes(hd, h), rows(wq_ref[...], sq_ref[...])).astype(BF16)
        return carry

    lax.fori_loop(0, tokens // 256, first, 0)
    o_part, od_part = o_ref.at[pl.ds(tokens, tokens), :], o_ref.at[pl.ds(0, tokens), :]
    attend(qkv_ref, qkvd_ref, a_ref, ad_ref, o_part, od_part, ones_ref, mask_ref)

    def second(i, carry):
        at = pl.ds(pl.multiple_of(i * 256, 256), 256)
        low = pl.ds(pl.multiple_of(i * 256 + tokens, 256), 256)
        od, o = o_ref[at, :], o_ref[low, :]
        g = nn(o, wo_ref[...]).astype(BF16).astype(F32)
        gd = nn(lanes(od, o), rows(wo_ref[...], so_ref[...])).astype(BF16).astype(F32)
        h, hd, inverse, slope = norm_pair(x_ref[at, :] + g, xd_ref[at, :] + gd)
        hb, hdb = h.astype(BF16), hd.astype(BF16)
        h2_ref[at, :] = hdb
        h2_ref[low, :] = hb
        t = t_ref[at, :]
        dh = jnp.zeros((256, 256), F32)
        dhd = jnp.zeros((256, 256), F32)
        for c in range(4):
            cols = pl.ds(256 * c, 256)
            wi, si = wi_ref[:, cols], si_ref[:, cols]
            z = nn(hb, wi)
            zd = nn(lanes(hdb, hb), rows(wi, si))
            du = nt(t, wf_ref[cols, :])
            dud = nt(t, sf_ref[cols, :])
            square = z * z
            bend = jnp.tanh(z * (GELU_K + GELU_K * GELU_C * square))
            inner = GELU_K + (3.0 * GELU_K * GELU_C) * square
            flat = (1.0 - bend * bend) * inner
            half = 0.5 * z
            slope1 = 0.5 + 0.5 * bend + half * flat
            slope2 = flat * (1.0 - z * bend * inner) + (1.0 - bend * bend) * (
                3.0 * GELU_K * GELU_C
            ) * square
            ud_ref[at, cols] = (slope1 * zd).astype(BF16)
            dz = (du * slope1).astype(BF16)
            dzd = (dud * slope1 + du * slope2 * zd).astype(BF16)
            dz_ref[at, cols] = dz
            dz_ref[low, cols] = dzd
            dh = dh + nt(dz, wi)
            dhd = dhd + nt(lanes(dzd, dz), lanes(wi, si))
        dx, dxd = norm_back_pair(h, hd, inverse, slope, dh, dhd)
        dx = dx + t.astype(F32)
        dx_ref[at, :] = dx
        dxd_ref[at, :] = dxd
        dg, dgd = dx.astype(BF16), dxd.astype(BF16)
        dg_ref[at, :] = dg
        dg_ref[low, :] = dgd
        do_ref[at, :] = nt(dg, wo_ref[...]).astype(BF16)
        dod_ref[at, :] = nt(lanes(dgd, dg), lanes(wo_ref[...], so_ref[...])).astype(BF16)
        return carry

    lax.fori_loop(0, tokens // 256, second, 0)
    dqkv, dqkvd = dqkv_ref.at[pl.ds(0, tokens), :], dqkv_ref.at[pl.ds(tokens, tokens), :]
    attend_back(
        qkv_ref, qkvd_ref, a_ref, ad_ref, do_ref, dod_ref, dqkv, dqkvd, ones_ref, mask_ref
    )

    for i in range(tokens // 256):
        at = pl.ds(i * 256, 256)
        low = pl.ds(i * 256 + tokens, 256)
        dqkv, dqkvd = dqkv_ref[at, :], dqkv_ref[low, :]
        dh = nt(dqkv, wq_ref[...])
        dhd = nt(lanes(dqkvd, dqkv), lanes(wq_ref[...], sq_ref[...]))
        h, hd, inverse, slope = norm_pair(x_ref[at, :], xd_ref[at, :])
        dx, dxd = norm_back_pair(h, hd, inverse, slope, dh, dhd)
        dx_ref[at, :] += dx
        dxd_ref[at, :] += dxd
    for w in range(8):
        at = pl.ds(WINDOW * w, WINDOW)
        for c in range(2):
            cols = pl.ds(128 * c, 128)
            mix_ref[c, pl.ds(w, WINDOW, stride=8), :] = dx_ref[at, cols]
            mixd_ref[c, pl.ds(w, WINDOW, stride=8), :] = dxd_ref[at, cols]
    for c in range(2):
        dx = mix_ref[c].reshape(tokens // 8, 8, 128)
        dxd = mixd_ref[c].reshape(tokens // 8, 8, 128)
        both = jnp.concatenate([dx, dxd], axis=1)
        back_ref[:, :, 128 * c : 128 * c + 128] = both.astype(BF16)

    def put(block, value):
        hv_ref[block] = value.astype(BF16)

    h1 = h1_ref[...]
    for c in range(3):
        put(c, tn(h1, dqkv_ref[:, 256 * c : 256 * c + 256]))
    put(3, tn(o_ref[...], dg_ref[...]))
    h2 = h2_ref[...]
    for c in range(4):
        put(4 + c, tn(h2, dz_ref[:, 256 * c : 256 * c + 256]))
    t = t_ref[...]
    for c in range(4):
        put(8 + c, tn(ud_ref[:, 256 * c : 256 * c + 256], t))
    split_halves(core_ref, hv_ref, keep_ref, send_ref)


def split_halves(core_ref, hv_ref, keep_ref, send_ref):
    core = core_ref[0]
    mine = pl.ds(pl.multiple_of(core * 128, 128), 128)
    other = pl.ds(pl.multiple_of((1 - core) * 128, 128), 128)
    for block in range(hv_ref.shape[0]):
        keep_ref[128 * block : 128 * block + 128, :] = hv_ref[block, mine, :]
        send_ref[128 * block : 128 * block + 128, :] = hv_ref[block, other, :]


def block_back_kernel(
    core_ref, back_ref, h_ref, qkv_ref, qkvd_ref, a_ref, ad_ref, o_ref, od_ref, wo_ref, so_ref,
    keep_ref, send_ref,
    ones_ref, mask_ref, do_ref, dod_ref, dqkvd_ref, hv_ref,
):
    tokens = h_ref.shape[0]
    fill_masks(ones_ref, mask_ref)
    arrived = back_ref[...].astype(F32)
    dx = arrived[:, 0:8, :].reshape(tokens, 256).astype(BF16)
    dxd = arrived[:, 8:16, :].reshape(tokens, 256).astype(BF16)
    do_ref[...] = nt(dx, wo_ref[...]).astype(BF16)
    dod_ref[...] = nt(lanes(dxd, dx), lanes(wo_ref[...], so_ref[...])).astype(BF16)
    hv_ref[3] = tn(rows(od_ref[...], o_ref[...]), rows(dx, dxd)).astype(BF16)
    attend_back(
        qkv_ref, qkvd_ref, a_ref, ad_ref, do_ref, dod_ref, None, dqkvd_ref, ones_ref, mask_ref
    )
    h = h_ref[...]
    for c in range(3):
        hv_ref[c] = tn(h, dqkvd_ref[:, 256 * c : 256 * c + 256]).astype(BF16)
    split_halves(core_ref, hv_ref, keep_ref, send_ref)


def pair_sum_kernel(mid_keep_ref, mid_got_ref, keep_ref, got_ref, out_ref):
    count = mid_keep_ref.shape[0]
    out_ref[0:count, :] = (mid_keep_ref[...].astype(F32) + mid_got_ref[...].astype(F32)).astype(BF16)
    out_ref[count:, :] = (keep_ref[...].astype(F32) + got_ref[...].astype(F32)).astype(BF16)


def peer_sum_kernel(parts_ref, out_ref):
    total = parts_ref[0].astype(F32)
    for i in range(1, parts_ref.shape[0]):
        total = total + parts_ref[i].astype(F32)
    total = total.astype(BF16)
    for i in range(parts_ref.shape[0]):
        out_ref[i] = total


def finish_kernel(
    core_ref, mine_ref, other_ref, sbq_ref, sbo_ref, sgq_ref, sgo_ref, smi_ref, smo_ref,
    bq_ref, bo_ref, gq_ref, go_ref, mi_ref, mo_ref, trace_ref,
):
    core = core_ref[0]
    lane = lax.broadcasted_iota(jnp.int32, (1, 128), 1)
    traces = jnp.zeros((1, 128), F32)
    plan = (
        (bq_ref, sbq_ref, 12, 0),
        (bo_ref, sbo_ref, 15, 1),
        (gq_ref, sgq_ref, 0, 2),
        (go_ref, sgo_ref, 3, 3),
        (mi_ref, smi_ref, 4, 4),
        (mo_ref, smo_ref, 8, 5),
    )
    for out_ref, sign_ref, base, place in plan:
        height, width = out_ref.shape
        across = width // 256
        for block in range(height * width // 65536):
            cols = pl.ds(256 * (block % across), 256)
            down = 256 * (block // across)
            for source_ref, who in ((mine_ref, core), (other_ref, 1 - core)):
                start = pl.multiple_of(down + who * 128, 128)
                value = source_ref[128 * (base + block) : 128 * (base + block) + 128, :]
                out_ref[pl.ds(start, 128), cols] = value.astype(F32)
        total = jnp.sum(out_ref[...] * sign_ref[...].astype(F32), axis=0, keepdims=True)
        total = jnp.sum(total, axis=1, keepdims=True) / math.sqrt(height * width)
        traces = jnp.where(lane == place, total, traces)
    trace_ref[...] = traces


def shaped(dtype, *shape):
    return jax.ShapeDtypeStruct(shape, dtype)


def held(*arrays):
    buffers = [pltpu.VMEM(array.shape, array.dtype) for array in arrays]
    return buffers + [pltpu.SemaphoreType.DMA((len(arrays),))]


def call(kernel, outs, scratch, places, operands, name, limit):
    kinds = {"s": pltpu.SMEM, "v": pltpu.VMEM, "h": pltpu.HBM}
    spaces = [kinds[place] for place in places]
    return pl.pallas_call(
        kernel,
        out_shape=outs,
        in_specs=[pl.BlockSpec(memory_space=space) for space in spaces],
        out_specs=[pl.BlockSpec(memory_space=pltpu.VMEM) for _ in outs],
        scratch_shapes=scratch,
        compiler_params=pltpu.CompilerParams(vmem_limit_bytes=limit * 2**20),
        name=name,
    )(*operands)


def body(
    tokens, target, block_qkv, block_out, grid_qkv, grid_out, mlp_in, mlp_out,
    probe_block_qkv, probe_block_out, probe_grid_qkv, probe_grid_out, probe_mlp_in, probe_mlp_out,
):
    count = tokens.shape[0] * tokens.shape[1]
    peers = lax.axis_size(PEERS)
    factor = 1.0 / math.sqrt(count * peers * lax.axis_size("core"))
    core = lax.axis_index("core").astype(jnp.int32).reshape(1)
    swap = [(0, 1), (1, 0)]
    masks = [pltpu.VMEM((256, 256), BF16), pltpu.VMEM((256, GROUP), BF16)]

    def exchange(values):
        return lax.all_to_all(values, PEERS, 0, 0, tiled=True)

    sources = (probe_block_qkv, tokens, block_qkv, probe_block_out, block_out, target)
    sources = [pltpu.with_memory_space_constraint(source, pltpu.HBM) for source in sources]
    pack, h0, qkv, qkvd, a, ad, o, od, sq, so = call(
        block_forward_kernel,
        [
            shaped(BF16, peers, 16, 384),
            shaped(BF16, count, 256),
            shaped(BF16, count, 768),
            shaped(BF16, count, 768),
            shaped(BF16, count, 512),
            shaped(BF16, count, 512),
            shaped(BF16, count, 256),
            shaped(BF16, count, 256),
            shaped(BF16, 256, 768),
            shaped(BF16, 256, 256),
        ],
        held(*sources) + [pltpu.VMEM((count, 256), F32)] + masks,
        "hhhhhh",
        sources,
        "block_forward",
        16,
    )
    pack = exchange(pack)
    sources = (
        probe_grid_qkv, grid_qkv, probe_grid_out, grid_out,
        probe_mlp_in, mlp_in, probe_mlp_out, mlp_out,
    )
    back, mid_keep, mid_send, sgq, sgo, smi, smo = call(
        functools.partial(middle_kernel, factor),
        [shaped(BF16, peers, 16, 256), shaped(BF16, 1536, 256), shaped(BF16, 1536, 256)]
        + [shaped(BF16, *weight.shape) for weight in sources[1::2]],
        masks
        + [pltpu.VMEM((2, count, 128), F32)] * 3
        + [pltpu.VMEM((count, 256), F32)] * 2
        + [
            pltpu.VMEM((count, 256), BF16),
            pltpu.VMEM((2 * count, 256), BF16),
            pltpu.VMEM((2 * count, 256), BF16),
            pltpu.VMEM((count, 768), BF16),
            pltpu.VMEM((count, 768), BF16),
            pltpu.VMEM((count, 512), BF16),
            pltpu.VMEM((count, 512), BF16),
            pltpu.VMEM((2 * count, 256), BF16),
            pltpu.VMEM((count, 1024), BF16),
            pltpu.VMEM((2 * count, 1024), BF16),
            pltpu.VMEM((count, 256), F32),
            pltpu.VMEM((count, 256), F32),
            pltpu.VMEM((2 * count, 256), BF16),
            pltpu.VMEM((count, 256), BF16),
            pltpu.VMEM((count, 256), BF16),
            pltpu.VMEM((2 * count, 768), BF16),
            pltpu.VMEM((12, 256, 256), BF16),
        ],
        "svvvvvvvvv",
        (core, pack, *sources),
        "middle",
        28,
    )
    mid_got = lax.ppermute(mid_send, "core", swap)
    back = exchange(back)
    keep, send = call(
        block_back_kernel,
        [shaped(BF16, 512, 256), shaped(BF16, 512, 256)],
        masks
        + [
            pltpu.VMEM((count, 256), BF16),
            pltpu.VMEM((count, 256), BF16),
            pltpu.VMEM((count, 768), BF16),
            pltpu.VMEM((4, 256, 256), BF16),
        ],
        "s" + "v" * 10,
        (core, back, h0, qkv, qkvd, a, ad, o, od, block_out, so),
        "block_back",
        12,
    )
    got = lax.ppermute(send, "core", swap)
    (parts,) = call(
        pair_sum_kernel,
        [shaped(BF16, 2048, 256)],
        [],
        "vvvv",
        (mid_keep, mid_got, keep, got),
        "pair_sum",
        8,
    )
    parts = exchange(parts.reshape(peers, 2048 // peers, 256))
    (copies,) = call(
        peer_sum_kernel,
        [shaped(BF16, peers, 2048 // peers, 256)],
        [],
        "v",
        (parts,),
        "peer_sum",
        8,
    )
    mine = exchange(copies).reshape(2048, 256)
    other = lax.ppermute(mine, "core", swap)
    results = call(
        finish_kernel,
        [
            shaped(F32, 256, 768),
            shaped(F32, 256, 256),
            shaped(F32, 256, 768),
            shaped(F32, 256, 256),
            shaped(F32, 256, 1024),
            shaped(F32, 1024, 256),
            shaped(F32, 1, 128),
        ],
        [],
        "s" + "v" * 8,
        (core, mine, other, sq, so, sgq, sgo, smi, smo),
        "finish",
        24,
    )
    return (*results[:6], results[6][0, :6])


def solution(mesh):
    fine = Mesh(mesh.devices.reshape(2, 4, 4, 2, 2), ("y_lo", "x", "z", "y_hi", "core"))
    placed = P(("y_lo", "x"), ("z", "y_hi", "core"), None)
    return jax.shard_map(
        body,
        mesh=fine,
        in_specs=(placed, placed) + (P(),) * 12,
        out_specs=(P(),) * 7,
        check_vma=False,
    )
```

```python
import functools
import math

import jax
import jax.numpy as jnp
from jax import lax
from jax.experimental import pallas as pl
from jax.experimental.pallas import tpu as pltpu
from jax.sharding import Mesh, PartitionSpec as P

F32 = jnp.float32
BF16 = jnp.bfloat16
HD = 32
WINDOW = 64
GROUP = 128
EPSILON = 1e-05
SCALE = HD ** (-0.5)
GELU_K = math.sqrt(2.0 / math.pi)
GELU_C = 0.044715
PEERS = ("y_lo", "x", "z", "y_hi")


def nn(a, b):
    return lax.dot_general(a, b, (((1,), (0,)), ((), ())), preferred_element_type=F32)


def nt(a, b):
    return lax.dot_general(a, b, (((1,), (1,)), ((), ())), preferred_element_type=F32)


def tn(a, b):
    return lax.dot_general(a, b, (((0,), (0,)), ((), ())), preferred_element_type=F32)


def lanes(*parts):
    return jnp.concatenate(parts, axis=1)


def rows(*parts):
    return jnp.concatenate(parts, axis=0)


def mean(values):
    return jnp.mean(values, axis=-1, keepdims=True)


def norm_pair(x, xd):
    center = x - mean(x)
    inverse = lax.rsqrt(mean(center * center) + EPSILON)
    h = center * inverse
    cd = xd - mean(xd)
    along = mean(h * cd)
    return h, inverse * (cd - h * along), inverse, -inverse * along


def norm_back_pair(h, hd, inverse, slope, dy, dyd):
    second = mean(dy * h)
    dx = inverse * (dy - mean(dy) - h * second)
    second_dot = mean(dyd * h + dy * hd)
    dxd = slope * dx + inverse * (dyd - mean(dyd) - hd * second - h * second_dot)
    return dx, dxd


def fetch(sources, buffers, sems):
    copies = [
        pltpu.make_async_copy(source, buffer, sems.at[i])
        for i, (source, buffer) in enumerate(zip(sources, buffers))
    ]
    for copy in copies:
        copy.start()
    return lambda *places: [copies[place].wait() for place in places]


def unpack_signs(words_ref, out_ref):
    total, width = out_ref.shape
    for start in range(0, total, 16):
        row = start + lax.broadcasted_iota(jnp.int32, (16, 1), 0)
        first = start // 30
        edge = 30 * (first + 1)
        word = jnp.broadcast_to(words_ref[first : first + 1, :], (16, width))
        shift = row - 30 * first
        if edge < start + 16:
            later = jnp.broadcast_to(words_ref[first + 1 : first + 2, :], (16, width))
            word = jnp.where(row < edge, word, later)
            shift = jnp.where(row < edge, shift, row - edge)
        bit = jnp.right_shift(word, jnp.broadcast_to(shift, (16, width))) & 1
        out_ref[start : start + 16, :] = (1 - 2 * bit).astype(F32).astype(BF16)


def fill_masks(ones_ref, mask_ref):
    head_row = lax.broadcasted_iota(jnp.int32, (256, 256), 0) // WINDOW
    head_col = lax.broadcasted_iota(jnp.int32, (256, 256), 1) // WINDOW
    ones_ref[...] = (head_row == head_col).astype(F32).astype(BF16)
    head_row = lax.broadcasted_iota(jnp.int32, (256, GROUP), 0) // WINDOW
    head_col = lax.broadcasted_iota(jnp.int32, (256, GROUP), 1) // HD
    mask_ref[...] = (head_row == head_col).astype(F32).astype(BF16)


def spread(values, mask):
    return rows(values, values, values, values) * mask


def collect(values):
    lane = lax.broadcasted_iota(jnp.int32, (WINDOW, GROUP), 1)
    parts = [values[WINDOW * i : WINDOW * (i + 1), :] for i in range(4)]
    low = jnp.where(lane < HD, parts[0], parts[1])
    high = jnp.where(lane < 3 * HD, parts[2], parts[3])
    return jnp.where(lane < 2 * HD, low, high)


BATCH = 8


def per_batch(windows, step):
    def some(i, carry):
        step(
            [
                pl.ds(pl.multiple_of((i * BATCH + n) * WINDOW, WINDOW), WINDOW)
                for n in range(BATCH)
            ]
        )
        return carry

    lax.fori_loop(0, windows // BATCH, some, 0)


def heads_of(ref, at, kind, g):
    return ref[at, pl.ds(256 * kind + GROUP * g, GROUP)]


def attend(qkv_ref, qkvd_ref, a_ref, ad_ref, o_ref, od_ref, ones_ref, mask_ref):
    def step(spots):
        ones = ones_ref[...]
        mask = mask_ref[...]
        units = [(at, g) for at in spots for g in range(2)]
        raised, scores_dot = [], []
        for at, g in units:
            q, qd = heads_of(qkv_ref, at, 0, g), heads_of(qkvd_ref, at, 0, g)
            kb = spread(heads_of(qkv_ref, at, 1, g), mask)
            kdb = spread(heads_of(qkvd_ref, at, 1, g), mask)
            raised.append(jnp.exp(nt(q, kb) * SCALE))
            scores_dot.append(nt(lanes(qd, q), lanes(kb, kdb)) * SCALE)
        sums = [nn(e.astype(BF16), ones) for e in raised]
        weights = [e / total for e, total in zip(raised, sums)]
        moved = [w * sd for w, sd in zip(weights, scores_dot)]
        sums = [nn(m.astype(BF16), ones) for m in moved]
        weights_dot = [m - w * total for m, w, total in zip(moved, weights, sums)]
        for (at, g), w, wd in zip(units, weights, weights_dot):
            a, ad = w.astype(BF16), wd.astype(BF16)
            spot = pl.ds(256 * g, 256)
            a_ref[at, spot] = a
            ad_ref[at, spot] = ad
            vb = spread(heads_of(qkv_ref, at, 2, g), mask)
            vdb = spread(heads_of(qkvd_ref, at, 2, g), mask)
            here = pl.ds(GROUP * g, GROUP)
            o_ref[at, here] = nn(a, vb).astype(BF16)
            od_ref[at, here] = nn(lanes(ad, a), rows(vb, vdb)).astype(BF16)

    per_batch(qkv_ref.shape[0] // WINDOW, step)


def attend_back(
    qkv_ref, qkvd_ref, a_ref, ad_ref, do_ref, dod_ref, dqkv_ref, dqkvd_ref, ones_ref, mask_ref
):
    def step(spots):
        ones = ones_ref[...]
        mask = mask_ref[...]
        units = [(at, g) for at in spots for g in range(2)]
        da, dad, first, second = [], [], [], []
        for at, g in units:
            here = pl.ds(GROUP * g, GROUP)
            do, dod = do_ref[at, here], dod_ref[at, here]
            vb = spread(heads_of(qkv_ref, at, 2, g), mask)
            vdb = spread(heads_of(qkvd_ref, at, 2, g), mask)
            da.append(nt(do, vb))
            dad.append(nt(lanes(dod, do), lanes(vb, vdb)))
        for (at, g), x, xd in zip(units, da, dad):
            spot = pl.ds(256 * g, 256)
            a, ad = a_ref[at, spot].astype(F32), ad_ref[at, spot].astype(F32)
            first.append((a * x).astype(BF16))
            second.append((ad * x + a * xd).astype(BF16))
        first = [nn(x, ones) for x in first]
        second = [nn(x, ones) for x in second]
        for (at, g), x, xd, total, total_dot in zip(units, da, dad, first, second):
            spot = pl.ds(256 * g, 256)
            here = pl.ds(GROUP * g, GROUP)
            qs, ks, vs = (pl.ds(256 * i + GROUP * g, GROUP) for i in range(3))
            ab, adb = a_ref[at, spot], ad_ref[at, spot]
            a, ad = ab.astype(F32), adb.astype(F32)
            rest = x - total
            rest_dot = xd - total_dot
            ds = (a * rest * SCALE).astype(BF16)
            dsd = ((ad * rest + a * rest_dot) * SCALE).astype(BF16)
            do, dod = do_ref[at, here], dod_ref[at, here]
            q, qd = qkv_ref[at, qs], qkvd_ref[at, qs]
            kb, kdb = spread(qkv_ref[at, ks], mask), spread(qkvd_ref[at, ks], mask)
            dqkvd_ref[at, qs] = nn(lanes(dsd, ds), rows(kb, kdb)).astype(BF16)
            dqkvd_ref[at, ks] = collect(tn(rows(dsd, ds), rows(q, qd))).astype(BF16)
            dqkvd_ref[at, vs] = collect(tn(rows(adb, ab), rows(do, dod))).astype(BF16)
            if dqkv_ref is not None:
                dqkv_ref[at, qs] = nn(ds, kb).astype(BF16)
                dqkv_ref[at, ks] = collect(tn(ds, q)).astype(BF16)
                dqkv_ref[at, vs] = collect(tn(ab, do)).astype(BF16)

    per_batch(qkv_ref.shape[0] // WINDOW, step)


def block_forward_kernel(
    pq_hbm, tok_hbm, wq_hbm, po_hbm, wo_hbm, tgt_hbm,
    pack_ref, qkv_ref, qkvd_ref, a_ref, ad_ref, h_hbm, o_hbm, od_hbm, sq_hbm, so_hbm,
    pq_ref, tok_ref, wq_ref, po_ref, wo_ref, tgt_ref, sems,
    h_ref, o_ref, od_ref, sq_ref, so_ref, out_sems, x_ref, ones_ref, mask_ref,
):
    wait = fetch(
        (pq_hbm, tok_hbm, wq_hbm, po_hbm, wo_hbm, tgt_hbm),
        (pq_ref, tok_ref, wq_ref, po_ref, wo_ref, tgt_ref),
        sems,
    )
    fill_masks(ones_ref, mask_ref)
    wait(0)
    unpack_signs(pq_ref, sq_ref)
    wait(1, 2)
    for half in range(2):
        at = pl.ds(256 * half, 256)
        slab = tok_ref[8 * half : 8 * half + 8].astype(F32)
        x = rows(*[slab[:, 8 * i : 8 * i + 8, :].reshape(WINDOW, 256) for i in range(4)])
        x_ref[at, :] = x
        center = x - mean(x)
        h = (center * lax.rsqrt(mean(center * center) + EPSILON)).astype(BF16)
        h_ref[at, :] = h
        qkv_ref[at, :] = nn(h, wq_ref[...]).astype(BF16)
        qkvd_ref[at, :] = nn(h, sq_ref[...]).astype(BF16)
    attend(qkv_ref, qkvd_ref, a_ref, ad_ref, o_ref, od_ref, ones_ref, mask_ref)
    wait(3, 4, 5)
    unpack_signs(po_ref, so_ref)
    saved = fetch(
        (h_ref, o_ref, od_ref, sq_ref, so_ref), (h_hbm, o_hbm, od_hbm, sq_hbm, so_hbm), out_sems
    )
    for half in range(2):
        at = pl.ds(256 * half, 256)
        out = pl.ds(32 * half, 32)
        o, od = o_ref[at, :], od_ref[at, :]
        x = x_ref[at, :] + nn(o, wo_ref[...])
        xd = nn(lanes(od, o), rows(wo_ref[...], so_ref[...]))
        both = jnp.concatenate([x.reshape(32, 8, 256), xd.reshape(32, 8, 256)], axis=1)
        pack_ref[out, :, 0:256] = both.astype(BF16)
        slab = tgt_ref[8 * half : 8 * half + 8].astype(F32)
        t = jnp.concatenate([slab[:, 8 * i : 8 * i + 8, :] for i in range(4)], axis=0)
        both = jnp.concatenate([t[:, :, 0:128], t[:, :, 128:256]], axis=1)
        pack_ref[out, :, 256:384] = both.astype(BF16)
    saved(0, 1, 2, 3, 4)


def middle_kernel(
    factor,
    core_ref, pack_ref, pq_hbm, wq_hbm, po_hbm, wo_hbm, pi_hbm, wi_hbm, pf_hbm, wf_hbm,
    back_ref, keep_ref, send_ref, sq_hbm, so_hbm, si_hbm, sf_hbm,
    pq_ref, wq_ref, po_ref, wo_ref, pi_ref, wi_ref, pf_ref, wf_ref, sems,
    sq_ref, so_ref, si_ref, sf_ref, out_sems, ones_ref, mask_ref, mix_ref, mixd_ref, mixt_ref,
    x_ref, xd_ref, t_ref, h1_ref, h2_ref, qkv_ref, qkvd_ref, a_ref, ad_ref, o_ref,
    ud_ref, dz_ref, dx_ref, dxd_ref, dg_ref, do_ref, dod_ref, dqkv_ref, hv_ref,
):
    tokens = x_ref.shape[0]
    wait = fetch(
        (pq_hbm, wq_hbm, po_hbm, wo_hbm, pi_hbm, wi_hbm, pf_hbm, wf_hbm),
        (pq_ref, wq_ref, po_ref, wo_ref, pi_ref, wi_ref, pf_ref, wf_ref),
        sems,
    )
    fill_masks(ones_ref, mask_ref)
    arrived = pack_ref[:, :, 0:256].astype(F32)
    for c in range(2):
        mix_ref[c] = arrived[:, 0:8, 128 * c : 128 * c + 128].reshape(tokens, 128)
        mixd_ref[c] = arrived[:, 8:16, 128 * c : 128 * c + 128].reshape(tokens, 128)
    arrived = pack_ref[:, :, 256:384].astype(F32) * factor
    for c in range(2):
        mixt_ref[c] = arrived[:, 8 * c : 8 * c + 8, :].reshape(tokens, 128)
    for w in range(8):
        at = pl.ds(WINDOW * w, WINDOW)
        for c in range(2):
            cols = pl.ds(128 * c, 128)
            x_ref[at, cols] = mix_ref[c, pl.ds(w, WINDOW, stride=8), :]
            xd_ref[at, cols] = mixd_ref[c, pl.ds(w, WINDOW, stride=8), :]
            t_ref[at, cols] = mixt_ref[c, pl.ds(w, WINDOW, stride=8), :].astype(BF16)
    wait(0)
    unpack_signs(pq_ref, sq_ref)
    wait(1)

    def first(i, carry):
        at = pl.ds(pl.multiple_of(i * 256, 256), 256)
        low = pl.ds(pl.multiple_of(i * 256 + tokens, 256), 256)
        h, hd, _, _ = norm_pair(x_ref[at, :], xd_ref[at, :])
        h, hd = h.astype(BF16), hd.astype(BF16)
        h1_ref[at, :] = hd
        h1_ref[low, :] = h
        qkv_ref[at, :] = nn(h, wq_ref[...]).astype(BF16)
        qkvd_ref[at, :] = nn(lanes(hd, h), rows(wq_ref[...], sq_ref[...])).astype(BF16)
        return carry

    lax.fori_loop(0, tokens // 256, first, 0)
    o_part, od_part = o_ref.at[pl.ds(tokens, tokens), :], o_ref.at[pl.ds(0, tokens), :]
    attend(qkv_ref, qkvd_ref, a_ref, ad_ref, o_part, od_part, ones_ref, mask_ref)
    wait(2, 3, 4, 5, 6, 7)
    unpack_signs(po_ref, so_ref)
    unpack_signs(pi_ref, si_ref)
    unpack_signs(pf_ref, sf_ref)
    saved = fetch(
        (sq_ref, so_ref, si_ref, sf_ref), (sq_hbm, so_hbm, si_hbm, sf_hbm), out_sems
    )

    def second(i, carry):
        at = pl.ds(pl.multiple_of(i * 256, 256), 256)
        low = pl.ds(pl.multiple_of(i * 256 + tokens, 256), 256)
        od, o = o_ref[at, :], o_ref[low, :]
        g = nn(o, wo_ref[...]).astype(BF16).astype(F32)
        gd = nn(lanes(od, o), rows(wo_ref[...], so_ref[...])).astype(BF16).astype(F32)
        h, hd, inverse, slope = norm_pair(x_ref[at, :] + g, xd_ref[at, :] + gd)
        hb, hdb = h.astype(BF16), hd.astype(BF16)
        h2_ref[at, :] = hdb
        h2_ref[low, :] = hb
        t = t_ref[at, :]
        dh = jnp.zeros((256, 256), F32)
        dhd = jnp.zeros((256, 256), F32)
        for c in range(4):
            cols = pl.ds(256 * c, 256)
            wi, si = wi_ref[:, cols], si_ref[:, cols]
            z = nn(hb, wi)
            zd = nn(lanes(hdb, hb), rows(wi, si))
            du = nt(t, wf_ref[cols, :])
            dud = nt(t, sf_ref[cols, :])
            square = z * z
            bend = jnp.tanh(z * (GELU_K + GELU_K * GELU_C * square))
            inner = GELU_K + (3.0 * GELU_K * GELU_C) * square
            flat = (1.0 - bend * bend) * inner
            half = 0.5 * z
            slope1 = 0.5 + 0.5 * bend + half * flat
            slope2 = flat * (1.0 - z * bend * inner) + (1.0 - bend * bend) * (
                3.0 * GELU_K * GELU_C
            ) * square
            ud_ref[at, cols] = (slope1 * zd).astype(BF16)
            dz = (du * slope1).astype(BF16)
            dzd = (dud * slope1 + du * slope2 * zd).astype(BF16)
            dz_ref[at, cols] = dz
            dz_ref[low, cols] = dzd
            dh = dh + nt(dz, wi)
            dhd = dhd + nt(lanes(dzd, dz), lanes(wi, si))
        dx, dxd = norm_back_pair(h, hd, inverse, slope, dh, dhd)
        dx = dx + t.astype(F32)
        dx_ref[at, :] = dx
        dxd_ref[at, :] = dxd
        dg, dgd = dx.astype(BF16), dxd.astype(BF16)
        dg_ref[at, :] = dg
        dg_ref[low, :] = dgd
        do_ref[at, :] = nt(dg, wo_ref[...]).astype(BF16)
        dod_ref[at, :] = nt(lanes(dgd, dg), lanes(wo_ref[...], so_ref[...])).astype(BF16)
        return carry

    lax.fori_loop(0, tokens // 256, second, 0)
    dqkv, dqkvd = dqkv_ref.at[pl.ds(0, tokens), :], dqkv_ref.at[pl.ds(tokens, tokens), :]
    attend_back(
        qkv_ref, qkvd_ref, a_ref, ad_ref, do_ref, dod_ref, dqkv, dqkvd, ones_ref, mask_ref
    )

    for i in range(tokens // 256):
        at = pl.ds(i * 256, 256)
        low = pl.ds(i * 256 + tokens, 256)
        dqkv, dqkvd = dqkv_ref[at, :], dqkv_ref[low, :]
        dh = nt(dqkv, wq_ref[...])
        dhd = nt(lanes(dqkvd, dqkv), lanes(wq_ref[...], sq_ref[...]))
        h, hd, inverse, slope = norm_pair(x_ref[at, :], xd_ref[at, :])
        dx, dxd = norm_back_pair(h, hd, inverse, slope, dh, dhd)
        dx_ref[at, :] += dx
        dxd_ref[at, :] += dxd
    for w in range(8):
        at = pl.ds(WINDOW * w, WINDOW)
        for c in range(2):
            cols = pl.ds(128 * c, 128)
            mix_ref[c, pl.ds(w, WINDOW, stride=8), :] = dx_ref[at, cols]
            mixd_ref[c, pl.ds(w, WINDOW, stride=8), :] = dxd_ref[at, cols]
    for c in range(2):
        dx = mix_ref[c].reshape(tokens // 8, 8, 128)
        dxd = mixd_ref[c].reshape(tokens // 8, 8, 128)
        both = jnp.concatenate([dx, dxd], axis=1)
        back_ref[:, :, 128 * c : 128 * c + 128] = both.astype(BF16)

    def put(block, value):
        hv_ref[block] = value.astype(BF16)

    h1 = h1_ref[...]
    for c in range(3):
        put(c, tn(h1, dqkv_ref[:, 256 * c : 256 * c + 256]))
    put(3, tn(o_ref[...], dg_ref[...]))
    h2 = h2_ref[...]
    for c in range(4):
        put(4 + c, tn(h2, dz_ref[:, 256 * c : 256 * c + 256]))
    t = t_ref[...]
    for c in range(4):
        put(8 + c, tn(ud_ref[:, 256 * c : 256 * c + 256], t))
    saved(0, 1, 2, 3)
    split_halves(core_ref, hv_ref, keep_ref, send_ref)


def split_halves(core_ref, hv_ref, keep_ref, send_ref):
    core = core_ref[0]
    mine = pl.ds(pl.multiple_of(core * 128, 128), 128)
    other = pl.ds(pl.multiple_of((1 - core) * 128, 128), 128)
    for block in range(hv_ref.shape[0]):
        keep_ref[128 * block : 128 * block + 128, :] = hv_ref[block, mine, :]
        send_ref[128 * block : 128 * block + 128, :] = hv_ref[block, other, :]


def block_back_kernel(
    core_ref, back_ref, qkv_ref, qkvd_ref, a_ref, ad_ref, wo_hbm, so_hbm, o_hbm, od_hbm, h_hbm,
    keep_ref, send_ref,
    wo_ref, so_ref, o_ref, od_ref, h_ref, sems,
    ones_ref, mask_ref, do_ref, dod_ref, dqkvd_ref, hv_ref,
):
    tokens = h_ref.shape[0]
    wait = fetch(
        (wo_hbm, so_hbm, o_hbm, od_hbm, h_hbm), (wo_ref, so_ref, o_ref, od_ref, h_ref), sems
    )
    fill_masks(ones_ref, mask_ref)
    arrived = back_ref[...].astype(F32)
    dx = arrived[:, 0:8, :].reshape(tokens, 256).astype(BF16)
    dxd = arrived[:, 8:16, :].reshape(tokens, 256).astype(BF16)
    wait(0, 1)
    do_ref[...] = nt(dx, wo_ref[...]).astype(BF16)
    dod_ref[...] = nt(lanes(dxd, dx), lanes(wo_ref[...], so_ref[...])).astype(BF16)
    wait(2, 3, 4)
    hv_ref[3] = tn(rows(od_ref[...], o_ref[...]), rows(dx, dxd)).astype(BF16)
    attend_back(
        qkv_ref, qkvd_ref, a_ref, ad_ref, do_ref, dod_ref, None, dqkvd_ref, ones_ref, mask_ref
    )
    h = h_ref[...]
    for c in range(3):
        hv_ref[c] = tn(h, dqkvd_ref[:, 256 * c : 256 * c + 256]).astype(BF16)
    split_halves(core_ref, hv_ref, keep_ref, send_ref)


def pair_sum_kernel(mid_keep_ref, mid_got_ref, keep_ref, got_ref, out_ref):
    count = mid_keep_ref.shape[0]
    out_ref[0:count, :] = (mid_keep_ref[...].astype(F32) + mid_got_ref[...].astype(F32)).astype(BF16)
    out_ref[count:, :] = (keep_ref[...].astype(F32) + got_ref[...].astype(F32)).astype(BF16)


def peer_sum_kernel(parts_ref, out_ref):
    total = parts_ref[0].astype(F32)
    for i in range(1, parts_ref.shape[0]):
        total = total + parts_ref[i].astype(F32)
    total = total.astype(BF16)
    for i in range(parts_ref.shape[0]):
        out_ref[i] = total


def finish_kernel(
    core_ref, mine_ref, other_ref, sbq_ref, sbo_ref, sgq_ref, sgo_ref, smi_ref, smo_ref,
    bq_ref, bo_ref, gq_ref, go_ref, mi_ref, mo_ref, trace_ref,
):
    core = core_ref[0]
    lane = lax.broadcasted_iota(jnp.int32, (1, 128), 1)
    traces = jnp.zeros((1, 128), F32)
    plan = (
        (bq_ref, sbq_ref, 12, 0),
        (bo_ref, sbo_ref, 15, 1),
        (gq_ref, sgq_ref, 0, 2),
        (go_ref, sgo_ref, 3, 3),
        (mi_ref, smi_ref, 4, 4),
        (mo_ref, smo_ref, 8, 5),
    )
    for out_ref, sign_ref, base, place in plan:
        height, width = out_ref.shape
        across = width // 256
        for block in range(height * width // 65536):
            cols = pl.ds(256 * (block % across), 256)
            down = 256 * (block // across)
            for source_ref, who in ((mine_ref, core), (other_ref, 1 - core)):
                start = pl.multiple_of(down + who * 128, 128)
                value = source_ref[128 * (base + block) : 128 * (base + block) + 128, :]
                out_ref[pl.ds(start, 128), cols] = value.astype(F32)
        total = jnp.sum(out_ref[...] * sign_ref[...].astype(F32), axis=0, keepdims=True)
        total = jnp.sum(total, axis=1, keepdims=True) / math.sqrt(height * width)
        traces = jnp.where(lane == place, total, traces)
    trace_ref[...] = traces


def shaped(dtype, *shape):
    return jax.ShapeDtypeStruct(shape, dtype)


def held(*arrays):
    buffers = [pltpu.VMEM(array.shape, array.dtype) for array in arrays]
    return buffers + [pltpu.SemaphoreType.DMA((len(arrays),))]


def call(kernel, outs, spaces, scratch, operands, places, name, limit):
    kinds = {"s": pltpu.SMEM, "v": pltpu.VMEM, "h": pltpu.HBM}
    pinned = [
        pltpu.with_memory_space_constraint(operand, pltpu.HBM) if place == "h" else operand
        for operand, place in zip(operands, places)
    ]
    return pl.pallas_call(
        kernel,
        out_shape=[
            pltpu.HBM(out.shape, out.dtype) if space == "h" else out
            for out, space in zip(outs, spaces)
        ],
        in_specs=[pl.BlockSpec(memory_space=kinds[place]) for place in places],
        out_specs=[pl.BlockSpec(memory_space=kinds[space]) for space in spaces],
        scratch_shapes=scratch,
        compiler_params=pltpu.CompilerParams(vmem_limit_bytes=limit * 2**20),
        name=name,
    )(*pinned)


MASKS = [pltpu.VMEM((256, 256), BF16), pltpu.VMEM((256, GROUP), BF16)]


def stage_forward(tokens, target, weight_qkv, weight_out, words_qkv, words_out, peers):
    count = tokens.shape[0] * tokens.shape[1]
    sources = (words_qkv, tokens, weight_qkv, words_out, weight_out, target)
    late = [
        shaped(BF16, count, 256),
        shaped(BF16, count, 256),
        shaped(BF16, count, 256),
        shaped(BF16, 256, 768),
        shaped(BF16, 256, 256),
    ]
    return call(
        block_forward_kernel,
        [
            shaped(BF16, peers, 16, 384),
            shaped(BF16, count, 768),
            shaped(BF16, count, 768),
            shaped(BF16, count, 512),
            shaped(BF16, count, 512),
        ]
        + late,
        "v" * 5 + "h" * 5,
        held(*sources) + held(*late) + [pltpu.VMEM((count, 256), F32)] + MASKS,
        sources,
        "hhhhhh",
        "block_forward",
        24,
    )


def stage_middle(core, pack, factor, sources):
    peers = pack.shape[0]
    count = peers * 8
    signs = [shaped(BF16, *weight.shape) for weight in sources[1::2]]
    return call(
        functools.partial(middle_kernel, factor),
        [shaped(BF16, peers, 16, 256), shaped(BF16, 1536, 256), shaped(BF16, 1536, 256)] + signs,
        "vvvhhhh",
        held(*sources)
        + held(*signs)
        + MASKS
        + [pltpu.VMEM((2, count, 128), F32)] * 3
        + [pltpu.VMEM((count, 256), F32)] * 2
        + [
            pltpu.VMEM((count, 256), BF16),
            pltpu.VMEM((2 * count, 256), BF16),
            pltpu.VMEM((2 * count, 256), BF16),
            pltpu.VMEM((count, 768), BF16),
            pltpu.VMEM((count, 768), BF16),
            pltpu.VMEM((count, 512), BF16),
            pltpu.VMEM((count, 512), BF16),
            pltpu.VMEM((2 * count, 256), BF16),
            pltpu.VMEM((count, 1024), BF16),
            pltpu.VMEM((2 * count, 1024), BF16),
            pltpu.VMEM((count, 256), F32),
            pltpu.VMEM((count, 256), F32),
            pltpu.VMEM((2 * count, 256), BF16),
            pltpu.VMEM((count, 256), BF16),
            pltpu.VMEM((count, 256), BF16),
            pltpu.VMEM((2 * count, 768), BF16),
            pltpu.VMEM((12, 256, 256), BF16),
        ],
        (core, pack, *sources),
        "sv" + "h" * 8,
        "middle",
        40,
    )


def stage_back(core, back, saved, weight_out):
    qkv, qkvd, a, ad, h, o, od, _, so = saved
    count = qkv.shape[0]
    late = (weight_out, so, o, od, h)
    return call(
        block_back_kernel,
        [shaped(BF16, 512, 256), shaped(BF16, 512, 256)],
        "vv",
        held(*late)
        + MASKS
        + [
            pltpu.VMEM((count, 256), BF16),
            pltpu.VMEM((count, 256), BF16),
            pltpu.VMEM((count, 768), BF16),
            pltpu.VMEM((4, 256, 256), BF16),
        ],
        (core, back, qkv, qkvd, a, ad, *late),
        "svvvvv" + "h" * 5,
        "block_back",
        20,
    )


def body(
    tokens, target, block_qkv, block_out, grid_qkv, grid_out, mlp_in, mlp_out,
    probe_block_qkv, probe_block_out, probe_grid_qkv, probe_grid_out, probe_mlp_in, probe_mlp_out,
):
    peers = lax.axis_size(PEERS)
    count = tokens.shape[0] * tokens.shape[1]
    factor = 1.0 / math.sqrt(count * peers * lax.axis_size("core"))
    core = lax.axis_index("core").astype(jnp.int32).reshape(1)
    swap = [(0, 1), (1, 0)]

    def exchange(values):
        return lax.all_to_all(values, PEERS, 0, 0, tiled=True)

    pack, *saved = stage_forward(
        tokens, target, block_qkv, block_out, probe_block_qkv, probe_block_out, peers
    )
    sources = (
        probe_grid_qkv, grid_qkv, probe_grid_out, grid_out,
        probe_mlp_in, mlp_in, probe_mlp_out, mlp_out,
    )
    back, mid_keep, mid_send, *signs = stage_middle(core, exchange(pack), factor, sources)
    mid_got = lax.ppermute(mid_send, "core", swap)
    keep, send = stage_back(core, exchange(back), saved, block_out)
    got = lax.ppermute(send, "core", swap)
    (parts,) = call(
        pair_sum_kernel,
        [shaped(BF16, 2048, 256)],
        "v",
        [],
        (mid_keep, mid_got, keep, got),
        "vvvv",
        "pair_sum",
        8,
    )
    parts = exchange(parts.reshape(peers, 2048 // peers, 256))
    (copies,) = call(
        peer_sum_kernel,
        [shaped(BF16, peers, 2048 // peers, 256)],
        "v",
        [],
        (parts,),
        "v",
        "peer_sum",
        8,
    )
    mine = exchange(copies).reshape(2048, 256)
    other = lax.ppermute(mine, "core", swap)
    weights = (block_qkv, block_out, grid_qkv, grid_out, mlp_in, mlp_out)
    results = call(
        finish_kernel,
        [shaped(F32, *weight.shape) for weight in weights] + [shaped(F32, 1, 128)],
        "v" * 7,
        [],
        (core, mine, other, *saved[7:9], *signs),
        "s" + "v" * 8,
        "finish",
        24,
    )
    return (*results[:6], results[6][0, :6])


def solution(mesh):
    fine = Mesh(mesh.devices.reshape(2, 4, 4, 2, 2), ("y_lo", "x", "z", "y_hi", "core"))
    placed = P(("y_lo", "x"), ("z", "y_hi", "core"), None)
    return jax.shard_map(
        body,
        mesh=fine,
        in_specs=(placed, placed) + (P(),) * 12,
        out_specs=(P(),) * 7,
        check_vma=False,
    )
```

```python
import functools
import math

import jax
import jax.numpy as jnp
from jax import lax
from jax.experimental import pallas as pl
from jax.experimental.pallas import tpu as pltpu
from jax.sharding import Mesh, PartitionSpec as P

F32 = jnp.float32
BF16 = jnp.bfloat16
HD = 32
WINDOW = 64
GROUP = 128
EPSILON = 1e-05
SCALE = HD ** (-0.5)
GELU_K = math.sqrt(2.0 / math.pi)
GELU_C = 0.044715
PEERS = ("y_lo", "x", "z", "y_hi")


def nn(a, b):
    return lax.dot_general(a, b, (((1,), (0,)), ((), ())), preferred_element_type=F32)


def nt(a, b):
    return lax.dot_general(a, b, (((1,), (1,)), ((), ())), preferred_element_type=F32)


def tn(a, b):
    return lax.dot_general(a, b, (((0,), (0,)), ((), ())), preferred_element_type=F32)


def lanes(*parts):
    return jnp.concatenate(parts, axis=1)


def rows(*parts):
    return jnp.concatenate(parts, axis=0)


def mean(values):
    return jnp.mean(values, axis=-1, keepdims=True)


def norm_pair(x, xd):
    center = x - mean(x)
    inverse = lax.rsqrt(mean(center * center) + EPSILON)
    h = center * inverse
    cd = xd - mean(xd)
    along = mean(h * cd)
    return h, inverse * (cd - h * along), inverse, -inverse * along


def norm_back_pair(h, hd, inverse, slope, dy, dyd):
    second = mean(dy * h)
    dx = inverse * (dy - mean(dy) - h * second)
    second_dot = mean(dyd * h + dy * hd)
    dxd = slope * dx + inverse * (dyd - mean(dyd) - hd * second - h * second_dot)
    return dx, dxd


def fetch(sources, buffers, sems):
    copies = [
        pltpu.make_async_copy(source, buffer, sems.at[i])
        for i, (source, buffer) in enumerate(zip(sources, buffers))
    ]
    for copy in copies:
        copy.start()
    return lambda *places: [copies[place].wait() for place in places]


def unpack_signs(words_ref, out_ref):
    total, width = out_ref.shape
    for start in range(0, total, 16):
        row = start + lax.broadcasted_iota(jnp.int32, (16, 1), 0)
        first = start // 30
        edge = 30 * (first + 1)
        word = jnp.broadcast_to(words_ref[first : first + 1, :], (16, width))
        shift = row - 30 * first
        if edge < start + 16:
            later = jnp.broadcast_to(words_ref[first + 1 : first + 2, :], (16, width))
            word = jnp.where(row < edge, word, later)
            shift = jnp.where(row < edge, shift, row - edge)
        bit = jnp.right_shift(word, jnp.broadcast_to(shift, (16, width))) & 1
        out_ref[start : start + 16, :] = (1 - 2 * bit).astype(F32).astype(BF16)


def fill_masks(ones_ref, mask_ref):
    head_row = lax.broadcasted_iota(jnp.int32, (256, 256), 0) // WINDOW
    head_col = lax.broadcasted_iota(jnp.int32, (256, 256), 1) // WINDOW
    ones_ref[...] = (head_row == head_col).astype(F32).astype(BF16)
    head_row = lax.broadcasted_iota(jnp.int32, (256, GROUP), 0) // WINDOW
    head_col = lax.broadcasted_iota(jnp.int32, (256, GROUP), 1) // HD
    mask_ref[...] = (head_row == head_col).astype(F32).astype(BF16)


def spread(values, mask):
    return rows(values, values, values, values) * mask


def collect(values):
    lane = lax.broadcasted_iota(jnp.int32, (WINDOW, GROUP), 1)
    parts = [values[WINDOW * i : WINDOW * (i + 1), :] for i in range(4)]
    low = jnp.where(lane < HD, parts[0], parts[1])
    high = jnp.where(lane < 3 * HD, parts[2], parts[3])
    return jnp.where(lane < 2 * HD, low, high)


BATCH = 8


def per_batch(windows, step):
    def some(i, carry):
        step(
            [
                pl.ds(pl.multiple_of((i * BATCH + n) * WINDOW, WINDOW), WINDOW)
                for n in range(BATCH)
            ]
        )
        return carry

    lax.fori_loop(0, windows // BATCH, some, 0)


def heads_of(ref, at, kind, g):
    return ref[at, pl.ds(256 * kind + GROUP * g, GROUP)]


def attend(qkv_ref, qkvd_ref, a_ref, ad_ref, o_ref, od_ref, ones_ref, mask_ref):
    def step(spots):
        ones = ones_ref[...]
        mask = mask_ref[...]
        units = [(at, g) for at in spots for g in range(2)]
        raised, scores_dot = [], []
        for at, g in units:
            q, qd = heads_of(qkv_ref, at, 0, g), heads_of(qkvd_ref, at, 0, g)
            kb = spread(heads_of(qkv_ref, at, 1, g), mask)
            kdb = spread(heads_of(qkvd_ref, at, 1, g), mask)
            raised.append(jnp.exp(nt(q, kb) * SCALE))
            scores_dot.append(nt(lanes(qd, q), lanes(kb, kdb)) * SCALE)
        sums = [nn(e.astype(BF16), ones) for e in raised]
        weights = [e / total for e, total in zip(raised, sums)]
        moved = [w * sd for w, sd in zip(weights, scores_dot)]
        sums = [nn(m.astype(BF16), ones) for m in moved]
        weights_dot = [m - w * total for m, w, total in zip(moved, weights, sums)]
        for (at, g), w, wd in zip(units, weights, weights_dot):
            a, ad = w.astype(BF16), wd.astype(BF16)
            spot = pl.ds(256 * g, 256)
            a_ref[at, spot] = a
            ad_ref[at, spot] = ad
            vb = spread(heads_of(qkv_ref, at, 2, g), mask)
            vdb = spread(heads_of(qkvd_ref, at, 2, g), mask)
            here = pl.ds(GROUP * g, GROUP)
            o_ref[at, here] = nn(a, vb).astype(BF16)
            od_ref[at, here] = nn(lanes(ad, a), rows(vb, vdb)).astype(BF16)

    per_batch(qkv_ref.shape[0] // WINDOW, step)


def attend_back(
    qkv_ref, qkvd_ref, a_ref, ad_ref, do_ref, dod_ref, dqkv_ref, dqkvd_ref, ones_ref, mask_ref
):
    def step(spots):
        ones = ones_ref[...]
        mask = mask_ref[...]
        units = [(at, g) for at in spots for g in range(2)]
        da, dad, first, second = [], [], [], []
        for at, g in units:
            here = pl.ds(GROUP * g, GROUP)
            do, dod = do_ref[at, here], dod_ref[at, here]
            vb = spread(heads_of(qkv_ref, at, 2, g), mask)
            vdb = spread(heads_of(qkvd_ref, at, 2, g), mask)
            da.append(nt(do, vb))
            dad.append(nt(lanes(dod, do), lanes(vb, vdb)))
        for (at, g), x, xd in zip(units, da, dad):
            spot = pl.ds(256 * g, 256)
            a, ad = a_ref[at, spot].astype(F32), ad_ref[at, spot].astype(F32)
            first.append((a * x).astype(BF16))
            second.append((ad * x + a * xd).astype(BF16))
        first = [nn(x, ones) for x in first]
        second = [nn(x, ones) for x in second]
        for (at, g), x, xd, total, total_dot in zip(units, da, dad, first, second):
            spot = pl.ds(256 * g, 256)
            here = pl.ds(GROUP * g, GROUP)
            qs, ks, vs = (pl.ds(256 * i + GROUP * g, GROUP) for i in range(3))
            ab, adb = a_ref[at, spot], ad_ref[at, spot]
            a, ad = ab.astype(F32), adb.astype(F32)
            rest = x - total
            rest_dot = xd - total_dot
            ds = (a * rest * SCALE).astype(BF16)
            dsd = ((ad * rest + a * rest_dot) * SCALE).astype(BF16)
            do, dod = do_ref[at, here], dod_ref[at, here]
            q, qd = qkv_ref[at, qs], qkvd_ref[at, qs]
            kb, kdb = spread(qkv_ref[at, ks], mask), spread(qkvd_ref[at, ks], mask)
            dqkvd_ref[at, qs] = nn(lanes(dsd, ds), rows(kb, kdb)).astype(BF16)
            dqkvd_ref[at, ks] = collect(tn(rows(dsd, ds), rows(q, qd))).astype(BF16)
            dqkvd_ref[at, vs] = collect(tn(rows(adb, ab), rows(do, dod))).astype(BF16)
            if dqkv_ref is not None:
                dqkv_ref[at, qs] = nn(ds, kb).astype(BF16)
                dqkv_ref[at, ks] = collect(tn(ds, q)).astype(BF16)
                dqkv_ref[at, vs] = collect(tn(ab, do)).astype(BF16)

    per_batch(qkv_ref.shape[0] // WINDOW, step)


def block_forward_kernel(
    core_ref, pq_hbm, tok_hbm, wq_hbm, po_hbm, wo_hbm, tgt_hbm,
    pack_ref, qkv_ref, qkvd_ref, a_ref, ad_ref, h_hbm, o_hbm, od_hbm, sq_hbm, so_hbm,
    pq_ref, tok_ref, wq_ref, po_ref, wo_ref, tgt_ref, sems,
    h_ref, o_ref, od_ref, sq_ref, so_ref, out_sems, x_ref, ones_ref, mask_ref,
):
    wait = fetch(
        (pq_hbm, tok_hbm, wq_hbm, po_hbm, wo_hbm, tgt_hbm),
        (pq_ref, tok_ref, wq_ref, po_ref, wo_ref, tgt_ref),
        sems,
    )
    fill_masks(ones_ref, mask_ref)
    wait(0)
    unpack_signs(pq_ref, sq_ref)
    wait(1, 2)
    for half in range(2):
        at = pl.ds(256 * half, 256)
        slab = tok_ref[8 * half : 8 * half + 8].astype(F32)
        x = rows(*[slab[:, 8 * i : 8 * i + 8, :].reshape(WINDOW, 256) for i in range(4)])
        x_ref[at, :] = x
        center = x - mean(x)
        h = (center * lax.rsqrt(mean(center * center) + EPSILON)).astype(BF16)
        h_ref[at, :] = h
        qkv_ref[at, :] = nn(h, wq_ref[...]).astype(BF16)
        qkvd_ref[at, :] = nn(h, sq_ref[...]).astype(BF16)
    attend(qkv_ref, qkvd_ref, a_ref, ad_ref, o_ref, od_ref, ones_ref, mask_ref)
    wait(3, 4, 5)
    unpack_signs(po_ref, so_ref)
    saved = fetch(
        (h_ref, o_ref, od_ref, sq_ref, so_ref), (h_hbm, o_hbm, od_hbm, sq_hbm, so_hbm), out_sems
    )
    for half in range(2):
        at = pl.ds(256 * half, 256)
        out = pl.ds(32 * half, 32)
        o, od = o_ref[at, :], od_ref[at, :]
        x = x_ref[at, :] + nn(o, wo_ref[...])
        xd = nn(lanes(od, o), rows(wo_ref[...], so_ref[...]))
        both = jnp.concatenate([x.reshape(32, 8, 256), xd.reshape(32, 8, 256)], axis=1)
        pack_ref[out, :, 0:256] = both.astype(BF16)
        slab = tgt_ref[8 * half : 8 * half + 8].astype(F32)
        t = jnp.concatenate([slab[:, 8 * i : 8 * i + 8, :] for i in range(4)], axis=0)
        both = jnp.concatenate([t[:, :, 0:128], t[:, :, 128:256]], axis=1)
        pack_ref[out, :, 256:384] = both.astype(BF16)
    saved(0, 1, 2, 3, 4)


def middle_kernel(
    factor,
    core_ref, pack_ref, pq_hbm, wq_hbm, po_hbm, wo_hbm, pi_hbm, wi_hbm, pf_hbm, wf_hbm,
    back_ref, keep_ref, send_ref, sq_hbm, so_hbm, si_hbm, sf_hbm,
    pq_ref, wq_ref, po_ref, wo_ref, pi_ref, wi_ref, pf_ref, wf_ref, sems,
    sq_ref, so_ref, si_ref, sf_ref, out_sems, ones_ref, mask_ref, mix_ref, mixd_ref, mixt_ref,
    x_ref, xd_ref, t_ref, h1_ref, h2_ref, qkv_ref, qkvd_ref, a_ref, ad_ref, o_ref,
    ud_ref, dz_ref, dx_ref, dxd_ref, dg_ref, do_ref, dod_ref, dqkv_ref, hv_ref,
):
    tokens = x_ref.shape[0]
    wait = fetch(
        (pq_hbm, wq_hbm, po_hbm, wo_hbm, pi_hbm, wi_hbm, pf_hbm, wf_hbm),
        (pq_ref, wq_ref, po_ref, wo_ref, pi_ref, wi_ref, pf_ref, wf_ref),
        sems,
    )
    fill_masks(ones_ref, mask_ref)
    arrived = pack_ref[:, :, 0:256].astype(F32)
    for c in range(2):
        mix_ref[c] = arrived[:, 0:8, 128 * c : 128 * c + 128].reshape(tokens, 128)
        mixd_ref[c] = arrived[:, 8:16, 128 * c : 128 * c + 128].reshape(tokens, 128)
    arrived = pack_ref[:, :, 256:384].astype(F32) * factor
    for c in range(2):
        mixt_ref[c] = arrived[:, 8 * c : 8 * c + 8, :].reshape(tokens, 128)
    for w in range(8):
        at = pl.ds(WINDOW * w, WINDOW)
        for c in range(2):
            cols = pl.ds(128 * c, 128)
            x_ref[at, cols] = mix_ref[c, pl.ds(w, WINDOW, stride=8), :]
            xd_ref[at, cols] = mixd_ref[c, pl.ds(w, WINDOW, stride=8), :]
            t_ref[at, cols] = mixt_ref[c, pl.ds(w, WINDOW, stride=8), :].astype(BF16)
    wait(0)
    unpack_signs(pq_ref, sq_ref)
    wait(1)

    def first(i):
        at = pl.ds(i * 256, 256)
        low = pl.ds(i * 256 + tokens, 256)
        h, hd, _, _ = norm_pair(x_ref[at, :], xd_ref[at, :])
        h, hd = h.astype(BF16), hd.astype(BF16)
        h1_ref[at, :] = hd
        h1_ref[low, :] = h
        qkv_ref[at, :] = nn(h, wq_ref[...]).astype(BF16)
        qkvd_ref[at, :] = nn(lanes(hd, h), rows(wq_ref[...], sq_ref[...])).astype(BF16)

    for i in range(tokens // 256):
        first(i)
    o_part, od_part = o_ref.at[pl.ds(tokens, tokens), :], o_ref.at[pl.ds(0, tokens), :]
    attend(qkv_ref, qkvd_ref, a_ref, ad_ref, o_part, od_part, ones_ref, mask_ref)
    wait(2, 3, 4, 5, 6, 7)
    unpack_signs(po_ref, so_ref)
    unpack_signs(pi_ref, si_ref)
    unpack_signs(pf_ref, sf_ref)
    saved = fetch(
        (sq_ref, so_ref, si_ref, sf_ref), (sq_hbm, so_hbm, si_hbm, sf_hbm), out_sems
    )

    def second(i):
        at = pl.ds(i * 256, 256)
        low = pl.ds(i * 256 + tokens, 256)
        od, o = o_ref[at, :], o_ref[low, :]
        g = nn(o, wo_ref[...]).astype(BF16).astype(F32)
        gd = nn(lanes(od, o), rows(wo_ref[...], so_ref[...])).astype(BF16).astype(F32)
        h, hd, inverse, slope = norm_pair(x_ref[at, :] + g, xd_ref[at, :] + gd)
        hb, hdb = h.astype(BF16), hd.astype(BF16)
        h2_ref[at, :] = hdb
        h2_ref[low, :] = hb
        t = t_ref[at, :]
        dh = jnp.zeros((256, 256), F32)
        dhd = jnp.zeros((256, 256), F32)
        for c in range(4):
            cols = pl.ds(256 * c, 256)
            wi, si = wi_ref[:, cols], si_ref[:, cols]
            z = nn(hb, wi)
            zd = nn(lanes(hdb, hb), rows(wi, si))
            du = nt(t, wf_ref[cols, :])
            dud = nt(t, sf_ref[cols, :])
            square = z * z
            bend = jnp.tanh(z * (GELU_K + GELU_K * GELU_C * square))
            inner = GELU_K + (3.0 * GELU_K * GELU_C) * square
            flat = (1.0 - bend * bend) * inner
            half = 0.5 * z
            slope1 = 0.5 + 0.5 * bend + half * flat
            slope2 = flat * (1.0 - z * bend * inner) + (1.0 - bend * bend) * (
                3.0 * GELU_K * GELU_C
            ) * square
            ud_ref[at, cols] = (slope1 * zd).astype(BF16)
            dz = (du * slope1).astype(BF16)
            dzd = (dud * slope1 + du * slope2 * zd).astype(BF16)
            dz_ref[at, cols] = dz
            dz_ref[low, cols] = dzd
            dh = dh + nt(dz, wi)
            dhd = dhd + nt(lanes(dzd, dz), lanes(wi, si))
        dx, dxd = norm_back_pair(h, hd, inverse, slope, dh, dhd)
        dx = dx + t.astype(F32)
        dx_ref[at, :] = dx
        dxd_ref[at, :] = dxd
        dg, dgd = dx.astype(BF16), dxd.astype(BF16)
        dg_ref[at, :] = dg
        dg_ref[low, :] = dgd
        do_ref[at, :] = nt(dg, wo_ref[...]).astype(BF16)
        dod_ref[at, :] = nt(lanes(dgd, dg), lanes(wo_ref[...], so_ref[...])).astype(BF16)

    for i in range(tokens // 256):
        second(i)
    dqkv, dqkvd = dqkv_ref.at[pl.ds(0, tokens), :], dqkv_ref.at[pl.ds(tokens, tokens), :]
    attend_back(
        qkv_ref, qkvd_ref, a_ref, ad_ref, do_ref, dod_ref, dqkv, dqkvd, ones_ref, mask_ref
    )

    for i in range(tokens // 256):
        at = pl.ds(i * 256, 256)
        low = pl.ds(i * 256 + tokens, 256)
        dqkv, dqkvd = dqkv_ref[at, :], dqkv_ref[low, :]
        dh = nt(dqkv, wq_ref[...])
        dhd = nt(lanes(dqkvd, dqkv), lanes(wq_ref[...], sq_ref[...]))
        h, hd, inverse, slope = norm_pair(x_ref[at, :], xd_ref[at, :])
        dx, dxd = norm_back_pair(h, hd, inverse, slope, dh, dhd)
        dx_ref[at, :] += dx
        dxd_ref[at, :] += dxd
    for w in range(8):
        at = pl.ds(WINDOW * w, WINDOW)
        for c in range(2):
            cols = pl.ds(128 * c, 128)
            mix_ref[c, pl.ds(w, WINDOW, stride=8), :] = dx_ref[at, cols]
            mixd_ref[c, pl.ds(w, WINDOW, stride=8), :] = dxd_ref[at, cols]
    for c in range(2):
        dx = mix_ref[c].reshape(tokens // 8, 8, 128)
        dxd = mixd_ref[c].reshape(tokens // 8, 8, 128)
        both = jnp.concatenate([dx, dxd], axis=1)
        back_ref[:, :, 128 * c : 128 * c + 128] = both.astype(BF16)

    def put(block, value):
        hv_ref[block] = value.astype(BF16)

    h1 = h1_ref[...]
    for c in range(3):
        put(c, tn(h1, dqkv_ref[:, 256 * c : 256 * c + 256]))
    put(3, tn(o_ref[...], dg_ref[...]))
    h2 = h2_ref[...]
    for c in range(4):
        put(4 + c, tn(h2, dz_ref[:, 256 * c : 256 * c + 256]))
    t = t_ref[...]
    for c in range(4):
        put(8 + c, tn(ud_ref[:, 256 * c : 256 * c + 256], t))
    saved(0, 1, 2, 3)
    split_halves(core_ref, hv_ref, keep_ref, send_ref)


def split_halves(core_ref, hv_ref, keep_ref, send_ref):
    core = core_ref[0]
    mine = pl.ds(pl.multiple_of(core * 128, 128), 128)
    other = pl.ds(pl.multiple_of((1 - core) * 128, 128), 128)
    for block in range(hv_ref.shape[0]):
        keep_ref[128 * block : 128 * block + 128, :] = hv_ref[block, mine, :]
        send_ref[128 * block : 128 * block + 128, :] = hv_ref[block, other, :]


def block_back_kernel(
    core_ref, back_ref, qkv_ref, qkvd_ref, a_ref, ad_ref, wo_hbm, so_hbm, o_hbm, od_hbm, h_hbm,
    keep_ref, send_ref,
    wo_ref, so_ref, o_ref, od_ref, h_ref, sems,
    ones_ref, mask_ref, do_ref, dod_ref, dqkvd_ref, hv_ref,
):
    tokens = h_ref.shape[0]
    wait = fetch(
        (wo_hbm, so_hbm, o_hbm, od_hbm, h_hbm), (wo_ref, so_ref, o_ref, od_ref, h_ref), sems
    )
    fill_masks(ones_ref, mask_ref)
    arrived = back_ref[...].astype(F32)
    dx = arrived[:, 0:8, :].reshape(tokens, 256).astype(BF16)
    dxd = arrived[:, 8:16, :].reshape(tokens, 256).astype(BF16)
    wait(0, 1)
    do_ref[...] = nt(dx, wo_ref[...]).astype(BF16)
    dod_ref[...] = nt(lanes(dxd, dx), lanes(wo_ref[...], so_ref[...])).astype(BF16)
    wait(2, 3, 4)
    hv_ref[3] = tn(rows(od_ref[...], o_ref[...]), rows(dx, dxd)).astype(BF16)
    attend_back(
        qkv_ref, qkvd_ref, a_ref, ad_ref, do_ref, dod_ref, None, dqkvd_ref, ones_ref, mask_ref
    )
    h = h_ref[...]
    for c in range(3):
        hv_ref[c] = tn(h, dqkvd_ref[:, 256 * c : 256 * c + 256]).astype(BF16)
    split_halves(core_ref, hv_ref, keep_ref, send_ref)


def pair_sum_kernel(mid_keep_ref, mid_got_ref, keep_ref, got_ref, out_ref):
    count = mid_keep_ref.shape[0]
    out_ref[0:count, :] = (mid_keep_ref[...].astype(F32) + mid_got_ref[...].astype(F32)).astype(BF16)
    out_ref[count:, :] = (keep_ref[...].astype(F32) + got_ref[...].astype(F32)).astype(BF16)


def peer_sum_kernel(parts_ref, out_ref):
    total = parts_ref[0].astype(F32)
    for i in range(1, parts_ref.shape[0]):
        total = total + parts_ref[i].astype(F32)
    total = total.astype(BF16)
    for i in range(parts_ref.shape[0]):
        out_ref[i] = total


PLACES = (12, 15, 0, 3, 4, 8)


def write_half(who, half_ref, sign_refs, out_hbms, wide_refs, sems):
    copies, sums = [], []
    for n, (base, sign_ref, out_hbm, wide_ref) in enumerate(
        zip(PLACES, sign_refs, out_hbms, wide_refs)
    ):
        height, width = out_hbm.shape
        across = width // 256
        total = jnp.zeros((8, 256), F32)
        for block in range(height * width // 65536):
            cols = pl.ds(256 * (block % across), 256)
            down = block // across
            at = pl.ds(pl.multiple_of(256 * down + who * 128, 128), 128)
            value = half_ref[128 * (base + block) : 128 * (base + block) + 128, :].astype(F32)
            wide_ref[128 * down : 128 * down + 128, cols] = value
            signed = value * sign_ref[at, cols].astype(F32)
            total = total + jnp.sum(signed.reshape(16, 8, 256), axis=0)
        for down in range(height // 256):
            at = pl.ds(pl.multiple_of(256 * down + who * 128, 128), 128)
            copies.append(
                pltpu.make_async_copy(
                    wide_ref.at[pl.ds(128 * down, 128), :], out_hbm.at[at, :], sems.at[len(copies)]
                )
            )
            copies[-1].start()
        sums.append(jnp.sum(total, axis=0, keepdims=True))
    for copy in copies:
        copy.wait()
    return rows(*sums, jnp.zeros((2, 256), F32))


def finish_mine_kernel(core_ref, half_ref, *refs):
    signs, outs, sum_ref, wides, sems = refs[:6], refs[6:12], refs[12], refs[13:19], refs[19]
    sum_ref[...] = write_half(core_ref[0], half_ref, signs, outs, wides, sems)


def finish_other_kernel(core_ref, half_ref, sum_ref, *refs):
    signs, outs, trace_ref, wides, sems = refs[:6], refs[12:18], refs[18], refs[19:25], refs[25]
    sums = sum_ref[...] + write_half(1 - core_ref[0], half_ref, signs, outs, wides, sems)
    for n, out in enumerate(outs):
        trace_ref[n] = jnp.sum(sums[n : n + 1, :]) / math.sqrt(out.shape[0] * out.shape[1])


def shaped(dtype, *shape):
    return jax.ShapeDtypeStruct(shape, dtype)


def held(*arrays):
    buffers = [pltpu.VMEM(array.shape, array.dtype) for array in arrays]
    return buffers + [pltpu.SemaphoreType.DMA((len(arrays),))]


def call(kernel, outs, spaces, scratch, operands, places, name, limit, aliases=None):
    kinds = {"s": pltpu.SMEM, "v": pltpu.VMEM, "h": pltpu.HBM}
    pinned = [
        pltpu.with_memory_space_constraint(operand, pltpu.HBM) if place == "h" else operand
        for operand, place in zip(operands, places)
    ]
    return pl.pallas_call(
        kernel,
        out_shape=[
            pltpu.HBM(out.shape, out.dtype) if space == "h" else out
            for out, space in zip(outs, spaces)
        ],
        in_specs=[pl.BlockSpec(memory_space=kinds[place]) for place in places],
        out_specs=[pl.BlockSpec(memory_space=kinds[space]) for space in spaces],
        scratch_shapes=scratch,
        input_output_aliases=aliases or {},
        compiler_params=pltpu.CompilerParams(vmem_limit_bytes=limit * 2**20),
        name=name,
    )(*pinned)


MASKS = [pltpu.VMEM((256, 256), BF16), pltpu.VMEM((256, GROUP), BF16)]


def stage_forward(core, tokens, target, weight_qkv, weight_out, words_qkv, words_out, peers):
    count = tokens.shape[0] * tokens.shape[1]
    sources = (words_qkv, tokens, weight_qkv, words_out, weight_out, target)
    late = [
        shaped(BF16, count, 256),
        shaped(BF16, count, 256),
        shaped(BF16, count, 256),
        shaped(BF16, 256, 768),
        shaped(BF16, 256, 256),
    ]
    return call(
        block_forward_kernel,
        [
            shaped(BF16, peers, 16, 384),
            shaped(BF16, count, 768),
            shaped(BF16, count, 768),
            shaped(BF16, count, 512),
            shaped(BF16, count, 512),
        ]
        + late,
        "v" * 5 + "h" * 5,
        held(*sources) + held(*late) + [pltpu.VMEM((count, 256), F32)] + MASKS,
        (core, *sources),
        "shhhhhh",
        "block_forward",
        24,
    )


def stage_middle(core, pack, factor, sources):
    peers = pack.shape[0]
    count = peers * 8
    signs = [shaped(BF16, *weight.shape) for weight in sources[1::2]]
    return call(
        functools.partial(middle_kernel, factor),
        [shaped(BF16, peers, 16, 256), shaped(BF16, 1536, 256), shaped(BF16, 1536, 256)] + signs,
        "vvvhhhh",
        held(*sources)
        + held(*signs)
        + MASKS
        + [pltpu.VMEM((2, count, 128), F32)] * 3
        + [pltpu.VMEM((count, 256), F32)] * 2
        + [
            pltpu.VMEM((count, 256), BF16),
            pltpu.VMEM((2 * count, 256), BF16),
            pltpu.VMEM((2 * count, 256), BF16),
            pltpu.VMEM((count, 768), BF16),
            pltpu.VMEM((count, 768), BF16),
            pltpu.VMEM((count, 512), BF16),
            pltpu.VMEM((count, 512), BF16),
            pltpu.VMEM((2 * count, 256), BF16),
            pltpu.VMEM((count, 1024), BF16),
            pltpu.VMEM((2 * count, 1024), BF16),
            pltpu.VMEM((count, 256), F32),
            pltpu.VMEM((count, 256), F32),
            pltpu.VMEM((2 * count, 256), BF16),
            pltpu.VMEM((count, 256), BF16),
            pltpu.VMEM((count, 256), BF16),
            pltpu.VMEM((2 * count, 768), BF16),
            pltpu.VMEM((12, 256, 256), BF16),
        ],
        (core, pack, *sources),
        "sv" + "h" * 8,
        "middle",
        40,
    )


def stage_back(core, back, saved, weight_out):
    qkv, qkvd, a, ad, h, o, od, _, so = saved
    count = qkv.shape[0]
    late = (weight_out, so, o, od, h)
    return call(
        block_back_kernel,
        [shaped(BF16, 512, 256), shaped(BF16, 512, 256)],
        "vv",
        held(*late)
        + MASKS
        + [
            pltpu.VMEM((count, 256), BF16),
            pltpu.VMEM((count, 256), BF16),
            pltpu.VMEM((count, 768), BF16),
            pltpu.VMEM((4, 256, 256), BF16),
        ],
        (core, back, qkv, qkvd, a, ad, *late),
        "svvvvv" + "h" * 5,
        "block_back",
        20,
    )


def body(
    tokens, target, block_qkv, block_out, grid_qkv, grid_out, mlp_in, mlp_out,
    probe_block_qkv, probe_block_out, probe_grid_qkv, probe_grid_out, probe_mlp_in, probe_mlp_out,
):
    peers = lax.axis_size(PEERS)
    count = tokens.shape[0] * tokens.shape[1]
    factor = 1.0 / math.sqrt(count * peers * lax.axis_size("core"))
    core = lax.axis_index("core").astype(jnp.int32).reshape(1)
    swap = [(0, 1), (1, 0)]

    def exchange(values):
        return lax.all_to_all(values, PEERS, 0, 0, tiled=True)

    pack, *saved = stage_forward(
        core, tokens, target, block_qkv, block_out, probe_block_qkv, probe_block_out, peers
    )
    sources = (
        probe_grid_qkv, grid_qkv, probe_grid_out, grid_out,
        probe_mlp_in, mlp_in, probe_mlp_out, mlp_out,
    )
    back, mid_keep, mid_send, *signs = stage_middle(core, exchange(pack), factor, sources)
    mid_got = lax.ppermute(mid_send, "core", swap)
    keep, send = stage_back(core, exchange(back), saved, block_out)
    got = lax.ppermute(send, "core", swap)
    (parts,) = call(
        pair_sum_kernel,
        [shaped(BF16, 2048, 256)],
        "v",
        [],
        (mid_keep, mid_got, keep, got),
        "vvvv",
        "pair_sum",
        8,
    )
    parts = exchange(parts.reshape(peers, 2048 // peers, 256))
    (copies,) = call(
        peer_sum_kernel,
        [shaped(BF16, peers, 2048 // peers, 256)],
        "v",
        [],
        (parts,),
        "v",
        "peer_sum",
        8,
    )
    mine = exchange(copies).reshape(2048, 256)
    other = lax.ppermute(mine, "core", swap)
    weights = (block_qkv, block_out, grid_qkv, grid_out, mlp_in, mlp_out)
    signs = (*saved[7:9], *signs)
    outs = [shaped(F32, *weight.shape) for weight in weights]
    wides = [pltpu.VMEM((out.shape[0] // 2, out.shape[1]), F32) for out in outs]
    wides.append(pltpu.SemaphoreType.DMA((9,)))
    *halves, sums = call(
        finish_mine_kernel,
        outs + [shaped(F32, 8, 256)],
        "hhhhhhv",
        wides,
        (core, mine, *signs),
        "s" + "v" * 7,
        "finish_mine",
        16,
    )
    return call(
        finish_other_kernel,
        outs + [shaped(F32, 6)],
        "hhhhhhs",
        wides,
        (core, other, sums, *signs, *halves),
        "s" + "v" * 8 + "h" * 6,
        "finish_other",
        16,
        {9 + n: n for n in range(6)},
    )


def solution(mesh):
    fine = Mesh(mesh.devices.reshape(2, 4, 4, 2, 2), ("y_lo", "x", "z", "y_hi", "core"))
    placed = P(("y_lo", "x"), ("z", "y_hi", "core"), None)
    return jax.shard_map(
        body,
        mesh=fine,
        in_specs=(placed, placed) + (P(),) * 12,
        out_specs=(P(),) * 7,
        check_vma=False,
    )
```

```python
import functools
import math

import jax
import jax.numpy as jnp
from jax import lax
from jax.experimental import pallas as pl
from jax.experimental.pallas import tpu as pltpu
from jax.sharding import Mesh, PartitionSpec as P

F32 = jnp.float32
BF16 = jnp.bfloat16
HD = 32
WINDOW = 64
GROUP = 128
EPSILON = 1e-05
SCALE = HD ** (-0.5)
GELU_K = math.sqrt(2.0 / math.pi)
GELU_C = 0.044715
PEERS = ("y_lo", "x", "z", "y_hi")


def nn(a, b):
    return lax.dot_general(a, b, (((1,), (0,)), ((), ())), preferred_element_type=F32)


def nt(a, b):
    return lax.dot_general(a, b, (((1,), (1,)), ((), ())), preferred_element_type=F32)


def tn(a, b):
    return lax.dot_general(a, b, (((0,), (0,)), ((), ())), preferred_element_type=F32)


def lanes(*parts):
    return jnp.concatenate(parts, axis=1)


def rows(*parts):
    return jnp.concatenate(parts, axis=0)


def mean(values):
    return jnp.mean(values, axis=-1, keepdims=True)


def norm_pair(x, xd):
    center = x - mean(x)
    inverse = lax.rsqrt(mean(center * center) + EPSILON)
    h = center * inverse
    cd = xd - mean(xd)
    along = mean(h * cd)
    return h, inverse * (cd - h * along), inverse, -inverse * along


def norm_back_pair(h, hd, inverse, slope, dy, dyd):
    second = mean(dy * h)
    dx = inverse * (dy - mean(dy) - h * second)
    second_dot = mean(dyd * h + dy * hd)
    dxd = slope * dx + inverse * (dyd - mean(dyd) - hd * second - h * second_dot)
    return dx, dxd


def fetch(sources, buffers, sems):
    copies = [
        pltpu.make_async_copy(source, buffer, sems.at[i])
        for i, (source, buffer) in enumerate(zip(sources, buffers))
    ]
    for copy in copies:
        copy.start()
    return lambda *places: [copies[place].wait() for place in places]


def unpack_signs(words_ref, out_ref):
    total, width = out_ref.shape
    for start in range(0, total, 16):
        row = start + lax.broadcasted_iota(jnp.int32, (16, 1), 0)
        first = start // 30
        edge = 30 * (first + 1)
        word = jnp.broadcast_to(words_ref[first : first + 1, :], (16, width))
        shift = row - 30 * first
        if edge < start + 16:
            later = jnp.broadcast_to(words_ref[first + 1 : first + 2, :], (16, width))
            word = jnp.where(row < edge, word, later)
            shift = jnp.where(row < edge, shift, row - edge)
        bit = jnp.right_shift(word, jnp.broadcast_to(shift, (16, width))) & 1
        out_ref[start : start + 16, :] = (1 - 2 * bit).astype(F32).astype(BF16)


def fill_masks(ones_ref, mask_ref):
    head_row = lax.broadcasted_iota(jnp.int32, (256, 256), 0) // WINDOW
    head_col = lax.broadcasted_iota(jnp.int32, (256, 256), 1) // WINDOW
    ones_ref[...] = (head_row == head_col).astype(F32).astype(BF16)
    head_row = lax.broadcasted_iota(jnp.int32, (256, GROUP), 0) // WINDOW
    head_col = lax.broadcasted_iota(jnp.int32, (256, GROUP), 1) // HD
    mask_ref[...] = (head_row == head_col).astype(F32).astype(BF16)


def spread(values, mask):
    return rows(values, values, values, values) * mask


def collect(values):
    lane = lax.broadcasted_iota(jnp.int32, (WINDOW, GROUP), 1)
    parts = [values[WINDOW * i : WINDOW * (i + 1), :] for i in range(4)]
    low = jnp.where(lane < HD, parts[0], parts[1])
    high = jnp.where(lane < 3 * HD, parts[2], parts[3])
    return jnp.where(lane < 2 * HD, low, high)


BATCH = 8


def per_batch(windows, step):
    def some(i, carry):
        step(
            [
                pl.ds(pl.multiple_of((i * BATCH + n) * WINDOW, WINDOW), WINDOW)
                for n in range(BATCH)
            ]
        )
        return carry

    lax.fori_loop(0, windows // BATCH, some, 0)


def heads_of(ref, at, kind, g):
    return ref[at, pl.ds(256 * kind + GROUP * g, GROUP)]


def twice(values, dots):
    return rows(lanes(values, jnp.zeros_like(values)), lanes(dots, values))


def segment_sums(values, ones):
    total = nn(rows(*[value.astype(BF16) for value in values]), ones)
    return [total[WINDOW * i : WINDOW * (i + 1), :] for i in range(len(values))]


def attend(qkv_ref, qkvd_ref, a_ref, ad_ref, o_ref, od_ref, ones_ref, mask_ref):
    def step(spots):
        ones = ones_ref[...]
        mask = mask_ref[...]
        units = [(at, g) for at in spots for g in range(2)]
        raised, scores_dot = [], []
        for at, g in units:
            q, qd = heads_of(qkv_ref, at, 0, g), heads_of(qkvd_ref, at, 0, g)
            kb = spread(heads_of(qkv_ref, at, 1, g), mask)
            kdb = spread(heads_of(qkvd_ref, at, 1, g), mask)
            both = nt(twice(q, qd), lanes(kb, kdb)) * SCALE
            raised.append(jnp.exp(both[:WINDOW]))
            scores_dot.append(both[WINDOW:])
        weights = [e / total for e, total in zip(raised, segment_sums(raised, ones))]
        moved = [w * sd for w, sd in zip(weights, scores_dot)]
        sums = segment_sums(moved, ones)
        weights_dot = [m - w * total for m, w, total in zip(moved, weights, sums)]
        for (at, g), w, wd in zip(units, weights, weights_dot):
            a, ad = w.astype(BF16), wd.astype(BF16)
            spot = pl.ds(256 * g, 256)
            a_ref[at, spot] = a
            ad_ref[at, spot] = ad
            vb = spread(heads_of(qkv_ref, at, 2, g), mask)
            vdb = spread(heads_of(qkvd_ref, at, 2, g), mask)
            here = pl.ds(GROUP * g, GROUP)
            both = nn(twice(a, ad), rows(vb, vdb)).astype(BF16)
            o_ref[at, here] = both[:WINDOW]
            od_ref[at, here] = both[WINDOW:]

    per_batch(qkv_ref.shape[0] // WINDOW, step)


def attend_back(
    qkv_ref, qkvd_ref, a_ref, ad_ref, do_ref, dod_ref, dqkv_ref, dqkvd_ref, ones_ref, mask_ref
):
    def step(spots):
        ones = ones_ref[...]
        mask = mask_ref[...]
        units = [(at, g) for at in spots for g in range(2)]
        da, dad, first, second = [], [], [], []
        for at, g in units:
            here = pl.ds(GROUP * g, GROUP)
            vb = spread(heads_of(qkv_ref, at, 2, g), mask)
            vdb = spread(heads_of(qkvd_ref, at, 2, g), mask)
            both = nt(twice(do_ref[at, here], dod_ref[at, here]), lanes(vb, vdb))
            da.append(both[:WINDOW])
            dad.append(both[WINDOW:])
        for (at, g), x, xd in zip(units, da, dad):
            spot = pl.ds(256 * g, 256)
            a, ad = a_ref[at, spot].astype(F32), ad_ref[at, spot].astype(F32)
            first.append(a * x)
            second.append(ad * x + a * xd)
        first, second = segment_sums(first, ones), segment_sums(second, ones)
        for (at, g), x, xd, total, total_dot in zip(units, da, dad, first, second):
            spot = pl.ds(256 * g, 256)
            here = pl.ds(GROUP * g, GROUP)
            qs, ks, vs = (pl.ds(256 * i + GROUP * g, GROUP) for i in range(3))
            ab, adb = a_ref[at, spot], ad_ref[at, spot]
            a, ad = ab.astype(F32) * SCALE, adb.astype(F32) * SCALE
            rest = x - total
            rest_dot = xd - total_dot
            ds = (a * rest).astype(BF16)
            dsd = (ad * rest + a * rest_dot).astype(BF16)
            do, dod = do_ref[at, here], dod_ref[at, here]
            q, qd = qkv_ref[at, qs], qkvd_ref[at, qs]
            kb, kdb = spread(qkv_ref[at, ks], mask), spread(qkvd_ref[at, ks], mask)
            if dqkv_ref is None:
                dqkvd_ref[at, qs] = nn(lanes(dsd, ds), rows(kb, kdb)).astype(BF16)
                dqkvd_ref[at, ks] = collect(tn(rows(dsd, ds), rows(q, qd))).astype(BF16)
                dqkvd_ref[at, vs] = collect(tn(rows(adb, ab), rows(do, dod))).astype(BF16)
            else:
                both = nn(twice(ds, dsd), rows(kb, kdb)).astype(BF16)
                dqkv_ref[at, qs] = both[:WINDOW]
                dqkvd_ref[at, qs] = both[WINDOW:]
                both = tn(rows(dsd, ds), twice(q, qd))
                dqkvd_ref[at, ks] = collect(both[:, :GROUP]).astype(BF16)
                dqkv_ref[at, ks] = collect(both[:, GROUP:]).astype(BF16)
                both = tn(rows(adb, ab), twice(do, dod))
                dqkvd_ref[at, vs] = collect(both[:, :GROUP]).astype(BF16)
                dqkv_ref[at, vs] = collect(both[:, GROUP:]).astype(BF16)

    per_batch(qkv_ref.shape[0] // WINDOW, step)


def block_forward_kernel(
    core_ref, pq_hbm, tok_hbm, wq_hbm, po_hbm, wo_hbm, tgt_hbm,
    pack_ref, qkv_ref, qkvd_ref, a_ref, ad_ref, h_hbm, o_hbm, od_hbm, sq_hbm, so_hbm,
    pq_ref, tok_ref, wq_ref, po_ref, wo_ref, tgt_ref, sems,
    h_ref, o_ref, od_ref, sq_ref, so_ref, out_sems, x_ref, ones_ref, mask_ref,
):
    wait = fetch(
        (pq_hbm, tok_hbm, wq_hbm, po_hbm, wo_hbm, tgt_hbm),
        (pq_ref, tok_ref, wq_ref, po_ref, wo_ref, tgt_ref),
        sems,
    )
    fill_masks(ones_ref, mask_ref)
    wait(0)
    unpack_signs(pq_ref, sq_ref)
    wait(1, 2)
    for half in range(2):
        at = pl.ds(256 * half, 256)
        slab = tok_ref[8 * half : 8 * half + 8].astype(F32)
        x = rows(*[slab[:, 8 * i : 8 * i + 8, :].reshape(WINDOW, 256) for i in range(4)])
        x_ref[at, :] = x
        center = x - mean(x)
        h = (center * lax.rsqrt(mean(center * center) + EPSILON)).astype(BF16)
        h_ref[at, :] = h
        qkv_ref[at, :] = nn(h, wq_ref[...]).astype(BF16)
        qkvd_ref[at, :] = nn(h, sq_ref[...]).astype(BF16)
    attend(qkv_ref, qkvd_ref, a_ref, ad_ref, o_ref, od_ref, ones_ref, mask_ref)
    wait(3, 4, 5)
    unpack_signs(po_ref, so_ref)
    saved = fetch(
        (h_ref, o_ref, od_ref, sq_ref, so_ref), (h_hbm, o_hbm, od_hbm, sq_hbm, so_hbm), out_sems
    )
    for half in range(2):
        at = pl.ds(256 * half, 256)
        out = pl.ds(32 * half, 32)
        o, od = o_ref[at, :], od_ref[at, :]
        x = x_ref[at, :] + nn(o, wo_ref[...])
        xd = nn(lanes(od, o), rows(wo_ref[...], so_ref[...]))
        both = jnp.concatenate([x.reshape(32, 8, 256), xd.reshape(32, 8, 256)], axis=1)
        pack_ref[out, :, 0:256] = both.astype(BF16)
        slab = tgt_ref[8 * half : 8 * half + 8].astype(F32)
        t = jnp.concatenate([slab[:, 8 * i : 8 * i + 8, :] for i in range(4)], axis=0)
        both = jnp.concatenate([t[:, :, 0:128], t[:, :, 128:256]], axis=1)
        pack_ref[out, :, 256:384] = both.astype(BF16)
    saved(0, 1, 2, 3, 4)


def middle_kernel(
    factor,
    core_ref, pack_ref, pq_ref, wq_ref, po_ref, wo_ref, pi_ref, wi_ref, pf_ref, wf_ref,
    back_ref, keep_ref, send_ref, sq_hbm, so_hbm, si_hbm, sf_hbm,
    sq_ref, so_ref, si_ref, sf_ref, out_sems, ones_ref, mask_ref, mix_ref, mixd_ref, mixt_ref,
    x_ref, xd_ref, t_ref, h1_ref, h2_ref, qkv_ref, qkvd_ref, a_ref, ad_ref, o_ref,
    ud_ref, dz_ref, dx_ref, dxd_ref, dg_ref, do_ref, dod_ref, dqkv_ref, hv_ref,
):
    tokens = x_ref.shape[0]
    fill_masks(ones_ref, mask_ref)
    arrived = pack_ref[:, :, 0:256].astype(F32)
    for c in range(2):
        mix_ref[c] = arrived[:, 0:8, 128 * c : 128 * c + 128].reshape(tokens, 128)
        mixd_ref[c] = arrived[:, 8:16, 128 * c : 128 * c + 128].reshape(tokens, 128)
    arrived = pack_ref[:, :, 256:384].astype(F32) * factor
    for c in range(2):
        mixt_ref[c] = arrived[:, 8 * c : 8 * c + 8, :].reshape(tokens, 128)
    for w in range(8):
        at = pl.ds(WINDOW * w, WINDOW)
        for c in range(2):
            cols = pl.ds(128 * c, 128)
            x_ref[at, cols] = mix_ref[c, pl.ds(w, WINDOW, stride=8), :]
            xd_ref[at, cols] = mixd_ref[c, pl.ds(w, WINDOW, stride=8), :]
            t_ref[at, cols] = mixt_ref[c, pl.ds(w, WINDOW, stride=8), :].astype(BF16)
    unpack_signs(pq_ref, sq_ref)

    def first(i):
        at = pl.ds(i * 256, 256)
        low = pl.ds(i * 256 + tokens, 256)
        h, hd, _, _ = norm_pair(x_ref[at, :], xd_ref[at, :])
        h, hd = h.astype(BF16), hd.astype(BF16)
        h1_ref[at, :] = hd
        h1_ref[low, :] = h
        qkv_ref[at, :] = nn(h, wq_ref[...]).astype(BF16)
        qkvd_ref[at, :] = nn(lanes(hd, h), rows(wq_ref[...], sq_ref[...])).astype(BF16)

    for i in range(tokens // 256):
        first(i)
    o_part, od_part = o_ref.at[pl.ds(tokens, tokens), :], o_ref.at[pl.ds(0, tokens), :]
    attend(qkv_ref, qkvd_ref, a_ref, ad_ref, o_part, od_part, ones_ref, mask_ref)
    unpack_signs(po_ref, so_ref)
    unpack_signs(pi_ref, si_ref)
    unpack_signs(pf_ref, sf_ref)
    saved = fetch(
        (sq_ref, so_ref, si_ref, sf_ref), (sq_hbm, so_hbm, si_hbm, sf_hbm), out_sems
    )

    def second(i):
        at = pl.ds(i * 512, 512)
        low = pl.ds(i * 512 + tokens, 512)
        od, o = o_ref[at, :], o_ref[low, :]
        g = nn(o, wo_ref[...]).astype(BF16).astype(F32)
        gd = nn(lanes(od, o), rows(wo_ref[...], so_ref[...])).astype(BF16).astype(F32)
        h, hd, inverse, slope = norm_pair(x_ref[at, :] + g, xd_ref[at, :] + gd)
        hb, hdb = h.astype(BF16), hd.astype(BF16)
        h2_ref[at, :] = hdb
        h2_ref[low, :] = hb
        t = t_ref[at, :]
        dh = jnp.zeros((512, 256), F32)
        dhd = jnp.zeros((512, 256), F32)
        for c in range(4):
            cols = pl.ds(256 * c, 256)
            wi, si = wi_ref[:, cols], si_ref[:, cols]
            z = nn(hb, wi)
            zd = nn(lanes(hdb, hb), rows(wi, si))
            du = nt(t, wf_ref[cols, :])
            dud = nt(t, sf_ref[cols, :])
            square = z * z
            bend = jnp.tanh(z * (GELU_K + GELU_K * GELU_C * square))
            inner = GELU_K + (3.0 * GELU_K * GELU_C) * square
            flat = (1.0 - bend * bend) * inner
            half = 0.5 * z
            slope1 = 0.5 + 0.5 * bend + half * flat
            slope2 = flat * (1.0 - z * bend * inner) + (1.0 - bend * bend) * (
                3.0 * GELU_K * GELU_C
            ) * square
            ud_ref[at, cols] = (slope1 * zd).astype(BF16)
            dz = (du * slope1).astype(BF16)
            dzd = (dud * slope1 + du * slope2 * zd).astype(BF16)
            dz_ref[at, cols] = dz
            dz_ref[low, cols] = dzd
            dh = dh + nt(dz, wi)
            dhd = dhd + nt(lanes(dzd, dz), lanes(wi, si))
        dx, dxd = norm_back_pair(h, hd, inverse, slope, dh, dhd)
        dx = dx + t.astype(F32)
        dx_ref[at, :] = dx
        dxd_ref[at, :] = dxd
        dg, dgd = dx.astype(BF16), dxd.astype(BF16)
        dg_ref[at, :] = dg
        dg_ref[low, :] = dgd
        do_ref[at, :] = nt(dg, wo_ref[...]).astype(BF16)
        dod_ref[at, :] = nt(lanes(dgd, dg), lanes(wo_ref[...], so_ref[...])).astype(BF16)

    for i in range(tokens // 512):
        second(i)
    dqkv, dqkvd = dqkv_ref.at[pl.ds(0, tokens), :], dqkv_ref.at[pl.ds(tokens, tokens), :]
    attend_back(
        qkv_ref, qkvd_ref, a_ref, ad_ref, do_ref, dod_ref, dqkv, dqkvd, ones_ref, mask_ref
    )

    for i in range(tokens // 256):
        at = pl.ds(i * 256, 256)
        low = pl.ds(i * 256 + tokens, 256)
        dqkv, dqkvd = dqkv_ref[at, :], dqkv_ref[low, :]
        dh = nt(dqkv, wq_ref[...])
        dhd = nt(lanes(dqkvd, dqkv), lanes(wq_ref[...], sq_ref[...]))
        h, hd, inverse, slope = norm_pair(x_ref[at, :], xd_ref[at, :])
        dx, dxd = norm_back_pair(h, hd, inverse, slope, dh, dhd)
        dx_ref[at, :] += dx
        dxd_ref[at, :] += dxd
    for w in range(8):
        at = pl.ds(WINDOW * w, WINDOW)
        for c in range(2):
            cols = pl.ds(128 * c, 128)
            mix_ref[c, pl.ds(w, WINDOW, stride=8), :] = dx_ref[at, cols]
            mixd_ref[c, pl.ds(w, WINDOW, stride=8), :] = dxd_ref[at, cols]
    for c in range(2):
        dx = mix_ref[c].reshape(tokens // 8, 8, 128)
        dxd = mixd_ref[c].reshape(tokens // 8, 8, 128)
        both = jnp.concatenate([dx, dxd], axis=1)
        back_ref[:, :, 128 * c : 128 * c + 128] = both.astype(BF16)

    def put(block, value):
        hv_ref[block] = value.astype(BF16)

    h1 = h1_ref[...]
    for c in range(3):
        put(c, tn(h1, dqkv_ref[:, 256 * c : 256 * c + 256]))
    put(3, tn(o_ref[...], dg_ref[...]))
    h2 = h2_ref[...]
    for c in range(4):
        put(4 + c, tn(h2, dz_ref[:, 256 * c : 256 * c + 256]))
    t = t_ref[...]
    for c in range(4):
        put(8 + c, tn(ud_ref[:, 256 * c : 256 * c + 256], t))
    saved(0, 1, 2, 3)
    split_halves(core_ref, hv_ref, keep_ref, send_ref)


def split_halves(core_ref, hv_ref, keep_ref, send_ref):
    core = core_ref[0]
    mine = pl.ds(pl.multiple_of(core * 128, 128), 128)
    other = pl.ds(pl.multiple_of((1 - core) * 128, 128), 128)
    for block in range(hv_ref.shape[0]):
        keep_ref[128 * block : 128 * block + 128, :] = hv_ref[block, mine, :]
        send_ref[128 * block : 128 * block + 128, :] = hv_ref[block, other, :]


def block_back_kernel(
    core_ref, back_ref, qkv_ref, qkvd_ref, a_ref, ad_ref, wo_ref, so_ref, o_ref, od_ref, h_ref,
    keep_ref, send_ref,
    ones_ref, mask_ref, do_ref, dod_ref, dqkvd_ref, hv_ref,
):
    tokens = h_ref.shape[0]
    fill_masks(ones_ref, mask_ref)
    arrived = back_ref[...].astype(F32)
    dx = arrived[:, 0:8, :].reshape(tokens, 256).astype(BF16)
    dxd = arrived[:, 8:16, :].reshape(tokens, 256).astype(BF16)
    do_ref[...] = nt(dx, wo_ref[...]).astype(BF16)
    dod_ref[...] = nt(lanes(dxd, dx), lanes(wo_ref[...], so_ref[...])).astype(BF16)
    hv_ref[3] = tn(rows(od_ref[...], o_ref[...]), rows(dx, dxd)).astype(BF16)
    attend_back(
        qkv_ref, qkvd_ref, a_ref, ad_ref, do_ref, dod_ref, None, dqkvd_ref, ones_ref, mask_ref
    )
    h = h_ref[...]
    for c in range(3):
        hv_ref[c] = tn(h, dqkvd_ref[:, 256 * c : 256 * c + 256]).astype(BF16)
    split_halves(core_ref, hv_ref, keep_ref, send_ref)


def pair_sum_kernel(mid_keep_ref, mid_got_ref, keep_ref, got_ref, out_ref):
    count = mid_keep_ref.shape[0]
    out_ref[0:count, :] = (mid_keep_ref[...].astype(F32) + mid_got_ref[...].astype(F32)).astype(BF16)
    out_ref[count:, :] = (keep_ref[...].astype(F32) + got_ref[...].astype(F32)).astype(BF16)


def peer_sum_kernel(parts_ref, out_ref):
    total = parts_ref[0].astype(F32)
    for i in range(1, parts_ref.shape[0]):
        total = total + parts_ref[i].astype(F32)
    total = total.astype(BF16)
    for i in range(parts_ref.shape[0]):
        out_ref[i] = total


PLACES = (12, 15, 0, 3, 4, 8)


def write_half(who, half_ref, sign_refs, out_hbms, wide_refs, sems):
    copies, sums = [], []
    for n, (base, sign_ref, out_hbm, wide_ref) in enumerate(
        zip(PLACES, sign_refs, out_hbms, wide_refs)
    ):
        height, width = out_hbm.shape
        across = width // 256
        total = jnp.zeros((8, 256), F32)
        for block in range(height * width // 65536):
            cols = pl.ds(256 * (block % across), 256)
            down = block // across
            at = pl.ds(pl.multiple_of(256 * down + who * 128, 128), 128)
            value = half_ref[128 * (base + block) : 128 * (base + block) + 128, :].astype(F32)
            wide_ref[128 * down : 128 * down + 128, cols] = value
            signed = value * sign_ref[at, cols].astype(F32)
            total = total + jnp.sum(signed.reshape(16, 8, 256), axis=0)
        for down in range(height // 256):
            at = pl.ds(pl.multiple_of(256 * down + who * 128, 128), 128)
            copies.append(
                pltpu.make_async_copy(
                    wide_ref.at[pl.ds(128 * down, 128), :], out_hbm.at[at, :], sems.at[len(copies)]
                )
            )
            copies[-1].start()
        sums.append(jnp.sum(total, axis=0, keepdims=True))
    for copy in copies:
        copy.wait()
    return rows(*sums, jnp.zeros((2, 256), F32))


def finish_mine_kernel(core_ref, half_ref, *refs):
    signs, outs, sum_ref, wides, sems = refs[:6], refs[6:12], refs[12], refs[13:19], refs[19]
    sum_ref[...] = write_half(core_ref[0], half_ref, signs, outs, wides, sems)


def finish_other_kernel(core_ref, half_ref, sum_ref, *refs):
    signs, outs, trace_ref, wides, sems = refs[:6], refs[12:18], refs[18], refs[19:25], refs[25]
    sums = sum_ref[...] + write_half(1 - core_ref[0], half_ref, signs, outs, wides, sems)
    for n, out in enumerate(outs):
        trace_ref[n] = jnp.sum(sums[n : n + 1, :]) / math.sqrt(out.shape[0] * out.shape[1])


def shaped(dtype, *shape):
    return jax.ShapeDtypeStruct(shape, dtype)


def held(*arrays):
    buffers = [pltpu.VMEM(array.shape, array.dtype) for array in arrays]
    return buffers + [pltpu.SemaphoreType.DMA((len(arrays),))]


def call(kernel, outs, spaces, scratch, operands, places, name, limit, aliases=None):
    kinds = {"s": pltpu.SMEM, "v": pltpu.VMEM, "h": pltpu.HBM}
    pinned = [
        pltpu.with_memory_space_constraint(operand, pltpu.HBM) if place == "h" else operand
        for operand, place in zip(operands, places)
    ]
    return pl.pallas_call(
        kernel,
        out_shape=[
            pltpu.HBM(out.shape, out.dtype) if space == "h" else out
            for out, space in zip(outs, spaces)
        ],
        in_specs=[pl.BlockSpec(memory_space=kinds[place]) for place in places],
        out_specs=[pl.BlockSpec(memory_space=kinds[space]) for space in spaces],
        scratch_shapes=scratch,
        input_output_aliases=aliases or {},
        compiler_params=pltpu.CompilerParams(vmem_limit_bytes=limit * 2**20),
        name=name,
    )(*pinned)


MASKS = [pltpu.VMEM((256, 256), BF16), pltpu.VMEM((256, GROUP), BF16)]


def stage_forward(core, tokens, target, weight_qkv, weight_out, words_qkv, words_out, peers):
    count = tokens.shape[0] * tokens.shape[1]
    sources = (words_qkv, tokens, weight_qkv, words_out, weight_out, target)
    late = [
        shaped(BF16, count, 256),
        shaped(BF16, count, 256),
        shaped(BF16, count, 256),
        shaped(BF16, 256, 768),
        shaped(BF16, 256, 256),
    ]
    return call(
        block_forward_kernel,
        [
            shaped(BF16, peers, 16, 384),
            shaped(BF16, count, 768),
            shaped(BF16, count, 768),
            shaped(BF16, count, 512),
            shaped(BF16, count, 512),
        ]
        + late,
        "v" * 5 + "h" * 5,
        held(*sources) + held(*late) + [pltpu.VMEM((count, 256), F32)] + MASKS,
        (core, *sources),
        "shhhhhh",
        "block_forward",
        24,
    )


def stage_middle(core, pack, factor, sources):
    peers = pack.shape[0]
    count = peers * 8
    signs = [shaped(BF16, *weight.shape) for weight in sources[1::2]]
    return call(
        functools.partial(middle_kernel, factor),
        [shaped(BF16, peers, 16, 256), shaped(BF16, 1536, 256), shaped(BF16, 1536, 256)] + signs,
        "vvvhhhh",
        held(*signs)
        + MASKS
        + [pltpu.VMEM((2, count, 128), F32)] * 3
        + [pltpu.VMEM((count, 256), F32)] * 2
        + [
            pltpu.VMEM((count, 256), BF16),
            pltpu.VMEM((2 * count, 256), BF16),
            pltpu.VMEM((2 * count, 256), BF16),
            pltpu.VMEM((count, 768), BF16),
            pltpu.VMEM((count, 768), BF16),
            pltpu.VMEM((count, 512), BF16),
            pltpu.VMEM((count, 512), BF16),
            pltpu.VMEM((2 * count, 256), BF16),
            pltpu.VMEM((count, 1024), BF16),
            pltpu.VMEM((2 * count, 1024), BF16),
            pltpu.VMEM((count, 256), F32),
            pltpu.VMEM((count, 256), F32),
            pltpu.VMEM((2 * count, 256), BF16),
            pltpu.VMEM((count, 256), BF16),
            pltpu.VMEM((count, 256), BF16),
            pltpu.VMEM((2 * count, 768), BF16),
            pltpu.VMEM((12, 256, 256), BF16),
        ],
        (core, pack, *sources),
        "s" + "v" * 9,
        "middle",
        40,
    )


def stage_back(core, back, saved, weight_out):
    qkv, qkvd, a, ad, h, o, od, _, so = saved
    count = qkv.shape[0]
    late = (weight_out, so, o, od, h)
    return call(
        block_back_kernel,
        [shaped(BF16, 512, 256), shaped(BF16, 512, 256)],
        "vv",
        MASKS
        + [
            pltpu.VMEM((count, 256), BF16),
            pltpu.VMEM((count, 256), BF16),
            pltpu.VMEM((count, 768), BF16),
            pltpu.VMEM((4, 256, 256), BF16),
        ],
        (core, back, qkv, qkvd, a, ad, *late),
        "s" + "v" * 10,
        "block_back",
        20,
    )


def body(
    tokens, target, block_qkv, block_out, grid_qkv, grid_out, mlp_in, mlp_out,
    probe_block_qkv, probe_block_out, probe_grid_qkv, probe_grid_out, probe_mlp_in, probe_mlp_out,
):
    peers = lax.axis_size(PEERS)
    count = tokens.shape[0] * tokens.shape[1]
    factor = 1.0 / math.sqrt(count * peers * lax.axis_size("core"))
    core = lax.axis_index("core").astype(jnp.int32).reshape(1)
    swap = [(0, 1), (1, 0)]

    def exchange(values):
        return lax.all_to_all(values, PEERS, 0, 0, tiled=True)

    pack, *saved = stage_forward(
        core, tokens, target, block_qkv, block_out, probe_block_qkv, probe_block_out, peers
    )
    sources = (
        probe_grid_qkv, grid_qkv, probe_grid_out, grid_out,
        probe_mlp_in, mlp_in, probe_mlp_out, mlp_out,
    )
    back, mid_keep, mid_send, *signs = stage_middle(core, exchange(pack), factor, sources)
    mid_got = lax.ppermute(mid_send, "core", swap)
    keep, send = stage_back(core, exchange(back), saved, block_out)
    got = lax.ppermute(send, "core", swap)
    (parts,) = call(
        pair_sum_kernel,
        [shaped(BF16, 2048, 256)],
        "v",
        [],
        (mid_keep, mid_got, keep, got),
        "vvvv",
        "pair_sum",
        8,
    )
    parts = exchange(parts.reshape(peers, 2048 // peers, 256))
    (copies,) = call(
        peer_sum_kernel,
        [shaped(BF16, peers, 2048 // peers, 256)],
        "v",
        [],
        (parts,),
        "v",
        "peer_sum",
        8,
    )
    mine = exchange(copies).reshape(2048, 256)
    other = lax.ppermute(mine, "core", swap)
    weights = (block_qkv, block_out, grid_qkv, grid_out, mlp_in, mlp_out)
    signs = (*saved[7:9], *signs)
    outs = [shaped(F32, *weight.shape) for weight in weights]
    wides = [pltpu.VMEM((out.shape[0] // 2, out.shape[1]), F32) for out in outs]
    wides.append(pltpu.SemaphoreType.DMA((9,)))
    *halves, sums = call(
        finish_mine_kernel,
        outs + [shaped(F32, 8, 256)],
        "hhhhhhv",
        wides,
        (core, mine, *signs),
        "s" + "v" * 7,
        "finish_mine",
        16,
    )
    return call(
        finish_other_kernel,
        outs + [shaped(F32, 6)],
        "hhhhhhs",
        wides,
        (core, other, sums, *signs, *halves),
        "s" + "v" * 8 + "h" * 6,
        "finish_other",
        16,
        {9 + n: n for n in range(6)},
    )


def solution(mesh):
    fine = Mesh(mesh.devices.reshape(2, 4, 4, 2, 2), ("y_lo", "x", "z", "y_hi", "core"))
    placed = P(("y_lo", "x"), ("z", "y_hi", "core"), None)
    return jax.shard_map(
        body,
        mesh=fine,
        in_specs=(placed, placed) + (P(),) * 12,
        out_specs=(P(),) * 7,
        check_vma=False,
    )
```

```python
import functools
import math

import jax
import jax.numpy as jnp
from jax import lax
from jax.experimental import pallas as pl
from jax.experimental.pallas import tpu as pltpu
from jax.sharding import Mesh, PartitionSpec as P

F32 = jnp.float32
BF16 = jnp.bfloat16
HD = 32
WINDOW = 64
GROUP = 128
EPSILON = 1e-05
SCALE = HD ** (-0.5)
GELU_K = math.sqrt(2.0 / math.pi)
GELU_C = 0.044715
PEERS = ("x", "z", "y_hi", "y_lo")


def nn(a, b):
    return lax.dot_general(a, b, (((1,), (0,)), ((), ())), preferred_element_type=F32)


def nt(a, b):
    return lax.dot_general(a, b, (((1,), (1,)), ((), ())), preferred_element_type=F32)


def tn(a, b):
    return lax.dot_general(a, b, (((0,), (0,)), ((), ())), preferred_element_type=F32)


def lanes(*parts):
    return jnp.concatenate(parts, axis=1)


def rows(*parts):
    return jnp.concatenate(parts, axis=0)


def mean(values):
    return jnp.mean(values, axis=-1, keepdims=True)


def norm_pair(x, xd):
    center = x - mean(x)
    inverse = lax.rsqrt(mean(center * center) + EPSILON)
    h = center * inverse
    cd = xd - mean(xd)
    along = mean(h * cd)
    return h, inverse * (cd - h * along), inverse, -inverse * along


def norm_back_pair(h, hd, inverse, slope, dy, dyd):
    second = mean(dy * h)
    dx = inverse * (dy - mean(dy) - h * second)
    second_dot = mean(dyd * h + dy * hd)
    dxd = slope * dx + inverse * (dyd - mean(dyd) - hd * second - h * second_dot)
    return dx, dxd


def fetch(sources, buffers, sems):
    copies = [
        pltpu.make_async_copy(source, buffer, sems.at[i])
        for i, (source, buffer) in enumerate(zip(sources, buffers))
    ]
    for copy in copies:
        copy.start()
    return lambda *places: [copies[place].wait() for place in places]


def unpack_signs(words_ref, out_ref):
    total, width = out_ref.shape
    for start in range(0, total, 16):
        row = start + lax.broadcasted_iota(jnp.int32, (16, 1), 0)
        first = start // 30
        edge = 30 * (first + 1)
        word = jnp.broadcast_to(words_ref[first : first + 1, :], (16, width))
        shift = row - 30 * first
        if edge < start + 16:
            later = jnp.broadcast_to(words_ref[first + 1 : first + 2, :], (16, width))
            word = jnp.where(row < edge, word, later)
            shift = jnp.where(row < edge, shift, row - edge)
        bit = jnp.right_shift(word, jnp.broadcast_to(shift, (16, width))) & 1
        out_ref[start : start + 16, :] = (1 - 2 * bit).astype(F32).astype(BF16)


def fill_masks(ones_ref, mask_ref):
    head_row = lax.broadcasted_iota(jnp.int32, (256, 256), 0) // WINDOW
    head_col = lax.broadcasted_iota(jnp.int32, (256, 256), 1) // WINDOW
    ones_ref[...] = (head_row == head_col).astype(F32).astype(BF16)
    head_row = lax.broadcasted_iota(jnp.int32, (256, GROUP), 0) // WINDOW
    head_col = lax.broadcasted_iota(jnp.int32, (256, GROUP), 1) // HD
    mask_ref[...] = (head_row == head_col).astype(F32).astype(BF16)


def spread(values, mask):
    return rows(values, values, values, values) * mask


def collect(values):
    lane = lax.broadcasted_iota(jnp.int32, (WINDOW, GROUP), 1)
    parts = [values[WINDOW * i : WINDOW * (i + 1), :] for i in range(4)]
    low = jnp.where(lane < HD, parts[0], parts[1])
    high = jnp.where(lane < 3 * HD, parts[2], parts[3])
    return jnp.where(lane < 2 * HD, low, high)


BATCH = 8


def per_batch(windows, step):
    def some(i, carry):
        step(
            [
                pl.ds(pl.multiple_of((i * BATCH + n) * WINDOW, WINDOW), WINDOW)
                for n in range(BATCH)
            ]
        )
        return carry

    lax.fori_loop(0, windows // BATCH, some, 0)


def heads_of(ref, at, kind, g):
    return ref[at, pl.ds(256 * kind + GROUP * g, GROUP)]


def twice(values, dots):
    return rows(lanes(values, jnp.zeros_like(values)), lanes(dots, values))


def stacked(values, dots, weight, weight_dot):
    both = nn(rows(values, dots), lanes(weight, weight_dot))
    width = weight.shape[1]
    return both[:WINDOW, :width], both[WINDOW:, :width] + both[:WINDOW, width:]


def segment_sums(values, ones):
    total = nn(rows(*[value.astype(BF16) for value in values]), ones)
    return [total[WINDOW * i : WINDOW * (i + 1), :] for i in range(len(values))]


def attend(qkv_ref, qkvd_ref, a_ref, ad_ref, o_ref, od_ref, ones_ref, mask_ref):
    def step(spots):
        ones = ones_ref[...]
        mask = mask_ref[...]
        units = [(at, g) for at in spots for g in range(2)]
        raised, scores_dot = [], []
        for at, g in units:
            q, qd = heads_of(qkv_ref, at, 0, g), heads_of(qkvd_ref, at, 0, g)
            kb = spread(heads_of(qkv_ref, at, 1, g), mask)
            kdb = spread(heads_of(qkvd_ref, at, 1, g), mask)
            both = nt(twice(q, qd), lanes(kb, kdb)) * SCALE
            raised.append(jnp.exp(both[:WINDOW]))
            scores_dot.append(both[WINDOW:])
        weights = [e / total for e, total in zip(raised, segment_sums(raised, ones))]
        moved = [w * sd for w, sd in zip(weights, scores_dot)]
        sums = segment_sums(moved, ones)
        weights_dot = [m - w * total for m, w, total in zip(moved, weights, sums)]
        for (at, g), w, wd in zip(units, weights, weights_dot):
            a, ad = w.astype(BF16), wd.astype(BF16)
            spot = pl.ds(256 * g, 256)
            a_ref[at, spot] = a
            ad_ref[at, spot] = ad
            vb = spread(heads_of(qkv_ref, at, 2, g), mask)
            vdb = spread(heads_of(qkvd_ref, at, 2, g), mask)
            here = pl.ds(GROUP * g, GROUP)
            o, od = stacked(a, ad, vb, vdb)
            o_ref[at, here] = o.astype(BF16)
            od_ref[at, here] = od.astype(BF16)

    per_batch(qkv_ref.shape[0] // WINDOW, step)


def attend_back(
    qkv_ref, qkvd_ref, a_ref, ad_ref, do_ref, dod_ref, dqkv_ref, dqkvd_ref, ones_ref, mask_ref
):
    def step(spots):
        ones = ones_ref[...]
        mask = mask_ref[...]
        units = [(at, g) for at in spots for g in range(2)]
        da, dad, first, second = [], [], [], []
        for at, g in units:
            here = pl.ds(GROUP * g, GROUP)
            vb = spread(heads_of(qkv_ref, at, 2, g), mask)
            vdb = spread(heads_of(qkvd_ref, at, 2, g), mask)
            both = nt(twice(do_ref[at, here], dod_ref[at, here]), lanes(vb, vdb))
            da.append(both[:WINDOW])
            dad.append(both[WINDOW:])
        for (at, g), x, xd in zip(units, da, dad):
            spot = pl.ds(256 * g, 256)
            a, ad = a_ref[at, spot].astype(F32), ad_ref[at, spot].astype(F32)
            first.append(a * x)
            second.append(ad * x + a * xd)
        first, second = segment_sums(first, ones), segment_sums(second, ones)
        for (at, g), x, xd, total, total_dot in zip(units, da, dad, first, second):
            spot = pl.ds(256 * g, 256)
            here = pl.ds(GROUP * g, GROUP)
            qs, ks, vs = (pl.ds(256 * i + GROUP * g, GROUP) for i in range(3))
            ab, adb = a_ref[at, spot], ad_ref[at, spot]
            a, ad = ab.astype(F32) * SCALE, adb.astype(F32) * SCALE
            rest = x - total
            rest_dot = xd - total_dot
            ds = (a * rest).astype(BF16)
            dsd = (ad * rest + a * rest_dot).astype(BF16)
            do, dod = do_ref[at, here], dod_ref[at, here]
            q, qd = qkv_ref[at, qs], qkvd_ref[at, qs]
            kb, kdb = spread(qkv_ref[at, ks], mask), spread(qkvd_ref[at, ks], mask)
            dq, dqd = stacked(ds, dsd, kb, kdb)
            dqkvd_ref[at, qs] = dqd.astype(BF16)
            if dqkv_ref is None:
                dqkvd_ref[at, ks] = collect(tn(rows(dsd, ds), rows(q, qd))).astype(BF16)
                dqkvd_ref[at, vs] = collect(tn(rows(adb, ab), rows(do, dod))).astype(BF16)
            else:
                dqkv_ref[at, qs] = dq.astype(BF16)
                both = tn(rows(dsd, ds), twice(q, qd))
                dqkvd_ref[at, ks] = collect(both[:, :GROUP]).astype(BF16)
                dqkv_ref[at, ks] = collect(both[:, GROUP:]).astype(BF16)
                both = tn(rows(adb, ab), twice(do, dod))
                dqkvd_ref[at, vs] = collect(both[:, :GROUP]).astype(BF16)
                dqkv_ref[at, vs] = collect(both[:, GROUP:]).astype(BF16)

    per_batch(qkv_ref.shape[0] // WINDOW, step)


def block_forward_kernel(
    core_ref, pq_hbm, tok_hbm, wq_hbm, po_hbm, wo_hbm, tgt_hbm,
    pack_ref, qkv_ref, qkvd_ref, a_ref, ad_ref, h_hbm, o_hbm, od_hbm, sq_hbm, so_hbm,
    pq_ref, tok_ref, wq_ref, po_ref, wo_ref, tgt_ref, sems,
    h_ref, o_ref, od_ref, sq_ref, so_ref, out_sems, x_ref, ones_ref, mask_ref,
):
    wait = fetch(
        (pq_hbm, tok_hbm, wq_hbm, po_hbm, wo_hbm, tgt_hbm),
        (pq_ref, tok_ref, wq_ref, po_ref, wo_ref, tgt_ref),
        sems,
    )
    fill_masks(ones_ref, mask_ref)
    wait(0)
    unpack_signs(pq_ref, sq_ref)
    wait(1, 2)
    for half in range(2):
        at = pl.ds(256 * half, 256)
        slab = tok_ref[8 * half : 8 * half + 8].astype(F32)
        x = rows(*[slab[:, 8 * i : 8 * i + 8, :].reshape(WINDOW, 256) for i in range(4)])
        x_ref[at, :] = x
        center = x - mean(x)
        h = (center * lax.rsqrt(mean(center * center) + EPSILON)).astype(BF16)
        h_ref[at, :] = h
        qkv_ref[at, :] = nn(h, wq_ref[...]).astype(BF16)
        qkvd_ref[at, :] = nn(h, sq_ref[...]).astype(BF16)
    attend(qkv_ref, qkvd_ref, a_ref, ad_ref, o_ref, od_ref, ones_ref, mask_ref)
    wait(3, 4, 5)
    unpack_signs(po_ref, so_ref)
    saved = fetch(
        (h_ref, o_ref, od_ref, sq_ref, so_ref), (h_hbm, o_hbm, od_hbm, sq_hbm, so_hbm), out_sems
    )
    for half in range(2):
        at = pl.ds(256 * half, 256)
        out = pl.ds(32 * half, 32)
        o, od = o_ref[at, :], od_ref[at, :]
        x = x_ref[at, :] + nn(o, wo_ref[...])
        xd = nn(lanes(od, o), rows(wo_ref[...], so_ref[...]))
        both = jnp.concatenate([x.reshape(32, 8, 256), xd.reshape(32, 8, 256)], axis=1)
        pack_ref[out, :, 0:256] = both.astype(BF16)
        slab = tgt_ref[8 * half : 8 * half + 8].astype(F32)
        t = jnp.concatenate([slab[:, 8 * i : 8 * i + 8, :] for i in range(4)], axis=0)
        both = jnp.concatenate([t[:, :, 0:128], t[:, :, 128:256]], axis=1)
        pack_ref[out, :, 256:384] = both.astype(BF16)
    saved(0, 1, 2, 3, 4)


def middle_kernel(
    factor,
    core_ref, pack_ref, pq_ref, wq_ref, po_ref, wo_ref, pi_ref, wi_ref, pf_ref, wf_ref,
    back_ref, keep_ref, send_ref, sq_hbm, so_hbm, si_hbm, sf_hbm,
    sq_ref, so_ref, si_ref, sf_ref, out_sems, ones_ref, mask_ref, mix_ref, mixd_ref, mixt_ref,
    x_ref, xd_ref, t_ref, h1_ref, h2_ref, qkv_ref, qkvd_ref, a_ref, ad_ref, o_ref,
    ud_ref, dz_ref, dx_ref, dxd_ref, dg_ref, do_ref, dod_ref, dqkv_ref, hv_ref,
):
    tokens = x_ref.shape[0]
    fill_masks(ones_ref, mask_ref)
    arrived = pack_ref[:, :, 0:256].astype(F32)
    for c in range(2):
        mix_ref[c] = arrived[:, 0:8, 128 * c : 128 * c + 128].reshape(tokens, 128)
        mixd_ref[c] = arrived[:, 8:16, 128 * c : 128 * c + 128].reshape(tokens, 128)
    arrived = pack_ref[:, :, 256:384].astype(F32) * factor
    for c in range(2):
        mixt_ref[c] = arrived[:, 8 * c : 8 * c + 8, :].reshape(tokens, 128)
    for w in range(8):
        at = pl.ds(WINDOW * w, WINDOW)
        for c in range(2):
            cols = pl.ds(128 * c, 128)
            x_ref[at, cols] = mix_ref[c, pl.ds(w, WINDOW, stride=8), :]
            xd_ref[at, cols] = mixd_ref[c, pl.ds(w, WINDOW, stride=8), :]
            t_ref[at, cols] = mixt_ref[c, pl.ds(w, WINDOW, stride=8), :].astype(BF16)
    unpack_signs(pq_ref, sq_ref)

    def first(i):
        at = pl.ds(i * 256, 256)
        low = pl.ds(i * 256 + tokens, 256)
        h, hd, _, _ = norm_pair(x_ref[at, :], xd_ref[at, :])
        h, hd = h.astype(BF16), hd.astype(BF16)
        h1_ref[at, :] = hd
        h1_ref[low, :] = h
        qkv_ref[at, :] = nn(h, wq_ref[...]).astype(BF16)
        qkvd_ref[at, :] = nn(lanes(hd, h), rows(wq_ref[...], sq_ref[...])).astype(BF16)

    for i in range(tokens // 256):
        first(i)
    o_part, od_part = o_ref.at[pl.ds(tokens, tokens), :], o_ref.at[pl.ds(0, tokens), :]
    attend(qkv_ref, qkvd_ref, a_ref, ad_ref, o_part, od_part, ones_ref, mask_ref)
    unpack_signs(po_ref, so_ref)
    unpack_signs(pi_ref, si_ref)
    unpack_signs(pf_ref, sf_ref)
    saved = fetch(
        (sq_ref, so_ref, si_ref, sf_ref), (sq_hbm, so_hbm, si_hbm, sf_hbm), out_sems
    )

    def second(i):
        at = pl.ds(i * 512, 512)
        low = pl.ds(i * 512 + tokens, 512)
        od, o = o_ref[at, :], o_ref[low, :]
        g = nn(o, wo_ref[...]).astype(BF16).astype(F32)
        gd = nn(lanes(od, o), rows(wo_ref[...], so_ref[...])).astype(BF16).astype(F32)
        h, hd, inverse, slope = norm_pair(x_ref[at, :] + g, xd_ref[at, :] + gd)
        hb, hdb = h.astype(BF16), hd.astype(BF16)
        h2_ref[at, :] = hdb
        h2_ref[low, :] = hb
        t = t_ref[at, :]
        dh = jnp.zeros((512, 256), F32)
        dhd = jnp.zeros((512, 256), F32)
        for c in range(4):
            cols = pl.ds(256 * c, 256)
            wi, si = wi_ref[:, cols], si_ref[:, cols]
            z = nn(hb, wi)
            zd = nn(lanes(hdb, hb), rows(wi, si))
            du = nt(t, wf_ref[cols, :])
            dud = nt(t, sf_ref[cols, :])
            square = z * z
            cubic = (GELU_K * GELU_C) * square
            bend = jnp.tanh(z * (GELU_K + cubic))
            inner = GELU_K + 3.0 * cubic
            level = 1.0 - bend * bend
            slope1 = 0.5 * (1.0 + bend + (z * inner) * level)
            slope2 = level * (GELU_K + 6.0 * cubic - (z * bend) * (inner * inner))
            ud_ref[at, cols] = (slope1 * zd).astype(BF16)
            dz = (du * slope1).astype(BF16)
            dzd = (dud * slope1 + (du * zd) * slope2).astype(BF16)
            dz_ref[at, cols] = dz
            dz_ref[low, cols] = dzd
            dh = dh + nt(dz, wi)
            dhd = dhd + nt(lanes(dzd, dz), lanes(wi, si))
        dx, dxd = norm_back_pair(h, hd, inverse, slope, dh, dhd)
        dx = dx + t.astype(F32)
        dx_ref[at, :] = dx
        dxd_ref[at, :] = dxd
        dg, dgd = dx.astype(BF16), dxd.astype(BF16)
        dg_ref[at, :] = dg
        dg_ref[low, :] = dgd
        do_ref[at, :] = nt(dg, wo_ref[...]).astype(BF16)
        dod_ref[at, :] = nt(lanes(dgd, dg), lanes(wo_ref[...], so_ref[...])).astype(BF16)

    for i in range(tokens // 512):
        second(i)
    dqkv, dqkvd = dqkv_ref.at[pl.ds(0, tokens), :], dqkv_ref.at[pl.ds(tokens, tokens), :]
    attend_back(
        qkv_ref, qkvd_ref, a_ref, ad_ref, do_ref, dod_ref, dqkv, dqkvd, ones_ref, mask_ref
    )

    for i in range(tokens // 256):
        at = pl.ds(i * 256, 256)
        low = pl.ds(i * 256 + tokens, 256)
        dqkv, dqkvd = dqkv_ref[at, :], dqkv_ref[low, :]
        dh = nt(dqkv, wq_ref[...])
        dhd = nt(lanes(dqkvd, dqkv), lanes(wq_ref[...], sq_ref[...]))
        h, hd, inverse, slope = norm_pair(x_ref[at, :], xd_ref[at, :])
        dx, dxd = norm_back_pair(h, hd, inverse, slope, dh, dhd)
        dx_ref[at, :] += dx
        dxd_ref[at, :] += dxd
    for w in range(8):
        at = pl.ds(WINDOW * w, WINDOW)
        for c in range(2):
            cols = pl.ds(128 * c, 128)
            mix_ref[c, pl.ds(w, WINDOW, stride=8), :] = dx_ref[at, cols]
            mixd_ref[c, pl.ds(w, WINDOW, stride=8), :] = dxd_ref[at, cols]
    for c in range(2):
        dx = mix_ref[c].reshape(tokens // 8, 8, 128)
        dxd = mixd_ref[c].reshape(tokens // 8, 8, 128)
        both = jnp.concatenate([dx, dxd], axis=1)
        back_ref[:, :, 128 * c : 128 * c + 128] = both.astype(BF16)

    def put(block, value):
        hv_ref[block] = value.astype(BF16)

    h1 = h1_ref[...]
    for c in range(3):
        put(c, tn(h1, dqkv_ref[:, 256 * c : 256 * c + 256]))
    put(3, tn(o_ref[...], dg_ref[...]))
    h2 = h2_ref[...]
    for c in range(4):
        put(4 + c, tn(h2, dz_ref[:, 256 * c : 256 * c + 256]))
    t = t_ref[...]
    for c in range(4):
        put(8 + c, tn(ud_ref[:, 256 * c : 256 * c + 256], t))
    saved(0, 1, 2, 3)
    split_halves(core_ref, hv_ref, keep_ref, send_ref)


def split_halves(core_ref, hv_ref, keep_ref, send_ref):
    core = core_ref[0]
    mine = pl.ds(pl.multiple_of(core * 128, 128), 128)
    other = pl.ds(pl.multiple_of((1 - core) * 128, 128), 128)
    for block in range(hv_ref.shape[0]):
        keep_ref[128 * block : 128 * block + 128, :] = hv_ref[block, mine, :]
        send_ref[128 * block : 128 * block + 128, :] = hv_ref[block, other, :]


def block_back_kernel(
    core_ref, back_ref, qkv_ref, qkvd_ref, a_ref, ad_ref, wo_ref, so_ref, o_ref, od_ref, h_ref,
    keep_ref, send_ref,
    ones_ref, mask_ref, do_ref, dod_ref, dqkvd_ref, hv_ref,
):
    tokens = h_ref.shape[0]
    fill_masks(ones_ref, mask_ref)
    arrived = back_ref[...].astype(F32)
    dx = arrived[:, 0:8, :].reshape(tokens, 256).astype(BF16)
    dxd = arrived[:, 8:16, :].reshape(tokens, 256).astype(BF16)
    do_ref[...] = nt(dx, wo_ref[...]).astype(BF16)
    dod_ref[...] = nt(lanes(dxd, dx), lanes(wo_ref[...], so_ref[...])).astype(BF16)
    hv_ref[3] = tn(rows(od_ref[...], o_ref[...]), rows(dx, dxd)).astype(BF16)
    attend_back(
        qkv_ref, qkvd_ref, a_ref, ad_ref, do_ref, dod_ref, None, dqkvd_ref, ones_ref, mask_ref
    )
    h = h_ref[...]
    for c in range(3):
        hv_ref[c] = tn(h, dqkvd_ref[:, 256 * c : 256 * c + 256]).astype(BF16)
    split_halves(core_ref, hv_ref, keep_ref, send_ref)


def pair_sum_kernel(mid_keep_ref, mid_got_ref, keep_ref, got_ref, out_ref):
    count = mid_keep_ref.shape[0]
    out_ref[0:count, :] = (mid_keep_ref[...].astype(F32) + mid_got_ref[...].astype(F32)).astype(BF16)
    out_ref[count:, :] = (keep_ref[...].astype(F32) + got_ref[...].astype(F32)).astype(BF16)


def peer_sum_kernel(parts_ref, out_ref):
    total = parts_ref[0].astype(F32)
    for i in range(1, parts_ref.shape[0]):
        total = total + parts_ref[i].astype(F32)
    total = total.astype(BF16)
    for i in range(parts_ref.shape[0]):
        out_ref[i] = total


PLACES = (12, 15, 0, 3, 4, 8)


def write_half(who, half_ref, sign_refs, out_hbms, wide_refs, sems):
    copies, sums = [], {}
    for n in (4, 5, 0, 2, 1, 3):
        base, sign_ref, out_hbm, wide_ref = PLACES[n], sign_refs[n], out_hbms[n], wide_refs[n]
        height, width = out_hbm.shape
        across = width // 256
        total = jnp.zeros((8, 256), F32)
        for block in range(height * width // 65536):
            cols = pl.ds(256 * (block % across), 256)
            down = block // across
            at = pl.ds(pl.multiple_of(256 * down + who * 128, 128), 128)
            value = half_ref[128 * (base + block) : 128 * (base + block) + 128, :].astype(F32)
            wide_ref[128 * down : 128 * down + 128, cols] = value
            signed = value * sign_ref[at, cols].astype(F32)
            total = total + jnp.sum(signed.reshape(16, 8, 256), axis=0)
        for down in range(height // 256):
            at = pl.ds(pl.multiple_of(256 * down + who * 128, 128), 128)
            copies.append(
                pltpu.make_async_copy(
                    wide_ref.at[pl.ds(128 * down, 128), :], out_hbm.at[at, :], sems.at[len(copies)]
                )
            )
            copies[-1].start()
        sums[n] = jnp.sum(total, axis=0, keepdims=True)
    for copy in copies:
        copy.wait()
    return rows(*[sums[n] for n in range(6)], jnp.zeros((2, 256), F32))


def finish_mine_kernel(core_ref, half_ref, *refs):
    signs, outs, sum_ref, wides, sems = refs[:6], refs[6:12], refs[12], refs[13:19], refs[19]
    sum_ref[...] = write_half(core_ref[0], half_ref, signs, outs, wides, sems)


def finish_other_kernel(core_ref, half_ref, sum_ref, *refs):
    signs, outs, trace_ref, wides, sems = refs[:6], refs[12:18], refs[18], refs[19:25], refs[25]
    sums = sum_ref[...] + write_half(1 - core_ref[0], half_ref, signs, outs, wides, sems)
    for n, out in enumerate(outs):
        trace_ref[n] = jnp.sum(sums[n : n + 1, :]) / math.sqrt(out.shape[0] * out.shape[1])


def shaped(dtype, *shape):
    return jax.ShapeDtypeStruct(shape, dtype)


def held(*arrays):
    buffers = [pltpu.VMEM(array.shape, array.dtype) for array in arrays]
    return buffers + [pltpu.SemaphoreType.DMA((len(arrays),))]


def call(kernel, outs, spaces, scratch, operands, places, name, limit, aliases=None):
    kinds = {"s": pltpu.SMEM, "v": pltpu.VMEM, "h": pltpu.HBM}
    pinned = [
        pltpu.with_memory_space_constraint(operand, pltpu.HBM) if place == "h" else operand
        for operand, place in zip(operands, places)
    ]
    return pl.pallas_call(
        kernel,
        out_shape=[
            pltpu.HBM(out.shape, out.dtype) if space == "h" else out
            for out, space in zip(outs, spaces)
        ],
        in_specs=[pl.BlockSpec(memory_space=kinds[place]) for place in places],
        out_specs=[pl.BlockSpec(memory_space=kinds[space]) for space in spaces],
        scratch_shapes=scratch,
        input_output_aliases=aliases or {},
        compiler_params=pltpu.CompilerParams(vmem_limit_bytes=limit * 2**20),
        name=name,
    )(*pinned)


MASKS = [pltpu.VMEM((256, 256), BF16), pltpu.VMEM((256, GROUP), BF16)]


def stage_forward(core, tokens, target, weight_qkv, weight_out, words_qkv, words_out, peers):
    count = tokens.shape[0] * tokens.shape[1]
    sources = (words_qkv, tokens, weight_qkv, words_out, weight_out, target)
    late = [
        shaped(BF16, count, 256),
        shaped(BF16, count, 256),
        shaped(BF16, count, 256),
        shaped(BF16, 256, 768),
        shaped(BF16, 256, 256),
    ]
    return call(
        block_forward_kernel,
        [
            shaped(BF16, peers, 16, 384),
            shaped(BF16, count, 768),
            shaped(BF16, count, 768),
            shaped(BF16, count, 512),
            shaped(BF16, count, 512),
        ]
        + late,
        "v" * 5 + "h" * 5,
        held(*sources) + held(*late) + [pltpu.VMEM((count, 256), F32)] + MASKS,
        (core, *sources),
        "shhhhhh",
        "block_forward",
        24,
    )


def stage_middle(core, pack, factor, sources):
    peers = pack.shape[0]
    count = peers * 8
    signs = [shaped(BF16, *weight.shape) for weight in sources[1::2]]
    return call(
        functools.partial(middle_kernel, factor),
        [shaped(BF16, peers, 16, 256), shaped(BF16, 1536, 256), shaped(BF16, 1536, 256)] + signs,
        "vvvhhhh",
        held(*signs)
        + MASKS
        + [pltpu.VMEM((2, count, 128), F32)] * 3
        + [pltpu.VMEM((count, 256), F32)] * 2
        + [
            pltpu.VMEM((count, 256), BF16),
            pltpu.VMEM((2 * count, 256), BF16),
            pltpu.VMEM((2 * count, 256), BF16),
            pltpu.VMEM((count, 768), BF16),
            pltpu.VMEM((count, 768), BF16),
            pltpu.VMEM((count, 512), BF16),
            pltpu.VMEM((count, 512), BF16),
            pltpu.VMEM((2 * count, 256), BF16),
            pltpu.VMEM((count, 1024), BF16),
            pltpu.VMEM((2 * count, 1024), BF16),
            pltpu.VMEM((count, 256), F32),
            pltpu.VMEM((count, 256), F32),
            pltpu.VMEM((2 * count, 256), BF16),
            pltpu.VMEM((count, 256), BF16),
            pltpu.VMEM((count, 256), BF16),
            pltpu.VMEM((2 * count, 768), BF16),
            pltpu.VMEM((12, 256, 256), BF16),
        ],
        (core, pack, *sources),
        "s" + "v" * 9,
        "middle",
        40,
    )


def stage_back(core, back, saved, weight_out):
    qkv, qkvd, a, ad, h, o, od, _, so = saved
    count = qkv.shape[0]
    late = (weight_out, so, o, od, h)
    return call(
        block_back_kernel,
        [shaped(BF16, 512, 256), shaped(BF16, 512, 256)],
        "vv",
        MASKS
        + [
            pltpu.VMEM((count, 256), BF16),
            pltpu.VMEM((count, 256), BF16),
            pltpu.VMEM((count, 768), BF16),
            pltpu.VMEM((4, 256, 256), BF16),
        ],
        (core, back, qkv, qkvd, a, ad, *late),
        "s" + "v" * 10,
        "block_back",
        20,
    )


def body(
    tokens, target, block_qkv, block_out, grid_qkv, grid_out, mlp_in, mlp_out,
    probe_block_qkv, probe_block_out, probe_grid_qkv, probe_grid_out, probe_mlp_in, probe_mlp_out,
):
    peers = lax.axis_size(PEERS)
    count = tokens.shape[0] * tokens.shape[1]
    factor = 1.0 / math.sqrt(count * peers * lax.axis_size("core"))
    core = lax.axis_index("core").astype(jnp.int32).reshape(1)
    swap = [(0, 1), (1, 0)]

    def exchange(values):
        return lax.all_to_all(values, PEERS, 0, 0, tiled=True)

    pack, *saved = stage_forward(
        core, tokens, target, block_qkv, block_out, probe_block_qkv, probe_block_out, peers
    )
    sources = (
        probe_grid_qkv, grid_qkv, probe_grid_out, grid_out,
        probe_mlp_in, mlp_in, probe_mlp_out, mlp_out,
    )
    back, mid_keep, mid_send, *signs = stage_middle(core, exchange(pack), factor, sources)
    mid_got = lax.ppermute(mid_send, "core", swap)
    keep, send = stage_back(core, exchange(back), saved, block_out)
    got = lax.ppermute(send, "core", swap)
    (parts,) = call(
        pair_sum_kernel,
        [shaped(BF16, 2048, 256)],
        "v",
        [],
        (mid_keep, mid_got, keep, got),
        "vvvv",
        "pair_sum",
        8,
    )
    parts = exchange(parts.reshape(peers, 2048 // peers, 256))
    (copies,) = call(
        peer_sum_kernel,
        [shaped(BF16, peers, 2048 // peers, 256)],
        "v",
        [],
        (parts,),
        "v",
        "peer_sum",
        8,
    )
    mine = exchange(copies).reshape(2048, 256)
    other = lax.ppermute(mine, "core", swap)
    weights = (block_qkv, block_out, grid_qkv, grid_out, mlp_in, mlp_out)
    signs = (*saved[7:9], *signs)
    outs = [shaped(F32, *weight.shape) for weight in weights]
    wides = [pltpu.VMEM((out.shape[0] // 2, out.shape[1]), F32) for out in outs]
    wides.append(pltpu.SemaphoreType.DMA((9,)))
    *halves, sums = call(
        finish_mine_kernel,
        outs + [shaped(F32, 8, 256)],
        "hhhhhhv",
        wides,
        (core, mine, *signs),
        "s" + "v" * 7,
        "finish_mine",
        16,
    )
    return call(
        finish_other_kernel,
        outs + [shaped(F32, 6)],
        "hhhhhhs",
        wides,
        (core, other, sums, *signs, *halves),
        "s" + "v" * 8 + "h" * 6,
        "finish_other",
        16,
        {9 + n: n for n in range(6)},
    )


def solution(mesh):
    fine = Mesh(mesh.devices.reshape(2, 4, 4, 2, 2), ("y_lo", "x", "z", "y_hi", "core"))
    placed = P(("y_lo", "x"), ("z", "y_hi", "core"), None)
    return jax.shard_map(
        body,
        mesh=fine,
        in_specs=(placed, placed) + (P(),) * 12,
        out_specs=(P(),) * 7,
        check_vma=False,
    )
```

```python
import functools
import math

import jax
import jax.numpy as jnp
from jax import lax
from jax.experimental import pallas as pl
from jax.experimental.pallas import tpu as pltpu
from jax.sharding import Mesh, PartitionSpec as P

F32 = jnp.float32
BF16 = jnp.bfloat16
HD = 32
WINDOW = 64
GROUP = 128
EPSILON = 1e-05
SCALE = HD ** (-0.5)
GELU_K = math.sqrt(2.0 / math.pi)
GELU_C = 0.044715
PEERS = ("x", "z", "y_hi", "y_lo")


def nn(a, b):
    return lax.dot_general(a, b, (((1,), (0,)), ((), ())), preferred_element_type=F32)


def nt(a, b):
    return lax.dot_general(a, b, (((1,), (1,)), ((), ())), preferred_element_type=F32)


def tn(a, b):
    return lax.dot_general(a, b, (((0,), (0,)), ((), ())), preferred_element_type=F32)


def lanes(*parts):
    return jnp.concatenate(parts, axis=1)


def rows(*parts):
    return jnp.concatenate(parts, axis=0)


def mean(values):
    return jnp.mean(values, axis=-1, keepdims=True)


def norm_pair(x, xd):
    center = x - mean(x)
    inverse = lax.rsqrt(mean(center * center) + EPSILON)
    h = center * inverse
    cd = xd - mean(xd)
    along = mean(h * cd)
    return h, inverse * (cd - h * along), inverse, -inverse * along


def norm_back_pair(h, hd, inverse, slope, dy, dyd):
    second = mean(dy * h)
    dx = inverse * (dy - mean(dy) - h * second)
    second_dot = mean(dyd * h + dy * hd)
    dxd = slope * dx + inverse * (dyd - mean(dyd) - hd * second - h * second_dot)
    return dx, dxd


def fetch(sources, buffers, sems):
    copies = [
        pltpu.make_async_copy(source, buffer, sems.at[i])
        for i, (source, buffer) in enumerate(zip(sources, buffers))
    ]
    for copy in copies:
        copy.start()
    return lambda *places: [copies[place].wait() for place in places]


def unpack_signs(words_ref, out_ref):
    total, width = out_ref.shape
    for start in range(0, total, 16):
        row = start + lax.broadcasted_iota(jnp.int32, (16, 1), 0)
        first = start // 30
        edge = 30 * (first + 1)
        word = jnp.broadcast_to(words_ref[first : first + 1, :], (16, width))
        shift = row - 30 * first
        if edge < start + 16:
            later = jnp.broadcast_to(words_ref[first + 1 : first + 2, :], (16, width))
            word = jnp.where(row < edge, word, later)
            shift = jnp.where(row < edge, shift, row - edge)
        bit = jnp.right_shift(word, jnp.broadcast_to(shift, (16, width))) & 1
        out_ref[start : start + 16, :] = (1 - 2 * bit).astype(F32).astype(BF16)


def fill_masks(ones_ref, mask_ref):
    head_row = lax.broadcasted_iota(jnp.int32, (256, 256), 0) // WINDOW
    head_col = lax.broadcasted_iota(jnp.int32, (256, 256), 1) // WINDOW
    ones_ref[...] = (head_row == head_col).astype(F32).astype(BF16)
    head_row = lax.broadcasted_iota(jnp.int32, (256, GROUP), 0) // WINDOW
    head_col = lax.broadcasted_iota(jnp.int32, (256, GROUP), 1) // HD
    mask_ref[...] = (head_row == head_col).astype(F32).astype(BF16)


def spread(values, mask):
    return rows(values, values, values, values) * mask


def collect(values):
    lane = lax.broadcasted_iota(jnp.int32, (WINDOW, GROUP), 1)
    parts = [values[WINDOW * i : WINDOW * (i + 1), :] for i in range(4)]
    low = jnp.where(lane < HD, parts[0], parts[1])
    high = jnp.where(lane < 3 * HD, parts[2], parts[3])
    return jnp.where(lane < 2 * HD, low, high)


BATCH = 8


def per_batch(windows, step):
    def some(i, carry):
        step(
            [
                pl.ds(pl.multiple_of((i * BATCH + n) * WINDOW, WINDOW), WINDOW)
                for n in range(BATCH)
            ]
        )
        return carry

    lax.fori_loop(0, windows // BATCH, some, 0)


def heads_of(ref, at, kind, g):
    return ref[at, pl.ds(256 * kind + GROUP * g, GROUP)]


def twice(values, dots):
    return rows(lanes(values, jnp.zeros_like(values)), lanes(dots, values))


def stacked(values, dots, weight, weight_dot):
    both = nn(rows(values, dots), lanes(weight, weight_dot))
    width = weight.shape[1]
    return both[:WINDOW, :width], both[WINDOW:, :width] + both[:WINDOW, width:]


def segment_sums(values, ones):
    total = nn(rows(*[value.astype(BF16) for value in values]), ones)
    return [total[WINDOW * i : WINDOW * (i + 1), :] for i in range(len(values))]


def attend(qkv_ref, qkvd_ref, a_ref, ad_ref, o_ref, od_ref, ones_ref, mask_ref):
    def step(spots):
        ones = ones_ref[...]
        mask = mask_ref[...]
        units = [(at, g) for at in spots for g in range(2)]
        raised, scores_dot = [], []
        for at, g in units:
            q, qd = heads_of(qkv_ref, at, 0, g), heads_of(qkvd_ref, at, 0, g)
            kb = spread(heads_of(qkv_ref, at, 1, g), mask)
            kdb = spread(heads_of(qkvd_ref, at, 1, g), mask)
            both = nt(twice(q, qd), lanes(kb, kdb)) * SCALE
            raised.append(jnp.exp(both[:WINDOW]))
            scores_dot.append(both[WINDOW:])
        weights = [e / total for e, total in zip(raised, segment_sums(raised, ones))]
        moved = [w * sd for w, sd in zip(weights, scores_dot)]
        sums = segment_sums(moved, ones)
        weights_dot = [m - w * total for m, w, total in zip(moved, weights, sums)]
        for (at, g), w, wd in zip(units, weights, weights_dot):
            a, ad = w.astype(BF16), wd.astype(BF16)
            spot = pl.ds(256 * g, 256)
            a_ref[at, spot] = a
            ad_ref[at, spot] = ad
            vb = spread(heads_of(qkv_ref, at, 2, g), mask)
            vdb = spread(heads_of(qkvd_ref, at, 2, g), mask)
            here = pl.ds(GROUP * g, GROUP)
            o, od = stacked(a, ad, vb, vdb)
            o_ref[at, here] = o.astype(BF16)
            od_ref[at, here] = od.astype(BF16)

    per_batch(qkv_ref.shape[0] // WINDOW, step)


def attend_back(
    qkv_ref, qkvd_ref, a_ref, ad_ref, do_ref, dod_ref, dqkv_ref, dqkvd_ref, ones_ref, mask_ref
):
    def step(spots):
        ones = ones_ref[...]
        mask = mask_ref[...]
        units = [(at, g) for at in spots for g in range(2)]
        da, dad, first, second = [], [], [], []
        for at, g in units:
            here = pl.ds(GROUP * g, GROUP)
            vb = spread(heads_of(qkv_ref, at, 2, g), mask)
            vdb = spread(heads_of(qkvd_ref, at, 2, g), mask)
            both = nt(twice(do_ref[at, here], dod_ref[at, here]), lanes(vb, vdb))
            da.append(both[:WINDOW])
            dad.append(both[WINDOW:])
        for (at, g), x, xd in zip(units, da, dad):
            spot = pl.ds(256 * g, 256)
            a, ad = a_ref[at, spot].astype(F32), ad_ref[at, spot].astype(F32)
            first.append(a * x)
            second.append(ad * x + a * xd)
        first, second = segment_sums(first, ones), segment_sums(second, ones)
        for (at, g), x, xd, total, total_dot in zip(units, da, dad, first, second):
            spot = pl.ds(256 * g, 256)
            here = pl.ds(GROUP * g, GROUP)
            qs, ks, vs = (pl.ds(256 * i + GROUP * g, GROUP) for i in range(3))
            ab, adb = a_ref[at, spot], ad_ref[at, spot]
            a, ad = ab.astype(F32) * SCALE, adb.astype(F32) * SCALE
            rest = x - total
            rest_dot = xd - total_dot
            ds = (a * rest).astype(BF16)
            dsd = (ad * rest + a * rest_dot).astype(BF16)
            do, dod = do_ref[at, here], dod_ref[at, here]
            q, qd = qkv_ref[at, qs], qkvd_ref[at, qs]
            kb, kdb = spread(qkv_ref[at, ks], mask), spread(qkvd_ref[at, ks], mask)
            dq, dqd = stacked(ds, dsd, kb, kdb)
            dqkvd_ref[at, qs] = dqd.astype(BF16)
            if dqkv_ref is None:
                dqkvd_ref[at, ks] = collect(tn(rows(dsd, ds), rows(q, qd))).astype(BF16)
                dqkvd_ref[at, vs] = collect(tn(rows(adb, ab), rows(do, dod))).astype(BF16)
            else:
                dqkv_ref[at, qs] = dq.astype(BF16)
                both = tn(rows(dsd, ds), twice(q, qd))
                dqkvd_ref[at, ks] = collect(both[:, :GROUP]).astype(BF16)
                dqkv_ref[at, ks] = collect(both[:, GROUP:]).astype(BF16)
                both = tn(rows(adb, ab), twice(do, dod))
                dqkvd_ref[at, vs] = collect(both[:, :GROUP]).astype(BF16)
                dqkv_ref[at, vs] = collect(both[:, GROUP:]).astype(BF16)

    per_batch(qkv_ref.shape[0] // WINDOW, step)


def block_forward_kernel(
    core_ref, pq_hbm, tok_hbm, wq_hbm, po_hbm, wo_hbm, tgt_hbm,
    pack_ref, qkv_ref, qkvd_ref, a_ref, ad_ref, h_hbm, o_hbm, od_hbm, sq_hbm, so_hbm,
    pq_ref, tok_ref, wq_ref, po_ref, wo_ref, tgt_ref, sems,
    h_ref, o_ref, od_ref, sq_ref, so_ref, out_sems, x_ref, ones_ref, mask_ref,
):
    wait = fetch(
        (pq_hbm, tok_hbm, wq_hbm, po_hbm, wo_hbm, tgt_hbm),
        (pq_ref, tok_ref, wq_ref, po_ref, wo_ref, tgt_ref),
        sems,
    )
    fill_masks(ones_ref, mask_ref)
    wait(0)
    unpack_signs(pq_ref, sq_ref)
    wait(1, 2)
    for half in range(2):
        at = pl.ds(256 * half, 256)
        slab = tok_ref[8 * half : 8 * half + 8].astype(F32)
        x = rows(*[slab[:, 8 * i : 8 * i + 8, :].reshape(WINDOW, 256) for i in range(4)])
        x_ref[at, :] = x
        center = x - mean(x)
        h = (center * lax.rsqrt(mean(center * center) + EPSILON)).astype(BF16)
        h_ref[at, :] = h
        qkv_ref[at, :] = nn(h, wq_ref[...]).astype(BF16)
        qkvd_ref[at, :] = nn(h, sq_ref[...]).astype(BF16)
    attend(qkv_ref, qkvd_ref, a_ref, ad_ref, o_ref, od_ref, ones_ref, mask_ref)
    wait(3, 4, 5)
    unpack_signs(po_ref, so_ref)
    saved = fetch(
        (h_ref, o_ref, od_ref, sq_ref, so_ref), (h_hbm, o_hbm, od_hbm, sq_hbm, so_hbm), out_sems
    )
    for half in range(2):
        at = pl.ds(256 * half, 256)
        out = pl.ds(32 * half, 32)
        o, od = o_ref[at, :], od_ref[at, :]
        x = x_ref[at, :] + nn(o, wo_ref[...])
        xd = nn(lanes(od, o), rows(wo_ref[...], so_ref[...]))
        both = jnp.concatenate([x.reshape(32, 8, 256), xd.reshape(32, 8, 256)], axis=1)
        pack_ref[out, :, 0:256] = both.astype(BF16)
        slab = tgt_ref[8 * half : 8 * half + 8].astype(F32)
        t = jnp.concatenate([slab[:, 8 * i : 8 * i + 8, :] for i in range(4)], axis=0)
        both = jnp.concatenate([t[:, :, 0:128], t[:, :, 128:256]], axis=1)
        pack_ref[out, :, 256:384] = both.astype(BF16)
    saved(0, 1, 2, 3, 4)


def middle_kernel(
    factor,
    core_ref, pack_ref, pq_ref, wq_ref, po_ref, wo_ref, pi_ref, wi_ref, pf_ref, wf_ref,
    back_ref, keep_ref, send_ref, sq_hbm, so_hbm, si_hbm, sf_hbm,
    sq_ref, so_ref, si_ref, sf_ref, out_sems, ones_ref, mask_ref, mix_ref, mixd_ref, mixt_ref,
    x_ref, xd_ref, t_ref, h1_ref, h2_ref, qkv_ref, qkvd_ref, a_ref, ad_ref, o_ref,
    ud_ref, dz_ref, dx_ref, dxd_ref, dg_ref, do_ref, dod_ref, dqkv_ref, hv_ref,
):
    tokens = x_ref.shape[0]
    fill_masks(ones_ref, mask_ref)
    arrived = pack_ref[:, :, 0:256].astype(F32)
    for c in range(2):
        mix_ref[c] = arrived[:, 0:8, 128 * c : 128 * c + 128].reshape(tokens, 128)
        mixd_ref[c] = arrived[:, 8:16, 128 * c : 128 * c + 128].reshape(tokens, 128)
    arrived = pack_ref[:, :, 256:384].astype(F32) * factor
    for c in range(2):
        mixt_ref[c] = arrived[:, 8 * c : 8 * c + 8, :].reshape(tokens, 128)
    for w in range(8):
        at = pl.ds(WINDOW * w, WINDOW)
        for c in range(2):
            cols = pl.ds(128 * c, 128)
            x_ref[at, cols] = mix_ref[c, pl.ds(w, WINDOW, stride=8), :]
            xd_ref[at, cols] = mixd_ref[c, pl.ds(w, WINDOW, stride=8), :]
            t_ref[at, cols] = mixt_ref[c, pl.ds(w, WINDOW, stride=8), :].astype(BF16)
    unpack_signs(pq_ref, sq_ref)

    def first(i):
        at = pl.ds(i * 256, 256)
        low = pl.ds(i * 256 + tokens, 256)
        h, hd, _, _ = norm_pair(x_ref[at, :], xd_ref[at, :])
        h, hd = h.astype(BF16), hd.astype(BF16)
        h1_ref[at, :] = hd
        h1_ref[low, :] = h
        qkv_ref[at, :] = nn(h, wq_ref[...]).astype(BF16)
        qkvd_ref[at, :] = nn(lanes(hd, h), rows(wq_ref[...], sq_ref[...])).astype(BF16)

    for i in range(tokens // 256):
        first(i)
    o_part, od_part = o_ref.at[pl.ds(tokens, tokens), :], o_ref.at[pl.ds(0, tokens), :]
    attend(qkv_ref, qkvd_ref, a_ref, ad_ref, o_part, od_part, ones_ref, mask_ref)
    unpack_signs(po_ref, so_ref)
    unpack_signs(pi_ref, si_ref)
    unpack_signs(pf_ref, sf_ref)
    saved = fetch(
        (sq_ref, so_ref, si_ref, sf_ref), (sq_hbm, so_hbm, si_hbm, sf_hbm), out_sems
    )

    def second(i):
        at = pl.ds(i * 512, 512)
        low = pl.ds(i * 512 + tokens, 512)
        od, o = o_ref[at, :], o_ref[low, :]
        g = nn(o, wo_ref[...]).astype(BF16).astype(F32)
        gd = nn(lanes(od, o), rows(wo_ref[...], so_ref[...])).astype(BF16).astype(F32)
        h, hd, inverse, slope = norm_pair(x_ref[at, :] + g, xd_ref[at, :] + gd)
        hb, hdb = h.astype(BF16), hd.astype(BF16)
        h2_ref[at, :] = hdb
        h2_ref[low, :] = hb
        t = t_ref[at, :]
        dh = jnp.zeros((512, 256), F32)
        dhd = jnp.zeros((512, 256), F32)
        for c in range(4):
            cols = pl.ds(256 * c, 256)
            wi, si = wi_ref[:, cols], si_ref[:, cols]
            z = nn(hb, wi)
            zd = nn(lanes(hdb, hb), rows(wi, si))
            du = nt(t, wf_ref[cols, :])
            dud = nt(t, sf_ref[cols, :])
            square = z * z
            cubic = (GELU_K * GELU_C) * square
            bend = jnp.tanh(z * (GELU_K + cubic))
            inner = GELU_K + 3.0 * cubic
            level = 1.0 - bend * bend
            slope1 = 0.5 * (1.0 + bend + (z * inner) * level)
            slope2 = level * (GELU_K + 6.0 * cubic - (z * bend) * (inner * inner))
            ud_ref[at, cols] = (slope1 * zd).astype(BF16)
            dz = (du * slope1).astype(BF16)
            dzd = (dud * slope1 + (du * zd) * slope2).astype(BF16)
            dz_ref[at, cols] = dz
            dz_ref[low, cols] = dzd
            dh = dh + nt(dz, wi)
            dhd = dhd + nt(lanes(dzd, dz), lanes(wi, si))
        dx, dxd = norm_back_pair(h, hd, inverse, slope, dh, dhd)
        dx = dx + t.astype(F32)
        dx_ref[at, :] = dx
        dxd_ref[at, :] = dxd
        dg, dgd = dx.astype(BF16), dxd.astype(BF16)
        dg_ref[at, :] = dg
        dg_ref[low, :] = dgd
        do_ref[at, :] = nt(dg, wo_ref[...]).astype(BF16)
        dod_ref[at, :] = nt(lanes(dgd, dg), lanes(wo_ref[...], so_ref[...])).astype(BF16)

    for i in range(tokens // 512):
        second(i)
    dqkv, dqkvd = dqkv_ref.at[pl.ds(0, tokens), :], dqkv_ref.at[pl.ds(tokens, tokens), :]
    attend_back(
        qkv_ref, qkvd_ref, a_ref, ad_ref, do_ref, dod_ref, dqkv, dqkvd, ones_ref, mask_ref
    )

    for i in range(tokens // 256):
        at = pl.ds(i * 256, 256)
        low = pl.ds(i * 256 + tokens, 256)
        dqkv, dqkvd = dqkv_ref[at, :], dqkv_ref[low, :]
        dh = nt(dqkv, wq_ref[...])
        dhd = nt(lanes(dqkvd, dqkv), lanes(wq_ref[...], sq_ref[...]))
        h, hd, inverse, slope = norm_pair(x_ref[at, :], xd_ref[at, :])
        dx, dxd = norm_back_pair(h, hd, inverse, slope, dh, dhd)
        dx_ref[at, :] += dx
        dxd_ref[at, :] += dxd
    for w in range(8):
        at = pl.ds(WINDOW * w, WINDOW)
        for c in range(2):
            cols = pl.ds(128 * c, 128)
            mix_ref[c, pl.ds(w, WINDOW, stride=8), :] = dx_ref[at, cols]
            mixd_ref[c, pl.ds(w, WINDOW, stride=8), :] = dxd_ref[at, cols]
    for c in range(2):
        dx = mix_ref[c].reshape(tokens // 8, 8, 128)
        dxd = mixd_ref[c].reshape(tokens // 8, 8, 128)
        both = jnp.concatenate([dx, dxd], axis=1)
        back_ref[:, :, 128 * c : 128 * c + 128] = both.astype(BF16)

    def put(block, value):
        hv_ref[block] = value.astype(BF16)

    h1 = h1_ref[...]
    for c in range(3):
        put(c, tn(h1, dqkv_ref[:, 256 * c : 256 * c + 256]))
    put(3, tn(o_ref[...], dg_ref[...]))
    h2 = h2_ref[...]
    for c in range(4):
        put(4 + c, tn(h2, dz_ref[:, 256 * c : 256 * c + 256]))
    t = t_ref[...]
    for c in range(4):
        put(8 + c, tn(ud_ref[:, 256 * c : 256 * c + 256], t))
    saved(0, 1, 2, 3)
    split_halves(core_ref, hv_ref, keep_ref, send_ref)


def split_halves(core_ref, hv_ref, keep_ref, send_ref):
    core = core_ref[0]
    mine = pl.ds(pl.multiple_of(core * 128, 128), 128)
    other = pl.ds(pl.multiple_of((1 - core) * 128, 128), 128)
    for block in range(hv_ref.shape[0]):
        keep_ref[128 * block : 128 * block + 128, :] = hv_ref[block, mine, :]
        send_ref[128 * block : 128 * block + 128, :] = hv_ref[block, other, :]


def block_back_kernel(
    core_ref, back_ref, qkv_ref, qkvd_ref, a_ref, ad_ref, wo_ref, so_ref, o_ref, od_ref, h_ref,
    keep_ref, send_ref,
    ones_ref, mask_ref, do_ref, dod_ref, dqkvd_ref, hv_ref,
):
    tokens = h_ref.shape[0]
    fill_masks(ones_ref, mask_ref)
    arrived = back_ref[...].astype(F32)
    dx = arrived[:, 0:8, :].reshape(tokens, 256).astype(BF16)
    dxd = arrived[:, 8:16, :].reshape(tokens, 256).astype(BF16)
    do_ref[...] = nt(dx, wo_ref[...]).astype(BF16)
    dod_ref[...] = nt(lanes(dxd, dx), lanes(wo_ref[...], so_ref[...])).astype(BF16)
    hv_ref[3] = tn(rows(od_ref[...], o_ref[...]), rows(dx, dxd)).astype(BF16)
    attend_back(
        qkv_ref, qkvd_ref, a_ref, ad_ref, do_ref, dod_ref, None, dqkvd_ref, ones_ref, mask_ref
    )
    h = h_ref[...]
    for c in range(3):
        hv_ref[c] = tn(h, dqkvd_ref[:, 256 * c : 256 * c + 256]).astype(BF16)
    split_halves(core_ref, hv_ref, keep_ref, send_ref)


def pair_sum_kernel(mid_keep_ref, mid_got_ref, keep_ref, got_ref, out_ref):
    peers, height, _ = out_ref.shape

    def put(first, keep, got):
        total = (keep.astype(F32) + got.astype(F32)).astype(BF16)
        side, place = first // 1024, first % 1024 // height
        count = total.shape[0] // height
        out_ref[place : place + count, :, 256 * side : 256 * side + 256] = total.reshape(
            count, height, 256
        )

    put(0, mid_keep_ref[0:1024, :], mid_got_ref[0:1024, :])
    put(1024, mid_keep_ref[1024:1536, :], mid_got_ref[1024:1536, :])
    put(1536, keep_ref[...], got_ref[...])


def peer_sum_kernel(parts_ref, out_ref):
    total = parts_ref[0].astype(F32)
    for i in range(1, parts_ref.shape[0]):
        total = total + parts_ref[i].astype(F32)
    total = total.astype(BF16)
    for i in range(parts_ref.shape[0]):
        out_ref[i] = total


PLACES = (12, 15, 0, 3, 4, 8)


def write_half(who, half_ref, sign_refs, out_hbms, wide_refs, sems):
    copies, sums = [], {}
    for n in (4, 5, 0, 2, 1, 3):
        base, sign_ref, out_hbm, wide_ref = PLACES[n], sign_refs[n], out_hbms[n], wide_refs[n]
        height, width = out_hbm.shape
        across = width // 256
        total = jnp.zeros((8, 256), F32)
        for block in range(height * width // 65536):
            cols = pl.ds(256 * (block % across), 256)
            down = block // across
            at = pl.ds(pl.multiple_of(256 * down + who * 128, 128), 128)
            spot = pl.ds(128 * ((base + block) % 8), 128)
            side = pl.ds(256 * ((base + block) // 8), 256)
            value = half_ref[spot, side].astype(F32)
            wide_ref[128 * down : 128 * down + 128, cols] = value
            signed = value * sign_ref[at, cols].astype(F32)
            total = total + jnp.sum(signed.reshape(16, 8, 256), axis=0)
        for down in range(height // 256):
            at = pl.ds(pl.multiple_of(256 * down + who * 128, 128), 128)
            copies.append(
                pltpu.make_async_copy(
                    wide_ref.at[pl.ds(128 * down, 128), :], out_hbm.at[at, :], sems.at[len(copies)]
                )
            )
            copies[-1].start()
        sums[n] = jnp.sum(total, axis=0, keepdims=True)
    for copy in copies:
        copy.wait()
    return rows(*[sums[n] for n in range(6)], jnp.zeros((2, 256), F32))


def finish_mine_kernel(core_ref, half_ref, *refs):
    signs, outs, sum_ref, wides, sems = refs[:6], refs[6:12], refs[12], refs[13:19], refs[19]
    sum_ref[...] = write_half(core_ref[0], half_ref, signs, outs, wides, sems)


def finish_other_kernel(core_ref, half_ref, sum_ref, *refs):
    signs, outs, trace_ref, wides, sems = refs[:6], refs[12:18], refs[18], refs[19:25], refs[25]
    sums = sum_ref[...] + write_half(1 - core_ref[0], half_ref, signs, outs, wides, sems)
    for n, out in enumerate(outs):
        trace_ref[n] = jnp.sum(sums[n : n + 1, :]) / math.sqrt(out.shape[0] * out.shape[1])


def shaped(dtype, *shape):
    return jax.ShapeDtypeStruct(shape, dtype)


def held(*arrays):
    buffers = [pltpu.VMEM(array.shape, array.dtype) for array in arrays]
    return buffers + [pltpu.SemaphoreType.DMA((len(arrays),))]


def call(kernel, outs, spaces, scratch, operands, places, name, limit, aliases=None):
    kinds = {"s": pltpu.SMEM, "v": pltpu.VMEM, "h": pltpu.HBM}
    pinned = [
        pltpu.with_memory_space_constraint(operand, pltpu.HBM) if place == "h" else operand
        for operand, place in zip(operands, places)
    ]
    return pl.pallas_call(
        kernel,
        out_shape=[
            pltpu.HBM(out.shape, out.dtype) if space == "h" else out
            for out, space in zip(outs, spaces)
        ],
        in_specs=[pl.BlockSpec(memory_space=kinds[place]) for place in places],
        out_specs=[pl.BlockSpec(memory_space=kinds[space]) for space in spaces],
        scratch_shapes=scratch,
        input_output_aliases=aliases or {},
        compiler_params=pltpu.CompilerParams(vmem_limit_bytes=limit * 2**20),
        name=name,
    )(*pinned)


MASKS = [pltpu.VMEM((256, 256), BF16), pltpu.VMEM((256, GROUP), BF16)]


def stage_forward(core, tokens, target, weight_qkv, weight_out, words_qkv, words_out, peers):
    count = tokens.shape[0] * tokens.shape[1]
    sources = (words_qkv, tokens, weight_qkv, words_out, weight_out, target)
    late = [
        shaped(BF16, count, 256),
        shaped(BF16, count, 256),
        shaped(BF16, count, 256),
        shaped(BF16, 256, 768),
        shaped(BF16, 256, 256),
    ]
    return call(
        block_forward_kernel,
        [
            shaped(BF16, peers, 16, 384),
            shaped(BF16, count, 768),
            shaped(BF16, count, 768),
            shaped(BF16, count, 512),
            shaped(BF16, count, 512),
        ]
        + late,
        "v" * 5 + "h" * 5,
        held(*sources) + held(*late) + [pltpu.VMEM((count, 256), F32)] + MASKS,
        (core, *sources),
        "shhhhhh",
        "block_forward",
        24,
    )


def stage_middle(core, pack, factor, sources):
    peers = pack.shape[0]
    count = peers * 8
    signs = [shaped(BF16, *weight.shape) for weight in sources[1::2]]
    return call(
        functools.partial(middle_kernel, factor),
        [shaped(BF16, peers, 16, 256), shaped(BF16, 1536, 256), shaped(BF16, 1536, 256)] + signs,
        "vvvhhhh",
        held(*signs)
        + MASKS
        + [pltpu.VMEM((2, count, 128), F32)] * 3
        + [pltpu.VMEM((count, 256), F32)] * 2
        + [
            pltpu.VMEM((count, 256), BF16),
            pltpu.VMEM((2 * count, 256), BF16),
            pltpu.VMEM((2 * count, 256), BF16),
            pltpu.VMEM((count, 768), BF16),
            pltpu.VMEM((count, 768), BF16),
            pltpu.VMEM((count, 512), BF16),
            pltpu.VMEM((count, 512), BF16),
            pltpu.VMEM((2 * count, 256), BF16),
            pltpu.VMEM((count, 1024), BF16),
            pltpu.VMEM((2 * count, 1024), BF16),
            pltpu.VMEM((count, 256), F32),
            pltpu.VMEM((count, 256), F32),
            pltpu.VMEM((2 * count, 256), BF16),
            pltpu.VMEM((count, 256), BF16),
            pltpu.VMEM((count, 256), BF16),
            pltpu.VMEM((2 * count, 768), BF16),
            pltpu.VMEM((12, 256, 256), BF16),
        ],
        (core, pack, *sources),
        "s" + "v" * 9,
        "middle",
        40,
    )


def stage_back(core, back, saved, weight_out):
    qkv, qkvd, a, ad, h, o, od, _, so = saved
    count = qkv.shape[0]
    late = (weight_out, so, o, od, h)
    return call(
        block_back_kernel,
        [shaped(BF16, 512, 256), shaped(BF16, 512, 256)],
        "vv",
        MASKS
        + [
            pltpu.VMEM((count, 256), BF16),
            pltpu.VMEM((count, 256), BF16),
            pltpu.VMEM((count, 768), BF16),
            pltpu.VMEM((4, 256, 256), BF16),
        ],
        (core, back, qkv, qkvd, a, ad, *late),
        "s" + "v" * 10,
        "block_back",
        20,
    )


def body(
    tokens, target, block_qkv, block_out, grid_qkv, grid_out, mlp_in, mlp_out,
    probe_block_qkv, probe_block_out, probe_grid_qkv, probe_grid_out, probe_mlp_in, probe_mlp_out,
):
    peers = lax.axis_size(PEERS)
    count = tokens.shape[0] * tokens.shape[1]
    factor = 1.0 / math.sqrt(count * peers * lax.axis_size("core"))
    core = lax.axis_index("core").astype(jnp.int32).reshape(1)
    swap = [(0, 1), (1, 0)]

    def exchange(values):
        return lax.all_to_all(values, PEERS, 0, 0, tiled=True)

    pack, *saved = stage_forward(
        core, tokens, target, block_qkv, block_out, probe_block_qkv, probe_block_out, peers
    )
    sources = (
        probe_grid_qkv, grid_qkv, probe_grid_out, grid_out,
        probe_mlp_in, mlp_in, probe_mlp_out, mlp_out,
    )
    back, mid_keep, mid_send, *signs = stage_middle(core, exchange(pack), factor, sources)
    mid_got = lax.ppermute(mid_send, "core", swap)
    keep, send = stage_back(core, exchange(back), saved, block_out)
    got = lax.ppermute(send, "core", swap)
    (parts,) = call(
        pair_sum_kernel,
        [shaped(BF16, peers, 1024 // peers, 512)],
        "v",
        [],
        (mid_keep, mid_got, keep, got),
        "vvvv",
        "pair_sum",
        8,
    )
    parts = exchange(parts)
    (copies,) = call(
        peer_sum_kernel,
        [shaped(BF16, peers, 1024 // peers, 512)],
        "v",
        [],
        (parts,),
        "v",
        "peer_sum",
        8,
    )
    mine = exchange(copies).reshape(1024, 512)
    other = lax.ppermute(mine, "core", swap)
    weights = (block_qkv, block_out, grid_qkv, grid_out, mlp_in, mlp_out)
    signs = (*saved[7:9], *signs)
    outs = [shaped(F32, *weight.shape) for weight in weights]
    wides = [pltpu.VMEM((out.shape[0] // 2, out.shape[1]), F32) for out in outs]
    wides.append(pltpu.SemaphoreType.DMA((9,)))
    *halves, sums = call(
        finish_mine_kernel,
        outs + [shaped(F32, 8, 256)],
        "hhhhhhv",
        wides,
        (core, mine, *signs),
        "s" + "v" * 7,
        "finish_mine",
        16,
    )
    return call(
        finish_other_kernel,
        outs + [shaped(F32, 6)],
        "hhhhhhs",
        wides,
        (core, other, sums, *signs, *halves),
        "s" + "v" * 8 + "h" * 6,
        "finish_other",
        16,
        {9 + n: n for n in range(6)},
    )


def solution(mesh):
    fine = Mesh(mesh.devices.reshape(2, 4, 4, 2, 2), ("y_lo", "x", "z", "y_hi", "core"))
    placed = P(("y_lo", "x"), ("z", "y_hi", "core"), None)
    return jax.shard_map(
        body,
        mesh=fine,
        in_specs=(placed, placed) + (P(),) * 12,
        out_specs=(P(),) * 7,
        check_vma=False,
    )
```

```python
import functools
import math

import jax
import jax.numpy as jnp
from jax import lax
from jax.experimental import pallas as pl
from jax.experimental.pallas import tpu as pltpu
from jax.sharding import Mesh, PartitionSpec as P

F32 = jnp.float32
BF16 = jnp.bfloat16
HD = 32
WINDOW = 64
GROUP = 128
EPSILON = 1e-05
SCALE = HD ** (-0.5)
GELU_K = math.sqrt(2.0 / math.pi)
GELU_C = 0.044715
PEERS = ("x", "z", "y_hi", "y_lo")


def nn(a, b):
    return lax.dot_general(a, b, (((1,), (0,)), ((), ())), preferred_element_type=F32)


def nt(a, b):
    return lax.dot_general(a, b, (((1,), (1,)), ((), ())), preferred_element_type=F32)


def tn(a, b):
    return lax.dot_general(a, b, (((0,), (0,)), ((), ())), preferred_element_type=F32)


def lanes(*parts):
    return jnp.concatenate(parts, axis=1)


def rows(*parts):
    return jnp.concatenate(parts, axis=0)


def mean(values):
    return jnp.mean(values, axis=-1, keepdims=True)


def norm_pair(x, xd):
    center = x - mean(x)
    inverse = lax.rsqrt(mean(center * center) + EPSILON)
    h = center * inverse
    cd = xd - mean(xd)
    along = mean(h * cd)
    return h, inverse * (cd - h * along), inverse, -inverse * along


def norm_back_pair(h, hd, inverse, slope, dy, dyd):
    second = mean(dy * h)
    dx = inverse * (dy - mean(dy) - h * second)
    second_dot = mean(dyd * h + dy * hd)
    dxd = slope * dx + inverse * (dyd - mean(dyd) - hd * second - h * second_dot)
    return dx, dxd


def fetch(sources, buffers, sems):
    copies = [
        pltpu.make_async_copy(source, buffer, sems.at[i])
        for i, (source, buffer) in enumerate(zip(sources, buffers))
    ]
    for copy in copies:
        copy.start()
    return lambda *places: [copies[place].wait() for place in places]


def unpack_signs(words_ref, out_ref):
    total, width = out_ref.shape
    for start in range(0, total, 16):
        row = start + lax.broadcasted_iota(jnp.int32, (16, 1), 0)
        first = start // 30
        edge = 30 * (first + 1)
        word = jnp.broadcast_to(words_ref[first : first + 1, :], (16, width))
        shift = row - 30 * first
        if edge < start + 16:
            later = jnp.broadcast_to(words_ref[first + 1 : first + 2, :], (16, width))
            word = jnp.where(row < edge, word, later)
            shift = jnp.where(row < edge, shift, row - edge)
        bit = jnp.right_shift(word, jnp.broadcast_to(shift, (16, width))) & 1
        out_ref[start : start + 16, :] = (1 - 2 * bit).astype(F32).astype(BF16)


def fill_masks(ones_ref, mask_ref):
    head_row = lax.broadcasted_iota(jnp.int32, (256, 256), 0) // WINDOW
    head_col = lax.broadcasted_iota(jnp.int32, (256, 256), 1) // WINDOW
    ones_ref[...] = (head_row == head_col).astype(F32).astype(BF16)
    head_row = lax.broadcasted_iota(jnp.int32, (256, GROUP), 0) // WINDOW
    head_col = lax.broadcasted_iota(jnp.int32, (256, GROUP), 1) // HD
    mask_ref[...] = (head_row == head_col).astype(F32).astype(BF16)


def spread(values, mask):
    return rows(values, values, values, values) * mask


def collect(values):
    lane = lax.broadcasted_iota(jnp.int32, (WINDOW, GROUP), 1)
    parts = [values[WINDOW * i : WINDOW * (i + 1), :] for i in range(4)]
    low = jnp.where(lane < HD, parts[0], parts[1])
    high = jnp.where(lane < 3 * HD, parts[2], parts[3])
    return jnp.where(lane < 2 * HD, low, high)


BATCH = 8


def per_batch(windows, step):
    def some(i, carry):
        step(
            [
                pl.ds(pl.multiple_of((i * BATCH + n) * WINDOW, WINDOW), WINDOW)
                for n in range(BATCH)
            ]
        )
        return carry

    lax.fori_loop(0, windows // BATCH, some, 0)


def heads_of(ref, at, kind, g):
    return ref[at, pl.ds(256 * kind + GROUP * g, GROUP)]


def twice(values, dots):
    return rows(lanes(values, jnp.zeros_like(values)), lanes(dots, values))


def stacked(values, dots, weight, weight_dot):
    both = nn(rows(values, dots), lanes(weight, weight_dot))
    width = weight.shape[1]
    return both[:WINDOW, :width], both[WINDOW:, :width] + both[:WINDOW, width:]


def segment_sums(values, ones):
    total = nn(rows(*[value.astype(BF16) for value in values]), ones)
    return [total[WINDOW * i : WINDOW * (i + 1), :] for i in range(len(values))]


def attend(qkv_ref, qkvd_ref, a_ref, ad_ref, o_ref, od_ref, ones_ref, mask_ref):
    def step(spots):
        ones = ones_ref[...]
        mask = mask_ref[...]
        units = [(at, g) for at in spots for g in range(2)]
        raised, scores_dot = [], []
        for at, g in units:
            q, qd = heads_of(qkv_ref, at, 0, g), heads_of(qkvd_ref, at, 0, g)
            kb = spread(heads_of(qkv_ref, at, 1, g), mask)
            kdb = spread(heads_of(qkvd_ref, at, 1, g), mask)
            both = nt(twice(q, qd), lanes(kb, kdb)) * SCALE
            raised.append(jnp.exp(both[:WINDOW]))
            scores_dot.append(both[WINDOW:])
        weights = [e / total for e, total in zip(raised, segment_sums(raised, ones))]
        moved = [w * sd for w, sd in zip(weights, scores_dot)]
        sums = segment_sums(moved, ones)
        weights_dot = [m - w * total for m, w, total in zip(moved, weights, sums)]
        for (at, g), w, wd in zip(units, weights, weights_dot):
            a, ad = w.astype(BF16), wd.astype(BF16)
            spot = pl.ds(256 * g, 256)
            a_ref[at, spot] = a
            ad_ref[at, spot] = ad
            vb = spread(heads_of(qkv_ref, at, 2, g), mask)
            vdb = spread(heads_of(qkvd_ref, at, 2, g), mask)
            here = pl.ds(GROUP * g, GROUP)
            o, od = stacked(a, ad, vb, vdb)
            o_ref[at, here] = o.astype(BF16)
            od_ref[at, here] = od.astype(BF16)

    per_batch(qkv_ref.shape[0] // WINDOW, step)


def attend_back(
    qkv_ref, qkvd_ref, a_ref, ad_ref, do_ref, dod_ref, dqkv_ref, dqkvd_ref, ones_ref, mask_ref
):
    def step(spots):
        ones = ones_ref[...]
        mask = mask_ref[...]
        units = [(at, g) for at in spots for g in range(2)]
        da, dad, first, second = [], [], [], []
        for at, g in units:
            here = pl.ds(GROUP * g, GROUP)
            vb = spread(heads_of(qkv_ref, at, 2, g), mask)
            vdb = spread(heads_of(qkvd_ref, at, 2, g), mask)
            both = nt(twice(do_ref[at, here], dod_ref[at, here]), lanes(vb, vdb))
            da.append(both[:WINDOW])
            dad.append(both[WINDOW:])
        for (at, g), x, xd in zip(units, da, dad):
            spot = pl.ds(256 * g, 256)
            a, ad = a_ref[at, spot].astype(F32), ad_ref[at, spot].astype(F32)
            first.append(a * x)
            second.append(ad * x + a * xd)
        first, second = segment_sums(first, ones), segment_sums(second, ones)
        for (at, g), x, xd, total, total_dot in zip(units, da, dad, first, second):
            spot = pl.ds(256 * g, 256)
            here = pl.ds(GROUP * g, GROUP)
            qs, ks, vs = (pl.ds(256 * i + GROUP * g, GROUP) for i in range(3))
            ab, adb = a_ref[at, spot], ad_ref[at, spot]
            a, ad = ab.astype(F32) * SCALE, adb.astype(F32) * SCALE
            rest = x - total
            rest_dot = xd - total_dot
            ds = (a * rest).astype(BF16)
            dsd = (ad * rest + a * rest_dot).astype(BF16)
            do, dod = do_ref[at, here], dod_ref[at, here]
            q, qd = qkv_ref[at, qs], qkvd_ref[at, qs]
            kb, kdb = spread(qkv_ref[at, ks], mask), spread(qkvd_ref[at, ks], mask)
            dq, dqd = stacked(ds, dsd, kb, kdb)
            dqkvd_ref[at, qs] = dqd.astype(BF16)
            if dqkv_ref is None:
                dqkvd_ref[at, ks] = collect(tn(rows(dsd, ds), rows(q, qd))).astype(BF16)
                dqkvd_ref[at, vs] = collect(tn(rows(adb, ab), rows(do, dod))).astype(BF16)
            else:
                dqkv_ref[at, qs] = dq.astype(BF16)
                both = tn(rows(dsd, ds), twice(q, qd))
                dqkvd_ref[at, ks] = collect(both[:, :GROUP]).astype(BF16)
                dqkv_ref[at, ks] = collect(both[:, GROUP:]).astype(BF16)
                both = tn(rows(adb, ab), twice(do, dod))
                dqkvd_ref[at, vs] = collect(both[:, :GROUP]).astype(BF16)
                dqkv_ref[at, vs] = collect(both[:, GROUP:]).astype(BF16)

    per_batch(qkv_ref.shape[0] // WINDOW, step)


def block_forward_kernel(
    core_ref, pq_hbm, tok_hbm, wq_hbm, po_hbm, wo_hbm, tgt_hbm,
    pack_ref, qkv_ref, qkvd_ref, a_ref, ad_ref, h_hbm, o_hbm, od_hbm, sq_hbm, so_hbm,
    pq_ref, tok_ref, wq_ref, po_ref, wo_ref, tgt_ref, sems,
    h_ref, o_ref, od_ref, sq_ref, so_ref, out_sems, x_ref, ones_ref, mask_ref,
):
    wait = fetch(
        (pq_hbm, tok_hbm, wq_hbm, po_hbm, wo_hbm, tgt_hbm),
        (pq_ref, tok_ref, wq_ref, po_ref, wo_ref, tgt_ref),
        sems,
    )
    fill_masks(ones_ref, mask_ref)
    wait(0)
    unpack_signs(pq_ref, sq_ref)
    wait(1, 2)
    for half in range(2):
        at = pl.ds(256 * half, 256)
        slab = tok_ref[8 * half : 8 * half + 8].astype(F32)
        x = rows(*[slab[:, 8 * i : 8 * i + 8, :].reshape(WINDOW, 256) for i in range(4)])
        x_ref[at, :] = x
        center = x - mean(x)
        h = (center * lax.rsqrt(mean(center * center) + EPSILON)).astype(BF16)
        h_ref[at, :] = h
        qkv_ref[at, :] = nn(h, wq_ref[...]).astype(BF16)
        qkvd_ref[at, :] = nn(h, sq_ref[...]).astype(BF16)
    attend(qkv_ref, qkvd_ref, a_ref, ad_ref, o_ref, od_ref, ones_ref, mask_ref)
    wait(3, 4, 5)
    unpack_signs(po_ref, so_ref)
    saved = fetch(
        (h_ref, o_ref, od_ref, sq_ref, so_ref), (h_hbm, o_hbm, od_hbm, sq_hbm, so_hbm), out_sems
    )
    for half in range(2):
        at = pl.ds(256 * half, 256)
        out = pl.ds(32 * half, 32)
        o, od = o_ref[at, :], od_ref[at, :]
        x = x_ref[at, :] + nn(o, wo_ref[...])
        xd = nn(lanes(od, o), rows(wo_ref[...], so_ref[...]))
        both = jnp.concatenate([x.reshape(32, 8, 256), xd.reshape(32, 8, 256)], axis=1)
        pack_ref[out, :, 0:256] = both.astype(BF16)
        slab = tgt_ref[8 * half : 8 * half + 8].astype(F32)
        t = jnp.concatenate([slab[:, 8 * i : 8 * i + 8, :] for i in range(4)], axis=0)
        both = jnp.concatenate([t[:, :, 0:128], t[:, :, 128:256]], axis=1)
        pack_ref[out, :, 256:384] = both.astype(BF16)
    saved(0, 1, 2, 3, 4)


def middle_kernel(
    factor,
    core_ref, pack_ref, pq_ref, wq_ref, po_ref, wo_ref, pi_ref, wi_ref, pf_ref, wf_ref,
    back_ref, keep_ref, send_ref, sq_hbm, so_hbm, si_hbm, sf_hbm,
    sq_ref, so_ref, si_ref, sf_ref, out_sems, ones_ref, mask_ref, mix_ref, mixd_ref, mixt_ref,
    x_ref, xd_ref, t_ref, h1_ref, h2_ref, qkv_ref, qkvd_ref, a_ref, ad_ref, o_ref,
    ud_ref, dz_ref, dx_ref, dxd_ref, dg_ref, do_ref, dod_ref, dqkv_ref, hv_ref,
):
    tokens = x_ref.shape[0]
    fill_masks(ones_ref, mask_ref)
    arrived = pack_ref[:, :, 0:256].astype(F32)
    for c in range(2):
        mix_ref[c] = arrived[:, 0:8, 128 * c : 128 * c + 128].reshape(tokens, 128)
        mixd_ref[c] = arrived[:, 8:16, 128 * c : 128 * c + 128].reshape(tokens, 128)
    arrived = pack_ref[:, :, 256:384].astype(F32) * factor
    for c in range(2):
        mixt_ref[c] = arrived[:, 8 * c : 8 * c + 8, :].reshape(tokens, 128)
    for w in range(8):
        at = pl.ds(WINDOW * w, WINDOW)
        for c in range(2):
            cols = pl.ds(128 * c, 128)
            x_ref[at, cols] = mix_ref[c, pl.ds(w, WINDOW, stride=8), :]
            xd_ref[at, cols] = mixd_ref[c, pl.ds(w, WINDOW, stride=8), :]
            t_ref[at, cols] = mixt_ref[c, pl.ds(w, WINDOW, stride=8), :].astype(BF16)
    unpack_signs(pq_ref, sq_ref)

    def first(i):
        at = pl.ds(i * 256, 256)
        low = pl.ds(i * 256 + tokens, 256)
        h, hd, _, _ = norm_pair(x_ref[at, :], xd_ref[at, :])
        h, hd = h.astype(BF16), hd.astype(BF16)
        h1_ref[at, :] = hd
        h1_ref[low, :] = h
        qkv_ref[at, :] = nn(h, wq_ref[...]).astype(BF16)
        qkvd_ref[at, :] = nn(lanes(hd, h), rows(wq_ref[...], sq_ref[...])).astype(BF16)

    for i in range(tokens // 256):
        first(i)
    o_part, od_part = o_ref.at[pl.ds(tokens, tokens), :], o_ref.at[pl.ds(0, tokens), :]
    attend(qkv_ref, qkvd_ref, a_ref, ad_ref, o_part, od_part, ones_ref, mask_ref)
    unpack_signs(po_ref, so_ref)
    unpack_signs(pi_ref, si_ref)
    unpack_signs(pf_ref, sf_ref)
    saved = fetch(
        (sq_ref, so_ref, si_ref, sf_ref), (sq_hbm, so_hbm, si_hbm, sf_hbm), out_sems
    )

    def second(i):
        at = pl.ds(i * 512, 512)
        low = pl.ds(i * 512 + tokens, 512)
        od, o = o_ref[at, :], o_ref[low, :]
        g = nn(o, wo_ref[...]).astype(BF16).astype(F32)
        gd = nn(lanes(od, o), rows(wo_ref[...], so_ref[...])).astype(BF16).astype(F32)
        h, hd, inverse, slope = norm_pair(x_ref[at, :] + g, xd_ref[at, :] + gd)
        hb, hdb = h.astype(BF16), hd.astype(BF16)
        h2_ref[at, :] = hdb
        h2_ref[low, :] = hb
        t = t_ref[at, :]
        dh = jnp.zeros((512, 256), F32)
        dhd = jnp.zeros((512, 256), F32)
        for c in range(4):
            cols = pl.ds(256 * c, 256)
            wi, si = wi_ref[:, cols], si_ref[:, cols]
            z = nn(hb, wi)
            zd = nn(lanes(hdb, hb), rows(wi, si))
            du = nt(t, wf_ref[cols, :])
            dud = nt(t, sf_ref[cols, :])
            square = z * z
            cubic = (GELU_K * GELU_C) * square
            bend = jnp.tanh(z * (GELU_K + cubic))
            inner = GELU_K + 3.0 * cubic
            level = 1.0 - bend * bend
            slope1 = 0.5 * (1.0 + bend + (z * inner) * level)
            slope2 = level * (GELU_K + 6.0 * cubic - (z * bend) * (inner * inner))
            ud_ref[at, cols] = (slope1 * zd).astype(BF16)
            dz = (du * slope1).astype(BF16)
            dzd = (dud * slope1 + (du * zd) * slope2).astype(BF16)
            dz_ref[at, cols] = dz
            dz_ref[low, cols] = dzd
            dh = dh + nt(dz, wi)
            dhd = dhd + nt(lanes(dzd, dz), lanes(wi, si))
        dx, dxd = norm_back_pair(h, hd, inverse, slope, dh, dhd)
        dx = dx + t.astype(F32)
        dx_ref[at, :] = dx
        dxd_ref[at, :] = dxd
        dg, dgd = dx.astype(BF16), dxd.astype(BF16)
        dg_ref[at, :] = dg
        dg_ref[low, :] = dgd
        do_ref[at, :] = nt(dg, wo_ref[...]).astype(BF16)
        dod_ref[at, :] = nt(lanes(dgd, dg), lanes(wo_ref[...], so_ref[...])).astype(BF16)

    for i in range(tokens // 512):
        second(i)
    dqkv, dqkvd = dqkv_ref.at[pl.ds(0, tokens), :], dqkv_ref.at[pl.ds(tokens, tokens), :]
    attend_back(
        qkv_ref, qkvd_ref, a_ref, ad_ref, do_ref, dod_ref, dqkv, dqkvd, ones_ref, mask_ref
    )

    for i in range(tokens // 256):
        at = pl.ds(i * 256, 256)
        low = pl.ds(i * 256 + tokens, 256)
        dqkv, dqkvd = dqkv_ref[at, :], dqkv_ref[low, :]
        dh = nt(dqkv, wq_ref[...])
        dhd = nt(lanes(dqkvd, dqkv), lanes(wq_ref[...], sq_ref[...]))
        h, hd, inverse, slope = norm_pair(x_ref[at, :], xd_ref[at, :])
        dx, dxd = norm_back_pair(h, hd, inverse, slope, dh, dhd)
        dx_ref[at, :] += dx
        dxd_ref[at, :] += dxd
    for w in range(8):
        at = pl.ds(WINDOW * w, WINDOW)
        for c in range(2):
            cols = pl.ds(128 * c, 128)
            mix_ref[c, pl.ds(w, WINDOW, stride=8), :] = dx_ref[at, cols]
            mixd_ref[c, pl.ds(w, WINDOW, stride=8), :] = dxd_ref[at, cols]
    for c in range(2):
        dx = mix_ref[c].reshape(tokens // 8, 8, 128)
        dxd = mixd_ref[c].reshape(tokens // 8, 8, 128)
        both = jnp.concatenate([dx, dxd], axis=1)
        back_ref[:, :, 128 * c : 128 * c + 128] = both.astype(BF16)

    def put(block, value):
        hv_ref[block] = value.astype(BF16)

    h1 = h1_ref[...]
    for c in range(3):
        put(c, tn(h1, dqkv_ref[:, 256 * c : 256 * c + 256]))
    put(3, tn(o_ref[...], dg_ref[...]))
    h2 = h2_ref[...]
    for c in range(4):
        put(4 + c, tn(h2, dz_ref[:, 256 * c : 256 * c + 256]))
    t = t_ref[...]
    for c in range(4):
        put(8 + c, tn(ud_ref[:, 256 * c : 256 * c + 256], t))
    saved(0, 1, 2, 3)
    split_halves(core_ref, hv_ref, keep_ref, send_ref)


def split_halves(core_ref, hv_ref, keep_ref, send_ref):
    core = core_ref[0]
    mine = pl.ds(pl.multiple_of(core * 128, 128), 128)
    other = pl.ds(pl.multiple_of((1 - core) * 128, 128), 128)
    for block in range(hv_ref.shape[0]):
        keep_ref[128 * block : 128 * block + 128, :] = hv_ref[block, mine, :]
        send_ref[128 * block : 128 * block + 128, :] = hv_ref[block, other, :]


def block_back_kernel(
    core_ref, back_ref, qkv_ref, qkvd_ref, a_ref, ad_ref, wo_ref, so_ref, o_ref, od_ref, h_ref,
    keep_ref, send_ref,
    ones_ref, mask_ref, do_ref, dod_ref, dqkvd_ref, hv_ref,
):
    tokens = h_ref.shape[0]
    fill_masks(ones_ref, mask_ref)
    arrived = back_ref[...].astype(F32)
    dx = arrived[:, 0:8, :].reshape(tokens, 256).astype(BF16)
    dxd = arrived[:, 8:16, :].reshape(tokens, 256).astype(BF16)
    do_ref[...] = nt(dx, wo_ref[...]).astype(BF16)
    dod_ref[...] = nt(lanes(dxd, dx), lanes(wo_ref[...], so_ref[...])).astype(BF16)
    hv_ref[3] = tn(rows(od_ref[...], o_ref[...]), rows(dx, dxd)).astype(BF16)
    attend_back(
        qkv_ref, qkvd_ref, a_ref, ad_ref, do_ref, dod_ref, None, dqkvd_ref, ones_ref, mask_ref
    )
    h = h_ref[...]
    for c in range(3):
        hv_ref[c] = tn(h, dqkvd_ref[:, 256 * c : 256 * c + 256]).astype(BF16)
    split_halves(core_ref, hv_ref, keep_ref, send_ref)


def pair_sum_kernel(mid_keep_ref, mid_got_ref, keep_ref, got_ref, out_ref):
    peers, height, _ = out_ref.shape

    def put(first, keep, got):
        total = (keep.astype(F32) + got.astype(F32)).astype(BF16)
        side, place = first // 1024, first % 1024 // height
        count = total.shape[0] // height
        out_ref[place : place + count, :, 256 * side : 256 * side + 256] = total.reshape(
            count, height, 256
        )

    put(0, mid_keep_ref[0:1024, :], mid_got_ref[0:1024, :])
    put(1024, mid_keep_ref[1024:1536, :], mid_got_ref[1024:1536, :])
    put(1536, keep_ref[...], got_ref[...])


def peer_sum_kernel(parts_ref, out_ref):
    total = parts_ref[0].astype(F32)
    for i in range(1, parts_ref.shape[0]):
        total = total + parts_ref[i].astype(F32)
    total = total.astype(BF16)
    for i in range(parts_ref.shape[0]):
        out_ref[i] = total


PLACES = (12, 15, 0, 3, 4, 8)


def write_half(who, half_ref, sign_refs, out_hbms, wide_refs, sems):
    copies, sums = [], {}
    for n in (4, 5, 0, 2, 1, 3):
        base, sign_ref, out_hbm, wide_ref = PLACES[n], sign_refs[n], out_hbms[n], wide_refs[n]
        height, width = out_hbm.shape
        across = width // 256
        total = jnp.zeros((8, 256), F32)
        for block in range(height * width // 65536):
            cols = pl.ds(256 * (block % across), 256)
            down = block // across
            at = pl.ds(pl.multiple_of(256 * down + who * 128, 128), 128)
            spot = pl.ds(128 * ((base + block) % 8), 128)
            side = pl.ds(256 * ((base + block) // 8), 256)
            value = half_ref[spot, side].astype(F32)
            wide_ref[128 * down : 128 * down + 128, cols] = value
            signed = value * sign_ref[at, cols].astype(F32)
            total = total + jnp.sum(signed.reshape(16, 8, 256), axis=0)
        for down in range(height // 256):
            at = pl.ds(pl.multiple_of(256 * down + who * 128, 128), 128)
            copies.append(
                pltpu.make_async_copy(
                    wide_ref.at[pl.ds(128 * down, 128), :], out_hbm.at[at, :], sems.at[len(copies)]
                )
            )
            copies[-1].start()
        sums[n] = jnp.sum(total, axis=0, keepdims=True)
    for copy in copies:
        copy.wait()
    return rows(*[sums[n] for n in range(6)], jnp.zeros((2, 256), F32))


def finish_mine_kernel(core_ref, half_ref, *refs):
    signs, outs, sum_ref, wides, sems = refs[:6], refs[6:12], refs[12], refs[13:19], refs[19]
    sum_ref[...] = write_half(core_ref[0], half_ref, signs, outs, wides, sems)


def finish_other_kernel(core_ref, half_ref, sum_ref, *refs):
    signs, outs, trace_ref, wides, sems = refs[:6], refs[12:18], refs[18], refs[19:25], refs[25]
    sums = sum_ref[...] + write_half(1 - core_ref[0], half_ref, signs, outs, wides, sems)
    for n, out in enumerate(outs):
        trace_ref[n] = jnp.sum(sums[n : n + 1, :]) / math.sqrt(out.shape[0] * out.shape[1])


def shaped(dtype, *shape):
    return jax.ShapeDtypeStruct(shape, dtype)


def held(*arrays):
    buffers = [pltpu.VMEM(array.shape, array.dtype) for array in arrays]
    return buffers + [pltpu.SemaphoreType.DMA((len(arrays),))]


def call(kernel, outs, spaces, scratch, operands, places, name, limit, aliases=None):
    kinds = {"s": pltpu.SMEM, "v": pltpu.VMEM, "h": pltpu.HBM}
    pinned = [
        pltpu.with_memory_space_constraint(operand, pltpu.HBM) if place == "h" else operand
        for operand, place in zip(operands, places)
    ]
    return pl.pallas_call(
        kernel,
        out_shape=[
            pltpu.HBM(out.shape, out.dtype) if space == "h" else out
            for out, space in zip(outs, spaces)
        ],
        in_specs=[pl.BlockSpec(memory_space=kinds[place]) for place in places],
        out_specs=[pl.BlockSpec(memory_space=kinds[space]) for space in spaces],
        scratch_shapes=scratch,
        input_output_aliases=aliases or {},
        compiler_params=pltpu.CompilerParams(vmem_limit_bytes=limit * 2**20),
        name=name,
    )(*pinned)


MASKS = [pltpu.VMEM((256, 256), BF16), pltpu.VMEM((256, GROUP), BF16)]


def stage_forward(core, tokens, target, weight_qkv, weight_out, words_qkv, words_out, peers):
    count = tokens.shape[0] * tokens.shape[1]
    sources = (words_qkv, tokens, weight_qkv, words_out, weight_out, target)
    late = [
        shaped(BF16, count, 256),
        shaped(BF16, count, 256),
        shaped(BF16, count, 256),
        shaped(BF16, 256, 768),
        shaped(BF16, 256, 256),
    ]
    return call(
        block_forward_kernel,
        [
            shaped(BF16, peers, 16, 384),
            shaped(BF16, count, 768),
            shaped(BF16, count, 768),
            shaped(BF16, count, 512),
            shaped(BF16, count, 512),
        ]
        + late,
        "v" * 5 + "h" * 5,
        held(*sources) + held(*late) + [pltpu.VMEM((count, 256), F32)] + MASKS,
        (core, *sources),
        "shhhhhh",
        "block_forward",
        24,
    )


def stage_middle(core, pack, factor, sources):
    peers = pack.shape[0]
    count = peers * 8
    signs = [shaped(BF16, *weight.shape) for weight in sources[1::2]]
    return call(
        functools.partial(middle_kernel, factor),
        [shaped(BF16, peers, 16, 256), shaped(BF16, 1536, 256), shaped(BF16, 1536, 256)] + signs,
        "vvvhhhh",
        held(*signs)
        + MASKS
        + [pltpu.VMEM((2, count, 128), F32)] * 3
        + [pltpu.VMEM((count, 256), F32)] * 2
        + [
            pltpu.VMEM((count, 256), BF16),
            pltpu.VMEM((2 * count, 256), BF16),
            pltpu.VMEM((2 * count, 256), BF16),
            pltpu.VMEM((count, 768), BF16),
            pltpu.VMEM((count, 768), BF16),
            pltpu.VMEM((count, 512), BF16),
            pltpu.VMEM((count, 512), BF16),
            pltpu.VMEM((2 * count, 256), BF16),
            pltpu.VMEM((count, 1024), BF16),
            pltpu.VMEM((2 * count, 1024), BF16),
            pltpu.VMEM((count, 256), F32),
            pltpu.VMEM((count, 256), F32),
            pltpu.VMEM((2 * count, 256), BF16),
            pltpu.VMEM((count, 256), BF16),
            pltpu.VMEM((count, 256), BF16),
            pltpu.VMEM((2 * count, 768), BF16),
            pltpu.VMEM((12, 256, 256), BF16),
        ],
        (core, pack, *sources),
        "s" + "v" * 9,
        "middle",
        40,
    )


def stage_back(core, back, saved, weight_out):
    qkv, qkvd, a, ad, h, o, od, _, so = saved
    count = qkv.shape[0]
    late = (weight_out, so, o, od, h)
    return call(
        block_back_kernel,
        [shaped(BF16, 512, 256), shaped(BF16, 512, 256)],
        "vv",
        MASKS
        + [
            pltpu.VMEM((count, 256), BF16),
            pltpu.VMEM((count, 256), BF16),
            pltpu.VMEM((count, 768), BF16),
            pltpu.VMEM((4, 256, 256), BF16),
        ],
        (core, back, qkv, qkvd, a, ad, *late),
        "s" + "v" * 10,
        "block_back",
        20,
    )


def body(
    tokens, target, block_qkv, block_out, grid_qkv, grid_out, mlp_in, mlp_out,
    probe_block_qkv, probe_block_out, probe_grid_qkv, probe_grid_out, probe_mlp_in, probe_mlp_out,
):
    peers = lax.axis_size(PEERS)
    count = tokens.shape[0] * tokens.shape[1]
    factor = 1.0 / math.sqrt(count * peers * lax.axis_size("core"))
    core = lax.axis_index("core").astype(jnp.int32).reshape(1)
    swap = [(0, 1), (1, 0)]

    def exchange(values):
        return lax.all_to_all(values, PEERS, 0, 0, tiled=True)

    pack, *saved = stage_forward(
        core, tokens, target, block_qkv, block_out, probe_block_qkv, probe_block_out, peers
    )
    sources = (
        probe_grid_qkv, grid_qkv, probe_grid_out, grid_out,
        probe_mlp_in, mlp_in, probe_mlp_out, mlp_out,
    )
    back, mid_keep, mid_send, *signs = stage_middle(core, exchange(pack), factor, sources)
    back, mid_send = lax.optimization_barrier((exchange(back), mid_send))
    mid_got = lax.ppermute(mid_send, "core", swap)
    keep, send = stage_back(core, back, saved, block_out)
    got = lax.ppermute(send, "core", swap)
    (parts,) = call(
        pair_sum_kernel,
        [shaped(BF16, peers, 1024 // peers, 512)],
        "v",
        [],
        (mid_keep, mid_got, keep, got),
        "vvvv",
        "pair_sum",
        8,
    )
    parts = exchange(parts)
    (copies,) = call(
        peer_sum_kernel,
        [shaped(BF16, peers, 1024 // peers, 512)],
        "v",
        [],
        (parts,),
        "v",
        "peer_sum",
        8,
    )
    mine = exchange(copies).reshape(1024, 512)
    other = lax.ppermute(mine, "core", swap)
    weights = (block_qkv, block_out, grid_qkv, grid_out, mlp_in, mlp_out)
    signs = (*saved[7:9], *signs)
    outs = [shaped(F32, *weight.shape) for weight in weights]
    wides = [pltpu.VMEM((out.shape[0] // 2, out.shape[1]), F32) for out in outs]
    wides.append(pltpu.SemaphoreType.DMA((9,)))
    *halves, sums = call(
        finish_mine_kernel,
        outs + [shaped(F32, 8, 256)],
        "hhhhhhv",
        wides,
        (core, mine, *signs),
        "s" + "v" * 7,
        "finish_mine",
        16,
    )
    return call(
        finish_other_kernel,
        outs + [shaped(F32, 6)],
        "hhhhhhs",
        wides,
        (core, other, sums, *signs, *halves),
        "s" + "v" * 8 + "h" * 6,
        "finish_other",
        16,
        {9 + n: n for n in range(6)},
    )


def solution(mesh):
    fine = Mesh(mesh.devices.reshape(2, 4, 4, 2, 2), ("y_lo", "x", "z", "y_hi", "core"))
    placed = P(("y_lo", "x"), ("z", "y_hi", "core"), None)
    return jax.shard_map(
        body,
        mesh=fine,
        in_specs=(placed, placed) + (P(),) * 12,
        out_specs=(P(),) * 7,
        check_vma=False,
    )
```

```python
import functools
import math

import jax
import jax.numpy as jnp
from jax import lax
from jax.experimental import pallas as pl
from jax.experimental.pallas import tpu as pltpu
from jax.sharding import Mesh, PartitionSpec as P

F32 = jnp.float32
BF16 = jnp.bfloat16
HD = 32
WINDOW = 64
GROUP = 128
EPSILON = 1e-05
SCALE = HD ** (-0.5)
GELU_K = math.sqrt(2.0 / math.pi)
GELU_C = 0.044715
PEERS = ("x", "z", "y_hi", "y_lo")


def nn(a, b):
    return lax.dot_general(a, b, (((1,), (0,)), ((), ())), preferred_element_type=F32)


def nt(a, b):
    return lax.dot_general(a, b, (((1,), (1,)), ((), ())), preferred_element_type=F32)


def tn(a, b):
    return lax.dot_general(a, b, (((0,), (0,)), ((), ())), preferred_element_type=F32)


def lanes(*parts):
    return jnp.concatenate(parts, axis=1)


def rows(*parts):
    return jnp.concatenate(parts, axis=0)


def mean(values):
    return jnp.mean(values, axis=-1, keepdims=True)


def norm_pair(x, xd):
    center = x - mean(x)
    inverse = lax.rsqrt(mean(center * center) + EPSILON)
    h = center * inverse
    cd = xd - mean(xd)
    along = mean(h * cd)
    return h, inverse * (cd - h * along), inverse, -inverse * along


def norm_back_pair(h, hd, inverse, slope, dy, dyd):
    second = mean(dy * h)
    dx = inverse * (dy - mean(dy) - h * second)
    second_dot = mean(dyd * h + dy * hd)
    dxd = slope * dx + inverse * (dyd - mean(dyd) - hd * second - h * second_dot)
    return dx, dxd


def fetch(sources, buffers, sems):
    copies = [
        pltpu.make_async_copy(source, buffer, sems.at[i])
        for i, (source, buffer) in enumerate(zip(sources, buffers))
    ]
    for copy in copies:
        copy.start()
    return lambda *places: [copies[place].wait() for place in places]


def unpack_signs(words_ref, out_ref):
    total, width = out_ref.shape
    for start in range(0, total, 16):
        row = start + lax.broadcasted_iota(jnp.int32, (16, 1), 0)
        first = start // 30
        edge = 30 * (first + 1)
        word = jnp.broadcast_to(words_ref[first : first + 1, :], (16, width))
        shift = row - 30 * first
        if edge < start + 16:
            later = jnp.broadcast_to(words_ref[first + 1 : first + 2, :], (16, width))
            word = jnp.where(row < edge, word, later)
            shift = jnp.where(row < edge, shift, row - edge)
        bit = jnp.right_shift(word, jnp.broadcast_to(shift, (16, width))) & 1
        out_ref[start : start + 16, :] = (1 - 2 * bit).astype(F32).astype(BF16)


def fill_masks(ones_ref, mask_ref):
    head_row = lax.broadcasted_iota(jnp.int32, (256, 256), 0) // WINDOW
    head_col = lax.broadcasted_iota(jnp.int32, (256, 256), 1) // WINDOW
    ones_ref[...] = (head_row == head_col).astype(F32).astype(BF16)
    head_row = lax.broadcasted_iota(jnp.int32, (256, GROUP), 0) // WINDOW
    head_col = lax.broadcasted_iota(jnp.int32, (256, GROUP), 1) // HD
    mask_ref[...] = (head_row == head_col).astype(F32).astype(BF16)


def spread(values, mask):
    return rows(values, values, values, values) * mask


def collect(values):
    lane = lax.broadcasted_iota(jnp.int32, (WINDOW, GROUP), 1)
    parts = [values[WINDOW * i : WINDOW * (i + 1), :] for i in range(4)]
    low = jnp.where(lane < HD, parts[0], parts[1])
    high = jnp.where(lane < 3 * HD, parts[2], parts[3])
    return jnp.where(lane < 2 * HD, low, high)


BATCH = 8


def per_batch(windows, step):
    def some(i, carry):
        step(
            [
                pl.ds(pl.multiple_of((i * BATCH + n) * WINDOW, WINDOW), WINDOW)
                for n in range(BATCH)
            ]
        )
        return carry

    lax.fori_loop(0, windows // BATCH, some, 0)


def heads_of(ref, at, kind, g):
    return ref[at, pl.ds(256 * kind + GROUP * g, GROUP)]


def twice(values, dots):
    return rows(lanes(values, jnp.zeros_like(values)), lanes(dots, values))


def stacked(values, dots, weight, weight_dot):
    both = nn(rows(values, dots), lanes(weight, weight_dot))
    width = weight.shape[1]
    return both[:WINDOW, :width], both[WINDOW:, :width] + both[:WINDOW, width:]


def head_sums(values, mask):
    total = nt(rows(*[value.astype(BF16) for value in values]), mask)
    return [total[WINDOW * i : WINDOW * (i + 1), :] for i in range(len(values))]


def segment_sums(values, ones):
    total = nn(rows(*[value.astype(BF16) for value in values]), ones)
    return [total[WINDOW * i : WINDOW * (i + 1), :] for i in range(len(values))]


def attend(qkv_ref, qkvd_ref, a_ref, ad_ref, o_ref, od_ref, ones_ref, mask_ref):
    def step(spots):
        ones = ones_ref[...]
        mask = mask_ref[...]
        units = [(at, g) for at in spots for g in range(2)]
        raised, scores_dot = [], []
        for at, g in units:
            q, qd = heads_of(qkv_ref, at, 0, g), heads_of(qkvd_ref, at, 0, g)
            kb = spread(heads_of(qkv_ref, at, 1, g), mask)
            kdb = spread(heads_of(qkvd_ref, at, 1, g), mask)
            both = nt(twice(q, qd), lanes(kb, kdb)) * SCALE
            raised.append(jnp.exp(both[:WINDOW]))
            scores_dot.append(both[WINDOW:])
        weights = [e / total for e, total in zip(raised, segment_sums(raised, ones))]
        moved = [w * sd for w, sd in zip(weights, scores_dot)]
        sums = segment_sums(moved, ones)
        weights_dot = [m - w * total for m, w, total in zip(moved, weights, sums)]
        for (at, g), w, wd in zip(units, weights, weights_dot):
            a, ad = w.astype(BF16), wd.astype(BF16)
            spot = pl.ds(256 * g, 256)
            a_ref[at, spot] = a
            ad_ref[at, spot] = ad
            vb = spread(heads_of(qkv_ref, at, 2, g), mask)
            vdb = spread(heads_of(qkvd_ref, at, 2, g), mask)
            here = pl.ds(GROUP * g, GROUP)
            o, od = stacked(a, ad, vb, vdb)
            o_ref[at, here] = o.astype(BF16)
            od_ref[at, here] = od.astype(BF16)

    per_batch(qkv_ref.shape[0] // WINDOW, step)


def attend_back(
    qkv_ref, qkvd_ref, a_ref, ad_ref, o_ref, od_ref, do_ref, dod_ref, dqkv_ref, dqkvd_ref,
    mask_ref,
):
    def step(spots):
        mask = mask_ref[...]
        units = [(at, g) for at in spots for g in range(2)]
        da, dad, first, second = [], [], [], []
        for at, g in units:
            here = pl.ds(GROUP * g, GROUP)
            vb = spread(heads_of(qkv_ref, at, 2, g), mask)
            vdb = spread(heads_of(qkvd_ref, at, 2, g), mask)
            both = nt(twice(do_ref[at, here], dod_ref[at, here]), lanes(vb, vdb))
            da.append(both[:WINDOW])
            dad.append(both[WINDOW:])
            do, dod = do_ref[at, here].astype(F32), dod_ref[at, here].astype(F32)
            o, od = o_ref[at, here].astype(F32), od_ref[at, here].astype(F32)
            first.append(do * o)
            second.append(dod * o + do * od)
        first, second = head_sums(first, mask), head_sums(second, mask)
        for (at, g), x, xd, total, total_dot in zip(units, da, dad, first, second):
            spot = pl.ds(256 * g, 256)
            here = pl.ds(GROUP * g, GROUP)
            qs, ks, vs = (pl.ds(256 * i + GROUP * g, GROUP) for i in range(3))
            ab, adb = a_ref[at, spot], ad_ref[at, spot]
            a, ad = ab.astype(F32) * SCALE, adb.astype(F32) * SCALE
            rest = x - total
            rest_dot = xd - total_dot
            ds = (a * rest).astype(BF16)
            dsd = (ad * rest + a * rest_dot).astype(BF16)
            do, dod = do_ref[at, here], dod_ref[at, here]
            q, qd = qkv_ref[at, qs], qkvd_ref[at, qs]
            kb, kdb = spread(qkv_ref[at, ks], mask), spread(qkvd_ref[at, ks], mask)
            dq, dqd = stacked(ds, dsd, kb, kdb)
            dqkvd_ref[at, qs] = dqd.astype(BF16)
            if dqkv_ref is None:
                dqkvd_ref[at, ks] = collect(tn(rows(dsd, ds), rows(q, qd))).astype(BF16)
                dqkvd_ref[at, vs] = collect(tn(rows(adb, ab), rows(do, dod))).astype(BF16)
            else:
                dqkv_ref[at, qs] = dq.astype(BF16)
                both = tn(rows(dsd, ds), twice(q, qd))
                dqkvd_ref[at, ks] = collect(both[:, :GROUP]).astype(BF16)
                dqkv_ref[at, ks] = collect(both[:, GROUP:]).astype(BF16)
                both = tn(rows(adb, ab), twice(do, dod))
                dqkvd_ref[at, vs] = collect(both[:, :GROUP]).astype(BF16)
                dqkv_ref[at, vs] = collect(both[:, GROUP:]).astype(BF16)

    per_batch(qkv_ref.shape[0] // WINDOW, step)


def block_forward_kernel(
    core_ref, pq_hbm, tok_hbm, wq_hbm, po_hbm, wo_hbm, tgt_hbm,
    pack_ref, qkv_ref, qkvd_ref, a_ref, ad_ref, h_hbm, o_hbm, od_hbm, sq_hbm, so_hbm,
    pq_ref, tok_ref, wq_ref, po_ref, wo_ref, tgt_ref, sems,
    h_ref, o_ref, od_ref, sq_ref, so_ref, out_sems, x_ref, ones_ref, mask_ref,
):
    wait = fetch(
        (pq_hbm, tok_hbm, wq_hbm, po_hbm, wo_hbm, tgt_hbm),
        (pq_ref, tok_ref, wq_ref, po_ref, wo_ref, tgt_ref),
        sems,
    )
    fill_masks(ones_ref, mask_ref)
    wait(0)
    unpack_signs(pq_ref, sq_ref)
    wait(1, 2)
    for half in range(2):
        at = pl.ds(256 * half, 256)
        slab = tok_ref[8 * half : 8 * half + 8].astype(F32)
        x = rows(*[slab[:, 8 * i : 8 * i + 8, :].reshape(WINDOW, 256) for i in range(4)])
        x_ref[at, :] = x
        center = x - mean(x)
        h = (center * lax.rsqrt(mean(center * center) + EPSILON)).astype(BF16)
        h_ref[at, :] = h
        qkv_ref[at, :] = nn(h, wq_ref[...]).astype(BF16)
        qkvd_ref[at, :] = nn(h, sq_ref[...]).astype(BF16)
    attend(qkv_ref, qkvd_ref, a_ref, ad_ref, o_ref, od_ref, ones_ref, mask_ref)
    wait(3, 4, 5)
    unpack_signs(po_ref, so_ref)
    saved = fetch(
        (h_ref, o_ref, od_ref, sq_ref, so_ref), (h_hbm, o_hbm, od_hbm, sq_hbm, so_hbm), out_sems
    )
    for half in range(2):
        at = pl.ds(256 * half, 256)
        out = pl.ds(32 * half, 32)
        o, od = o_ref[at, :], od_ref[at, :]
        x = x_ref[at, :] + nn(o, wo_ref[...])
        xd = nn(lanes(od, o), rows(wo_ref[...], so_ref[...]))
        both = jnp.concatenate([x.reshape(32, 8, 256), xd.reshape(32, 8, 256)], axis=1)
        pack_ref[out, :, 0:256] = both.astype(BF16)
        slab = tgt_ref[8 * half : 8 * half + 8].astype(F32)
        t = jnp.concatenate([slab[:, 8 * i : 8 * i + 8, :] for i in range(4)], axis=0)
        both = jnp.concatenate([t[:, :, 0:128], t[:, :, 128:256]], axis=1)
        pack_ref[out, :, 256:384] = both.astype(BF16)
    saved(0, 1, 2, 3, 4)


def middle_kernel(
    factor,
    core_ref, pack_ref, pq_ref, wq_ref, po_ref, wo_ref, pi_ref, wi_ref, pf_ref, wf_ref,
    back_ref, keep_ref, send_ref, sq_hbm, so_hbm, si_hbm, sf_hbm,
    sq_ref, so_ref, si_ref, sf_ref, out_sems, ones_ref, mask_ref, mix_ref, mixd_ref, mixt_ref,
    x_ref, xd_ref, t_ref, h1_ref, h2_ref, qkv_ref, qkvd_ref, a_ref, ad_ref, o_ref,
    ud_ref, dz_ref, dx_ref, dxd_ref, dg_ref, do_ref, dod_ref, dqkv_ref, hv_ref,
):
    tokens = x_ref.shape[0]
    fill_masks(ones_ref, mask_ref)
    arrived = pack_ref[:, :, 0:256].astype(F32)
    for c in range(2):
        mix_ref[c] = arrived[:, 0:8, 128 * c : 128 * c + 128].reshape(tokens, 128)
        mixd_ref[c] = arrived[:, 8:16, 128 * c : 128 * c + 128].reshape(tokens, 128)
    arrived = pack_ref[:, :, 256:384].astype(F32) * factor
    for c in range(2):
        mixt_ref[c] = arrived[:, 8 * c : 8 * c + 8, :].reshape(tokens, 128)
    for w in range(8):
        at = pl.ds(WINDOW * w, WINDOW)
        for c in range(2):
            cols = pl.ds(128 * c, 128)
            x_ref[at, cols] = mix_ref[c, pl.ds(w, WINDOW, stride=8), :]
            xd_ref[at, cols] = mixd_ref[c, pl.ds(w, WINDOW, stride=8), :]
            t_ref[at, cols] = mixt_ref[c, pl.ds(w, WINDOW, stride=8), :].astype(BF16)
    unpack_signs(pq_ref, sq_ref)

    def first(i):
        at = pl.ds(i * 256, 256)
        low = pl.ds(i * 256 + tokens, 256)
        h, hd, _, _ = norm_pair(x_ref[at, :], xd_ref[at, :])
        h, hd = h.astype(BF16), hd.astype(BF16)
        h1_ref[at, :] = hd
        h1_ref[low, :] = h
        qkv_ref[at, :] = nn(h, wq_ref[...]).astype(BF16)
        qkvd_ref[at, :] = nn(lanes(hd, h), rows(wq_ref[...], sq_ref[...])).astype(BF16)

    for i in range(tokens // 256):
        first(i)
    o_part, od_part = o_ref.at[pl.ds(tokens, tokens), :], o_ref.at[pl.ds(0, tokens), :]
    attend(qkv_ref, qkvd_ref, a_ref, ad_ref, o_part, od_part, ones_ref, mask_ref)
    unpack_signs(po_ref, so_ref)
    unpack_signs(pi_ref, si_ref)
    unpack_signs(pf_ref, sf_ref)
    saved = fetch(
        (sq_ref, so_ref, si_ref, sf_ref), (sq_hbm, so_hbm, si_hbm, sf_hbm), out_sems
    )

    def second(i):
        at = pl.ds(i * 512, 512)
        low = pl.ds(i * 512 + tokens, 512)
        od, o = o_ref[at, :], o_ref[low, :]
        g = nn(o, wo_ref[...]).astype(BF16).astype(F32)
        gd = nn(lanes(od, o), rows(wo_ref[...], so_ref[...])).astype(BF16).astype(F32)
        h, hd, inverse, slope = norm_pair(x_ref[at, :] + g, xd_ref[at, :] + gd)
        hb, hdb = h.astype(BF16), hd.astype(BF16)
        h2_ref[at, :] = hdb
        h2_ref[low, :] = hb
        t = t_ref[at, :]
        dh = jnp.zeros((512, 256), F32)
        dhd = jnp.zeros((512, 256), F32)
        for c in range(4):
            cols = pl.ds(256 * c, 256)
            wi, si = wi_ref[:, cols], si_ref[:, cols]
            z = nn(hb, wi)
            zd = nn(lanes(hdb, hb), rows(wi, si))
            du = nt(t, wf_ref[cols, :])
            dud = nt(t, sf_ref[cols, :])
            square = z * z
            cubic = (GELU_K * GELU_C) * square
            bend = jnp.tanh(z * (GELU_K + cubic))
            inner = GELU_K + 3.0 * cubic
            level = 1.0 - bend * bend
            slope1 = 0.5 * (1.0 + bend + (z * inner) * level)
            slope2 = level * (GELU_K + 6.0 * cubic - (z * bend) * (inner * inner))
            ud_ref[at, cols] = (slope1 * zd).astype(BF16)
            dz = (du * slope1).astype(BF16)
            dzd = (dud * slope1 + (du * zd) * slope2).astype(BF16)
            dz_ref[at, cols] = dz
            dz_ref[low, cols] = dzd
            dh = dh + nt(dz, wi)
            dhd = dhd + nt(lanes(dzd, dz), lanes(wi, si))
        dx, dxd = norm_back_pair(h, hd, inverse, slope, dh, dhd)
        dx = dx + t.astype(F32)
        dx_ref[at, :] = dx
        dxd_ref[at, :] = dxd
        dg, dgd = dx.astype(BF16), dxd.astype(BF16)
        dg_ref[at, :] = dg
        dg_ref[low, :] = dgd
        do_ref[at, :] = nt(dg, wo_ref[...]).astype(BF16)
        dod_ref[at, :] = nt(lanes(dgd, dg), lanes(wo_ref[...], so_ref[...])).astype(BF16)

    for i in range(tokens // 512):
        second(i)
    dqkv, dqkvd = dqkv_ref.at[pl.ds(0, tokens), :], dqkv_ref.at[pl.ds(tokens, tokens), :]
    attend_back(
        qkv_ref, qkvd_ref, a_ref, ad_ref, o_part, od_part, do_ref, dod_ref, dqkv, dqkvd, mask_ref
    )

    for i in range(tokens // 256):
        at = pl.ds(i * 256, 256)
        low = pl.ds(i * 256 + tokens, 256)
        dqkv, dqkvd = dqkv_ref[at, :], dqkv_ref[low, :]
        dh = nt(dqkv, wq_ref[...])
        dhd = nt(lanes(dqkvd, dqkv), lanes(wq_ref[...], sq_ref[...]))
        h, hd, inverse, slope = norm_pair(x_ref[at, :], xd_ref[at, :])
        dx, dxd = norm_back_pair(h, hd, inverse, slope, dh, dhd)
        dx_ref[at, :] += dx
        dxd_ref[at, :] += dxd
    for w in range(8):
        at = pl.ds(WINDOW * w, WINDOW)
        for c in range(2):
            cols = pl.ds(128 * c, 128)
            mix_ref[c, pl.ds(w, WINDOW, stride=8), :] = dx_ref[at, cols]
            mixd_ref[c, pl.ds(w, WINDOW, stride=8), :] = dxd_ref[at, cols]
    for c in range(2):
        dx = mix_ref[c].reshape(tokens // 8, 8, 128)
        dxd = mixd_ref[c].reshape(tokens // 8, 8, 128)
        both = jnp.concatenate([dx, dxd], axis=1)
        back_ref[:, :, 128 * c : 128 * c + 128] = both.astype(BF16)

    def put(block, value):
        hv_ref[block] = value.astype(BF16)

    h1 = h1_ref[...]
    for c in range(3):
        put(c, tn(h1, dqkv_ref[:, 256 * c : 256 * c + 256]))
    put(3, tn(o_ref[...], dg_ref[...]))
    h2 = h2_ref[...]
    for c in range(4):
        put(4 + c, tn(h2, dz_ref[:, 256 * c : 256 * c + 256]))
    t = t_ref[...]
    for c in range(4):
        put(8 + c, tn(ud_ref[:, 256 * c : 256 * c + 256], t))
    saved(0, 1, 2, 3)
    split_halves(core_ref, hv_ref, keep_ref, send_ref)


def split_halves(core_ref, hv_ref, keep_ref, send_ref):
    core = core_ref[0]
    mine = pl.ds(pl.multiple_of(core * 128, 128), 128)
    other = pl.ds(pl.multiple_of((1 - core) * 128, 128), 128)
    for block in range(hv_ref.shape[0]):
        keep_ref[128 * block : 128 * block + 128, :] = hv_ref[block, mine, :]
        send_ref[128 * block : 128 * block + 128, :] = hv_ref[block, other, :]


def block_back_kernel(
    core_ref, back_ref, qkv_ref, qkvd_ref, a_ref, ad_ref, wo_ref, so_ref, o_ref, od_ref, h_ref,
    keep_ref, send_ref,
    ones_ref, mask_ref, do_ref, dod_ref, dqkvd_ref, hv_ref,
):
    tokens = h_ref.shape[0]
    fill_masks(ones_ref, mask_ref)
    arrived = back_ref[...].astype(F32)
    dx = arrived[:, 0:8, :].reshape(tokens, 256).astype(BF16)
    dxd = arrived[:, 8:16, :].reshape(tokens, 256).astype(BF16)
    do_ref[...] = nt(dx, wo_ref[...]).astype(BF16)
    dod_ref[...] = nt(lanes(dxd, dx), lanes(wo_ref[...], so_ref[...])).astype(BF16)
    hv_ref[3] = tn(rows(od_ref[...], o_ref[...]), rows(dx, dxd)).astype(BF16)
    attend_back(
        qkv_ref, qkvd_ref, a_ref, ad_ref, o_ref, od_ref, do_ref, dod_ref, None, dqkvd_ref, mask_ref
    )
    h = h_ref[...]
    for c in range(3):
        hv_ref[c] = tn(h, dqkvd_ref[:, 256 * c : 256 * c + 256]).astype(BF16)
    split_halves(core_ref, hv_ref, keep_ref, send_ref)


def pair_sum_kernel(mid_keep_ref, mid_got_ref, keep_ref, got_ref, out_ref):
    peers, height, _ = out_ref.shape

    def put(first, keep, got):
        total = (keep.astype(F32) + got.astype(F32)).astype(BF16)
        side, place = first // 1024, first % 1024 // height
        count = total.shape[0] // height
        out_ref[place : place + count, :, 256 * side : 256 * side + 256] = total.reshape(
            count, height, 256
        )

    put(0, mid_keep_ref[0:1024, :], mid_got_ref[0:1024, :])
    put(1024, mid_keep_ref[1024:1536, :], mid_got_ref[1024:1536, :])
    put(1536, keep_ref[...], got_ref[...])


def peer_sum_kernel(parts_ref, out_ref):
    total = parts_ref[0].astype(F32)
    for i in range(1, parts_ref.shape[0]):
        total = total + parts_ref[i].astype(F32)
    total = total.astype(BF16)
    for i in range(parts_ref.shape[0]):
        out_ref[i] = total


PLACES = (12, 15, 0, 3, 4, 8)


def write_half(who, half_ref, sign_refs, out_hbms, wide_refs, sems):
    copies, sums = [], {}
    for n in (4, 5, 0, 2, 1, 3):
        base, sign_ref, out_hbm, wide_ref = PLACES[n], sign_refs[n], out_hbms[n], wide_refs[n]
        height, width = out_hbm.shape
        across = width // 256
        total = jnp.zeros((8, 256), F32)
        for block in range(height * width // 65536):
            cols = pl.ds(256 * (block % across), 256)
            down = block // across
            at = pl.ds(pl.multiple_of(256 * down + who * 128, 128), 128)
            spot = pl.ds(128 * ((base + block) % 8), 128)
            side = pl.ds(256 * ((base + block) // 8), 256)
            value = half_ref[spot, side].astype(F32)
            wide_ref[128 * down : 128 * down + 128, cols] = value
            signed = value * sign_ref[at, cols].astype(F32)
            total = total + jnp.sum(signed.reshape(16, 8, 256), axis=0)
        for down in range(height // 256):
            at = pl.ds(pl.multiple_of(256 * down + who * 128, 128), 128)
            copies.append(
                pltpu.make_async_copy(
                    wide_ref.at[pl.ds(128 * down, 128), :], out_hbm.at[at, :], sems.at[len(copies)]
                )
            )
            copies[-1].start()
        sums[n] = jnp.sum(total, axis=0, keepdims=True)
    return copies, rows(*[sums[n] for n in range(6)], jnp.zeros((2, 256), F32))


def finish_mine_kernel(core_ref, half_ref, *refs):
    signs, outs, sum_ref, wides, sems = refs[:6], refs[6:12], refs[12], refs[13:19], refs[19]
    copies, sums = write_half(core_ref[0], half_ref, signs, outs, wides, sems)
    sum_ref[...] = sums
    for copy in copies:
        copy.wait()


def finish_other_kernel(core_ref, half_ref, sum_ref, *refs):
    signs, outs, trace_ref, wides, sems = refs[:6], refs[12:18], refs[18], refs[19:25], refs[25]
    copies, sums = write_half(1 - core_ref[0], half_ref, signs, outs, wides, sems)
    sums = sums + sum_ref[...]
    for n, out in enumerate(outs):
        trace_ref[n] = jnp.sum(sums[n : n + 1, :]) / math.sqrt(out.shape[0] * out.shape[1])
    for copy in copies:
        copy.wait()


def shaped(dtype, *shape):
    return jax.ShapeDtypeStruct(shape, dtype)


def held(*arrays):
    buffers = [pltpu.VMEM(array.shape, array.dtype) for array in arrays]
    return buffers + [pltpu.SemaphoreType.DMA((len(arrays),))]


def call(kernel, outs, spaces, scratch, operands, places, name, limit, aliases=None):
    kinds = {"s": pltpu.SMEM, "v": pltpu.VMEM, "h": pltpu.HBM}
    pinned = [
        pltpu.with_memory_space_constraint(operand, pltpu.HBM) if place == "h" else operand
        for operand, place in zip(operands, places)
    ]
    return pl.pallas_call(
        kernel,
        out_shape=[
            pltpu.HBM(out.shape, out.dtype) if space == "h" else out
            for out, space in zip(outs, spaces)
        ],
        in_specs=[pl.BlockSpec(memory_space=kinds[place]) for place in places],
        out_specs=[pl.BlockSpec(memory_space=kinds[space]) for space in spaces],
        scratch_shapes=scratch,
        input_output_aliases=aliases or {},
        compiler_params=pltpu.CompilerParams(vmem_limit_bytes=limit * 2**20),
        name=name,
    )(*pinned)


MASKS = [pltpu.VMEM((256, 256), BF16), pltpu.VMEM((256, GROUP), BF16)]


def stage_forward(core, tokens, target, weight_qkv, weight_out, words_qkv, words_out, peers):
    count = tokens.shape[0] * tokens.shape[1]
    sources = (words_qkv, tokens, weight_qkv, words_out, weight_out, target)
    late = [
        shaped(BF16, count, 256),
        shaped(BF16, count, 256),
        shaped(BF16, count, 256),
        shaped(BF16, 256, 768),
        shaped(BF16, 256, 256),
    ]
    return call(
        block_forward_kernel,
        [
            shaped(BF16, peers, 16, 384),
            shaped(BF16, count, 768),
            shaped(BF16, count, 768),
            shaped(BF16, count, 512),
            shaped(BF16, count, 512),
        ]
        + late,
        "v" * 5 + "h" * 5,
        held(*sources) + held(*late) + [pltpu.VMEM((count, 256), F32)] + MASKS,
        (core, *sources),
        "shhhhhh",
        "block_forward",
        24,
    )


def stage_middle(core, pack, factor, sources):
    peers = pack.shape[0]
    count = peers * 8
    signs = [shaped(BF16, *weight.shape) for weight in sources[1::2]]
    return call(
        functools.partial(middle_kernel, factor),
        [shaped(BF16, peers, 16, 256), shaped(BF16, 1536, 256), shaped(BF16, 1536, 256)] + signs,
        "vvvhhhh",
        held(*signs)
        + MASKS
        + [pltpu.VMEM((2, count, 128), F32)] * 3
        + [pltpu.VMEM((count, 256), F32)] * 2
        + [
            pltpu.VMEM((count, 256), BF16),
            pltpu.VMEM((2 * count, 256), BF16),
            pltpu.VMEM((2 * count, 256), BF16),
            pltpu.VMEM((count, 768), BF16),
            pltpu.VMEM((count, 768), BF16),
            pltpu.VMEM((count, 512), BF16),
            pltpu.VMEM((count, 512), BF16),
            pltpu.VMEM((2 * count, 256), BF16),
            pltpu.VMEM((count, 1024), BF16),
            pltpu.VMEM((2 * count, 1024), BF16),
            pltpu.VMEM((count, 256), F32),
            pltpu.VMEM((count, 256), F32),
            pltpu.VMEM((2 * count, 256), BF16),
            pltpu.VMEM((count, 256), BF16),
            pltpu.VMEM((count, 256), BF16),
            pltpu.VMEM((2 * count, 768), BF16),
            pltpu.VMEM((12, 256, 256), BF16),
        ],
        (core, pack, *sources),
        "s" + "v" * 9,
        "middle",
        40,
    )


def stage_back(core, back, saved, weight_out):
    qkv, qkvd, a, ad, h, o, od, _, so = saved
    count = qkv.shape[0]
    late = (weight_out, so, o, od, h)
    return call(
        block_back_kernel,
        [shaped(BF16, 512, 256), shaped(BF16, 512, 256)],
        "vv",
        MASKS
        + [
            pltpu.VMEM((count, 256), BF16),
            pltpu.VMEM((count, 256), BF16),
            pltpu.VMEM((count, 768), BF16),
            pltpu.VMEM((4, 256, 256), BF16),
        ],
        (core, back, qkv, qkvd, a, ad, *late),
        "s" + "v" * 10,
        "block_back",
        20,
    )


def body(
    tokens, target, block_qkv, block_out, grid_qkv, grid_out, mlp_in, mlp_out,
    probe_block_qkv, probe_block_out, probe_grid_qkv, probe_grid_out, probe_mlp_in, probe_mlp_out,
):
    peers = lax.axis_size(PEERS)
    count = tokens.shape[0] * tokens.shape[1]
    factor = 1.0 / math.sqrt(count * peers * lax.axis_size("core"))
    core = lax.axis_index("core").astype(jnp.int32).reshape(1)
    swap = [(0, 1), (1, 0)]

    def exchange(values):
        return lax.all_to_all(values, PEERS, 0, 0, tiled=True)

    pack, *saved = stage_forward(
        core, tokens, target, block_qkv, block_out, probe_block_qkv, probe_block_out, peers
    )
    sources = (
        probe_grid_qkv, grid_qkv, probe_grid_out, grid_out,
        probe_mlp_in, mlp_in, probe_mlp_out, mlp_out,
    )
    back, mid_keep, mid_send, *signs = stage_middle(core, exchange(pack), factor, sources)
    back, mid_send = lax.optimization_barrier((exchange(back), mid_send))
    mid_got = lax.ppermute(mid_send, "core", swap)
    keep, send = stage_back(core, back, saved, block_out)
    got = lax.ppermute(send, "core", swap)
    (parts,) = call(
        pair_sum_kernel,
        [shaped(BF16, peers, 1024 // peers, 512)],
        "v",
        [],
        (mid_keep, mid_got, keep, got),
        "vvvv",
        "pair_sum",
        8,
    )
    parts = exchange(parts)
    (copies,) = call(
        peer_sum_kernel,
        [shaped(BF16, peers, 1024 // peers, 512)],
        "v",
        [],
        (parts,),
        "v",
        "peer_sum",
        8,
    )
    mine = exchange(copies).reshape(1024, 512)
    other = lax.ppermute(mine, "core", swap)
    weights = (block_qkv, block_out, grid_qkv, grid_out, mlp_in, mlp_out)
    signs = (*saved[7:9], *signs)
    outs = [shaped(F32, *weight.shape) for weight in weights]
    wides = [pltpu.VMEM((out.shape[0] // 2, out.shape[1]), F32) for out in outs]
    wides.append(pltpu.SemaphoreType.DMA((9,)))
    *halves, sums = call(
        finish_mine_kernel,
        outs + [shaped(F32, 8, 256)],
        "hhhhhhv",
        wides,
        (core, mine, *signs),
        "s" + "v" * 7,
        "finish_mine",
        16,
    )
    return call(
        finish_other_kernel,
        outs + [shaped(F32, 6)],
        "hhhhhhs",
        wides,
        (core, other, sums, *signs, *halves),
        "s" + "v" * 8 + "h" * 6,
        "finish_other",
        16,
        {9 + n: n for n in range(6)},
    )


def solution(mesh):
    fine = Mesh(mesh.devices.reshape(2, 4, 4, 2, 2), ("y_lo", "x", "z", "y_hi", "core"))
    placed = P(("y_lo", "x"), ("z", "y_hi", "core"), None)
    return jax.shard_map(
        body,
        mesh=fine,
        in_specs=(placed, placed) + (P(),) * 12,
        out_specs=(P(),) * 7,
        check_vma=False,
    )
```

```python
import functools
import math

import jax
import jax.numpy as jnp
from jax import lax
from jax.experimental import pallas as pl
from jax.experimental.pallas import tpu as pltpu
from jax.sharding import Mesh, PartitionSpec as P

F32 = jnp.float32
BF16 = jnp.bfloat16
HD = 32
WINDOW = 64
GROUP = 128
EPSILON = 1e-05
SCALE = HD ** (-0.5)
GELU_K = math.sqrt(2.0 / math.pi)
GELU_C = 0.044715
PEERS = ("y_lo", "z", "x", "y_hi")


def nn(a, b):
    return lax.dot_general(a, b, (((1,), (0,)), ((), ())), preferred_element_type=F32)


def nt(a, b):
    return lax.dot_general(a, b, (((1,), (1,)), ((), ())), preferred_element_type=F32)


def tn(a, b):
    return lax.dot_general(a, b, (((0,), (0,)), ((), ())), preferred_element_type=F32)


def lanes(*parts):
    return jnp.concatenate(parts, axis=1)


def rows(*parts):
    return jnp.concatenate(parts, axis=0)


def mean(values):
    return jnp.mean(values, axis=-1, keepdims=True)


def norm_pair(x, xd):
    center = x - mean(x)
    inverse = lax.rsqrt(mean(center * center) + EPSILON)
    h = center * inverse
    cd = xd - mean(xd)
    along = mean(h * cd)
    return h, inverse * (cd - h * along), inverse, -inverse * along


def norm_back_pair(h, hd, inverse, slope, dy, dyd):
    second = mean(dy * h)
    dx = inverse * (dy - mean(dy) - h * second)
    second_dot = mean(dyd * h + dy * hd)
    dxd = slope * dx + inverse * (dyd - mean(dyd) - hd * second - h * second_dot)
    return dx, dxd


def fetch(sources, buffers, sems):
    copies = [
        pltpu.make_async_copy(source, buffer, sems.at[i])
        for i, (source, buffer) in enumerate(zip(sources, buffers))
    ]
    for copy in copies:
        copy.start()
    return lambda *places: [copies[place].wait() for place in places]


def unpack_signs(words_ref, out_ref):
    total, width = out_ref.shape
    for start in range(0, total, 16):
        row = start + lax.broadcasted_iota(jnp.int32, (16, 1), 0)
        first = start // 30
        edge = 30 * (first + 1)
        word = jnp.broadcast_to(words_ref[first : first + 1, :], (16, width))
        shift = row - 30 * first
        if edge < start + 16:
            later = jnp.broadcast_to(words_ref[first + 1 : first + 2, :], (16, width))
            word = jnp.where(row < edge, word, later)
            shift = jnp.where(row < edge, shift, row - edge)
        bit = jnp.right_shift(word, jnp.broadcast_to(shift, (16, width))) & 1
        out_ref[start : start + 16, :] = (1 - 2 * bit).astype(F32).astype(BF16)


def fill_masks(ones_ref, mask_ref):
    head_row = lax.broadcasted_iota(jnp.int32, (256, 256), 0) // WINDOW
    head_col = lax.broadcasted_iota(jnp.int32, (256, 256), 1) // WINDOW
    ones_ref[...] = (head_row == head_col).astype(F32).astype(BF16)
    head_row = lax.broadcasted_iota(jnp.int32, (256, GROUP), 0) // WINDOW
    head_col = lax.broadcasted_iota(jnp.int32, (256, GROUP), 1) // HD
    mask_ref[...] = (head_row == head_col).astype(F32).astype(BF16)


def spread(values, mask):
    return rows(values, values, values, values) * mask


def collect(values):
    lane = lax.broadcasted_iota(jnp.int32, (WINDOW, GROUP), 1)
    parts = [values[WINDOW * i : WINDOW * (i + 1), :] for i in range(4)]
    low = jnp.where(lane < HD, parts[0], parts[1])
    high = jnp.where(lane < 3 * HD, parts[2], parts[3])
    return jnp.where(lane < 2 * HD, low, high)


BATCH = 8


def per_batch(windows, step):
    def some(i, carry):
        step(
            [
                pl.ds(pl.multiple_of((i * BATCH + n) * WINDOW, WINDOW), WINDOW)
                for n in range(BATCH)
            ]
        )
        return carry

    lax.fori_loop(0, windows // BATCH, some, 0)


def heads_of(ref, at, kind, g):
    return ref[at, pl.ds(256 * kind + GROUP * g, GROUP)]


def twice(values, dots):
    return rows(lanes(values, jnp.zeros_like(values)), lanes(dots, values))


def stacked(values, dots, weight, weight_dot):
    both = nn(rows(values, dots), lanes(weight, weight_dot))
    width = weight.shape[1]
    return both[:WINDOW, :width], both[WINDOW:, :width] + both[:WINDOW, width:]


def segment_sums(values, ones):
    total = nn(rows(*[value.astype(BF16) for value in values]), ones)
    return [total[WINDOW * i : WINDOW * (i + 1), :] for i in range(len(values))]


def attend(qkv_ref, qkvd_ref, a_ref, ad_ref, o_ref, od_ref, ones_ref, mask_ref):
    def step(spots):
        ones = ones_ref[...]
        mask = mask_ref[...]
        units = [(at, g) for at in spots for g in range(2)]
        raised, scores_dot = [], []
        for at, g in units:
            q, qd = heads_of(qkv_ref, at, 0, g), heads_of(qkvd_ref, at, 0, g)
            kb = spread(heads_of(qkv_ref, at, 1, g), mask)
            kdb = spread(heads_of(qkvd_ref, at, 1, g), mask)
            both = nt(twice(q, qd), lanes(kb, kdb)) * SCALE
            raised.append(jnp.exp(both[:WINDOW]))
            scores_dot.append(both[WINDOW:])
        weights = [e / total for e, total in zip(raised, segment_sums(raised, ones))]
        moved = [w * sd for w, sd in zip(weights, scores_dot)]
        sums = segment_sums(moved, ones)
        weights_dot = [m - w * total for m, w, total in zip(moved, weights, sums)]
        for (at, g), w, wd in zip(units, weights, weights_dot):
            a, ad = w.astype(BF16), wd.astype(BF16)
            spot = pl.ds(256 * g, 256)
            a_ref[at, spot] = a
            ad_ref[at, spot] = ad
            vb = spread(heads_of(qkv_ref, at, 2, g), mask)
            vdb = spread(heads_of(qkvd_ref, at, 2, g), mask)
            here = pl.ds(GROUP * g, GROUP)
            o, od = stacked(a, ad, vb, vdb)
            o_ref[at, here] = o.astype(BF16)
            od_ref[at, here] = od.astype(BF16)

    per_batch(qkv_ref.shape[0] // WINDOW, step)


def attend_back(
    qkv_ref, qkvd_ref, a_ref, ad_ref, do_ref, dod_ref, dqkv_ref, dqkvd_ref, ones_ref, mask_ref
):
    def step(spots):
        ones = ones_ref[...]
        mask = mask_ref[...]
        units = [(at, g) for at in spots for g in range(2)]
        da, dad, first, second = [], [], [], []
        for at, g in units:
            here = pl.ds(GROUP * g, GROUP)
            vb = spread(heads_of(qkv_ref, at, 2, g), mask)
            vdb = spread(heads_of(qkvd_ref, at, 2, g), mask)
            both = nt(twice(do_ref[at, here], dod_ref[at, here]), lanes(vb, vdb))
            da.append(both[:WINDOW])
            dad.append(both[WINDOW:])
        for (at, g), x, xd in zip(units, da, dad):
            spot = pl.ds(256 * g, 256)
            a, ad = a_ref[at, spot].astype(F32), ad_ref[at, spot].astype(F32)
            first.append(a * x)
            second.append(ad * x + a * xd)
        first, second = segment_sums(first, ones), segment_sums(second, ones)
        for (at, g), x, xd, total, total_dot in zip(units, da, dad, first, second):
            spot = pl.ds(256 * g, 256)
            here = pl.ds(GROUP * g, GROUP)
            qs, ks, vs = (pl.ds(256 * i + GROUP * g, GROUP) for i in range(3))
            ab, adb = a_ref[at, spot], ad_ref[at, spot]
            a, ad = ab.astype(F32) * SCALE, adb.astype(F32) * SCALE
            rest = x - total
            rest_dot = xd - total_dot
            ds = (a * rest).astype(BF16)
            dsd = (ad * rest + a * rest_dot).astype(BF16)
            do, dod = do_ref[at, here], dod_ref[at, here]
            q, qd = qkv_ref[at, qs], qkvd_ref[at, qs]
            kb, kdb = spread(qkv_ref[at, ks], mask), spread(qkvd_ref[at, ks], mask)
            dq, dqd = stacked(ds, dsd, kb, kdb)
            dqkvd_ref[at, qs] = dqd.astype(BF16)
            if dqkv_ref is None:
                dqkvd_ref[at, ks] = collect(tn(rows(dsd, ds), rows(q, qd))).astype(BF16)
                dqkvd_ref[at, vs] = collect(tn(rows(adb, ab), rows(do, dod))).astype(BF16)
            else:
                dqkv_ref[at, qs] = dq.astype(BF16)
                both = tn(rows(dsd, ds), twice(q, qd))
                dqkvd_ref[at, ks] = collect(both[:, :GROUP]).astype(BF16)
                dqkv_ref[at, ks] = collect(both[:, GROUP:]).astype(BF16)
                both = tn(rows(adb, ab), twice(do, dod))
                dqkvd_ref[at, vs] = collect(both[:, :GROUP]).astype(BF16)
                dqkv_ref[at, vs] = collect(both[:, GROUP:]).astype(BF16)

    per_batch(qkv_ref.shape[0] // WINDOW, step)


def block_forward_kernel(
    core_ref, pq_hbm, tok_hbm, wq_hbm, po_hbm, wo_hbm, tgt_hbm,
    pack_ref, qkv_ref, qkvd_ref, a_ref, ad_ref, h_hbm, o_hbm, od_hbm, sq_hbm, so_hbm,
    pq_ref, tok_ref, wq_ref, po_ref, wo_ref, tgt_ref, sems,
    h_ref, o_ref, od_ref, sq_ref, so_ref, out_sems, x_ref, ones_ref, mask_ref,
):
    wait = fetch(
        (pq_hbm, tok_hbm, wq_hbm, po_hbm, wo_hbm, tgt_hbm),
        (pq_ref, tok_ref, wq_ref, po_ref, wo_ref, tgt_ref),
        sems,
    )
    fill_masks(ones_ref, mask_ref)
    wait(0)
    unpack_signs(pq_ref, sq_ref)
    wait(1, 2)
    for half in range(2):
        at = pl.ds(256 * half, 256)
        slab = tok_ref[8 * half : 8 * half + 8].astype(F32)
        x = rows(*[slab[:, 8 * i : 8 * i + 8, :].reshape(WINDOW, 256) for i in range(4)])
        x_ref[at, :] = x
        center = x - mean(x)
        h = (center * lax.rsqrt(mean(center * center) + EPSILON)).astype(BF16)
        h_ref[at, :] = h
        qkv_ref[at, :] = nn(h, wq_ref[...]).astype(BF16)
        qkvd_ref[at, :] = nn(h, sq_ref[...]).astype(BF16)
    attend(qkv_ref, qkvd_ref, a_ref, ad_ref, o_ref, od_ref, ones_ref, mask_ref)
    wait(3, 4, 5)
    unpack_signs(po_ref, so_ref)
    saved = fetch(
        (h_ref, o_ref, od_ref, sq_ref, so_ref), (h_hbm, o_hbm, od_hbm, sq_hbm, so_hbm), out_sems
    )
    for half in range(2):
        at = pl.ds(256 * half, 256)
        out = pl.ds(32 * half, 32)
        o, od = o_ref[at, :], od_ref[at, :]
        x = x_ref[at, :] + nn(o, wo_ref[...])
        xd = nn(lanes(od, o), rows(wo_ref[...], so_ref[...]))
        both = jnp.concatenate([x.reshape(32, 8, 256), xd.reshape(32, 8, 256)], axis=1)
        pack_ref[out, :, 0:256] = both.astype(BF16)
        slab = tgt_ref[8 * half : 8 * half + 8].astype(F32)
        t = jnp.concatenate([slab[:, 8 * i : 8 * i + 8, :] for i in range(4)], axis=0)
        both = jnp.concatenate([t[:, :, 0:128], t[:, :, 128:256]], axis=1)
        pack_ref[out, :, 256:384] = both.astype(BF16)
    saved(0, 1, 2, 3, 4)


def middle_kernel(
    factor,
    core_ref, pack_ref, pq_ref, wq_ref, po_ref, wo_ref, pi_ref, wi_ref, pf_ref, wf_ref,
    back_ref, keep_ref, send_ref, sq_hbm, so_hbm, si_hbm, sf_hbm,
    sq_ref, so_ref, si_ref, sf_ref, out_sems, ones_ref, mask_ref, mix_ref, mixd_ref, mixt_ref,
    x_ref, xd_ref, t_ref, h1_ref, h2_ref, qkv_ref, qkvd_ref, a_ref, ad_ref, o_ref,
    ud_ref, dz_ref, dx_ref, dxd_ref, dg_ref, do_ref, dod_ref, dqkv_ref, hv_ref,
):
    tokens = x_ref.shape[0]
    fill_masks(ones_ref, mask_ref)
    arrived = pack_ref[:, :, 0:256].astype(F32)
    for c in range(2):
        mix_ref[c] = arrived[:, 0:8, 128 * c : 128 * c + 128].reshape(tokens, 128)
        mixd_ref[c] = arrived[:, 8:16, 128 * c : 128 * c + 128].reshape(tokens, 128)
    arrived = pack_ref[:, :, 256:384].astype(F32) * factor
    for c in range(2):
        mixt_ref[c] = arrived[:, 8 * c : 8 * c + 8, :].reshape(tokens, 128)
    for w in range(8):
        at = pl.ds(WINDOW * w, WINDOW)
        for c in range(2):
            cols = pl.ds(128 * c, 128)
            x_ref[at, cols] = mix_ref[c, pl.ds(w, WINDOW, stride=8), :]
            xd_ref[at, cols] = mixd_ref[c, pl.ds(w, WINDOW, stride=8), :]
            t_ref[at, cols] = mixt_ref[c, pl.ds(w, WINDOW, stride=8), :].astype(BF16)
    unpack_signs(pq_ref, sq_ref)

    def first(i):
        at = pl.ds(i * 256, 256)
        low = pl.ds(i * 256 + tokens, 256)
        h, hd, _, _ = norm_pair(x_ref[at, :], xd_ref[at, :])
        h, hd = h.astype(BF16), hd.astype(BF16)
        h1_ref[at, :] = hd
        h1_ref[low, :] = h
        qkv_ref[at, :] = nn(h, wq_ref[...]).astype(BF16)
        qkvd_ref[at, :] = nn(lanes(hd, h), rows(wq_ref[...], sq_ref[...])).astype(BF16)

    for i in range(tokens // 256):
        first(i)
    o_part, od_part = o_ref.at[pl.ds(tokens, tokens), :], o_ref.at[pl.ds(0, tokens), :]
    attend(qkv_ref, qkvd_ref, a_ref, ad_ref, o_part, od_part, ones_ref, mask_ref)
    unpack_signs(po_ref, so_ref)
    unpack_signs(pi_ref, si_ref)
    unpack_signs(pf_ref, sf_ref)
    saved = fetch(
        (sq_ref, so_ref, si_ref, sf_ref), (sq_hbm, so_hbm, si_hbm, sf_hbm), out_sems
    )

    def second(i):
        at = pl.ds(i * 512, 512)
        low = pl.ds(i * 512 + tokens, 512)
        od, o = o_ref[at, :], o_ref[low, :]
        g = nn(o, wo_ref[...]).astype(BF16).astype(F32)
        gd = nn(lanes(od, o), rows(wo_ref[...], so_ref[...])).astype(BF16).astype(F32)
        h, hd, inverse, slope = norm_pair(x_ref[at, :] + g, xd_ref[at, :] + gd)
        hb, hdb = h.astype(BF16), hd.astype(BF16)
        h2_ref[at, :] = hdb
        h2_ref[low, :] = hb
        t = t_ref[at, :]
        dh = jnp.zeros((512, 256), F32)
        dhd = jnp.zeros((512, 256), F32)
        for c in range(4):
            cols = pl.ds(256 * c, 256)
            wi, si = wi_ref[:, cols], si_ref[:, cols]
            z = nn(hb, wi)
            zd = nn(lanes(hdb, hb), rows(wi, si))
            du = nt(t, wf_ref[cols, :])
            dud = nt(t, sf_ref[cols, :])
            square = z * z
            cubic = (GELU_K * GELU_C) * square
            bend = jnp.tanh(z * (GELU_K + cubic))
            inner = GELU_K + 3.0 * cubic
            level = 1.0 - bend * bend
            slope1 = 0.5 * (1.0 + bend + (z * inner) * level)
            slope2 = level * (GELU_K + 6.0 * cubic - (z * bend) * (inner * inner))
            ud_ref[at, cols] = (slope1 * zd).astype(BF16)
            dz = (du * slope1).astype(BF16)
            dzd = (dud * slope1 + (du * zd) * slope2).astype(BF16)
            dz_ref[at, cols] = dz
            dz_ref[low, cols] = dzd
            dh = dh + nt(dz, wi)
            dhd = dhd + nt(lanes(dzd, dz), lanes(wi, si))
        dx, dxd = norm_back_pair(h, hd, inverse, slope, dh, dhd)
        dx = dx + t.astype(F32)
        dx_ref[at, :] = dx
        dxd_ref[at, :] = dxd
        dg, dgd = dx.astype(BF16), dxd.astype(BF16)
        dg_ref[at, :] = dg
        dg_ref[low, :] = dgd
        do_ref[at, :] = nt(dg, wo_ref[...]).astype(BF16)
        dod_ref[at, :] = nt(lanes(dgd, dg), lanes(wo_ref[...], so_ref[...])).astype(BF16)

    for i in range(tokens // 512):
        second(i)
    dqkv, dqkvd = dqkv_ref.at[pl.ds(0, tokens), :], dqkv_ref.at[pl.ds(tokens, tokens), :]
    attend_back(
        qkv_ref, qkvd_ref, a_ref, ad_ref, do_ref, dod_ref, dqkv, dqkvd, ones_ref, mask_ref
    )

    for i in range(tokens // 256):
        at = pl.ds(i * 256, 256)
        low = pl.ds(i * 256 + tokens, 256)
        dqkv, dqkvd = dqkv_ref[at, :], dqkv_ref[low, :]
        dh = nt(dqkv, wq_ref[...])
        dhd = nt(lanes(dqkvd, dqkv), lanes(wq_ref[...], sq_ref[...]))
        h, hd, inverse, slope = norm_pair(x_ref[at, :], xd_ref[at, :])
        dx, dxd = norm_back_pair(h, hd, inverse, slope, dh, dhd)
        dx_ref[at, :] += dx
        dxd_ref[at, :] += dxd
    for w in range(8):
        at = pl.ds(WINDOW * w, WINDOW)
        for c in range(2):
            cols = pl.ds(128 * c, 128)
            mix_ref[c, pl.ds(w, WINDOW, stride=8), :] = dx_ref[at, cols]
            mixd_ref[c, pl.ds(w, WINDOW, stride=8), :] = dxd_ref[at, cols]
    for c in range(2):
        dx = mix_ref[c].reshape(tokens // 8, 8, 128)
        dxd = mixd_ref[c].reshape(tokens // 8, 8, 128)
        both = jnp.concatenate([dx, dxd], axis=1)
        back_ref[:, :, 128 * c : 128 * c + 128] = both.astype(BF16)

    def put(block, value):
        hv_ref[block] = value.astype(BF16)

    h1 = h1_ref[...]
    for c in range(3):
        put(c, tn(h1, dqkv_ref[:, 256 * c : 256 * c + 256]))
    put(3, tn(o_ref[...], dg_ref[...]))
    h2 = h2_ref[...]
    for c in range(4):
        put(4 + c, tn(h2, dz_ref[:, 256 * c : 256 * c + 256]))
    t = t_ref[...]
    for c in range(4):
        put(8 + c, tn(ud_ref[:, 256 * c : 256 * c + 256], t))
    saved(0, 1, 2, 3)
    split_halves(core_ref, hv_ref, keep_ref, send_ref)


def split_halves(core_ref, hv_ref, keep_ref, send_ref):
    core = core_ref[0]
    mine = pl.ds(pl.multiple_of(core * 128, 128), 128)
    other = pl.ds(pl.multiple_of((1 - core) * 128, 128), 128)
    for block in range(hv_ref.shape[0]):
        keep_ref[128 * block : 128 * block + 128, :] = hv_ref[block, mine, :]
        send_ref[128 * block : 128 * block + 128, :] = hv_ref[block, other, :]


def block_back_kernel(
    core_ref, back_ref, qkv_ref, qkvd_ref, a_ref, ad_ref, wo_ref, so_ref, o_ref, od_ref, h_ref,
    keep_ref, send_ref,
    ones_ref, mask_ref, do_ref, dod_ref, dqkvd_ref, hv_ref,
):
    tokens = h_ref.shape[0]
    fill_masks(ones_ref, mask_ref)
    arrived = back_ref[...].astype(F32)
    dx = arrived[:, 0:8, :].reshape(tokens, 256).astype(BF16)
    dxd = arrived[:, 8:16, :].reshape(tokens, 256).astype(BF16)
    do_ref[...] = nt(dx, wo_ref[...]).astype(BF16)
    dod_ref[...] = nt(lanes(dxd, dx), lanes(wo_ref[...], so_ref[...])).astype(BF16)
    hv_ref[3] = tn(rows(od_ref[...], o_ref[...]), rows(dx, dxd)).astype(BF16)
    attend_back(
        qkv_ref, qkvd_ref, a_ref, ad_ref, do_ref, dod_ref, None, dqkvd_ref, ones_ref, mask_ref
    )
    h = h_ref[...]
    for c in range(3):
        hv_ref[c] = tn(h, dqkvd_ref[:, 256 * c : 256 * c + 256]).astype(BF16)
    split_halves(core_ref, hv_ref, keep_ref, send_ref)


def pair_sum_kernel(mid_keep_ref, mid_got_ref, keep_ref, got_ref, out_ref):
    peers, height, _ = out_ref.shape

    def put(first, keep, got):
        total = (keep.astype(F32) + got.astype(F32)).astype(BF16)
        side, place = first // 1024, first % 1024 // height
        count = total.shape[0] // height
        out_ref[place : place + count, :, 256 * side : 256 * side + 256] = total.reshape(
            count, height, 256
        )

    put(0, mid_keep_ref[0:1024, :], mid_got_ref[0:1024, :])
    put(1024, mid_keep_ref[1024:1536, :], mid_got_ref[1024:1536, :])
    put(1536, keep_ref[...], got_ref[...])


def peer_sum_kernel(parts_ref, out_ref):
    total = parts_ref[0].astype(F32)
    for i in range(1, parts_ref.shape[0]):
        total = total + parts_ref[i].astype(F32)
    total = total.astype(BF16)
    for i in range(parts_ref.shape[0]):
        out_ref[i] = total


PLACES = (12, 15, 0, 3, 4, 8)


def write_half(who, half_ref, sign_refs, out_hbms, wide_refs, sems):
    copies, sums = [], {}
    for n in (4, 5, 0, 2, 1, 3):
        base, sign_ref, out_hbm, wide_ref = PLACES[n], sign_refs[n], out_hbms[n], wide_refs[n]
        height, width = out_hbm.shape
        across = width // 256
        total = jnp.zeros((8, 256), F32)
        for block in range(height * width // 65536):
            cols = pl.ds(256 * (block % across), 256)
            down = block // across
            at = pl.ds(pl.multiple_of(256 * down + who * 128, 128), 128)
            spot = pl.ds(128 * ((base + block) % 8), 128)
            side = pl.ds(256 * ((base + block) // 8), 256)
            value = half_ref[spot, side].astype(F32)
            wide_ref[128 * down : 128 * down + 128, cols] = value
            signed = value * sign_ref[at, cols].astype(F32)
            total = total + jnp.sum(signed.reshape(16, 8, 256), axis=0)
        for down in range(height // 256):
            at = pl.ds(pl.multiple_of(256 * down + who * 128, 128), 128)
            copies.append(
                pltpu.make_async_copy(
                    wide_ref.at[pl.ds(128 * down, 128), :], out_hbm.at[at, :], sems.at[len(copies)]
                )
            )
            copies[-1].start()
        sums[n] = jnp.sum(total, axis=0, keepdims=True)
    for copy in copies:
        copy.wait()
    return rows(*[sums[n] for n in range(6)], jnp.zeros((2, 256), F32))


def finish_mine_kernel(core_ref, half_ref, *refs):
    signs, outs, sum_ref, wides, sems = refs[:6], refs[6:12], refs[12], refs[13:19], refs[19]
    sum_ref[...] = write_half(core_ref[0], half_ref, signs, outs, wides, sems)


def finish_other_kernel(core_ref, half_ref, sum_ref, *refs):
    signs, outs, trace_ref, wides, sems = refs[:6], refs[12:18], refs[18], refs[19:25], refs[25]
    sums = sum_ref[...] + write_half(1 - core_ref[0], half_ref, signs, outs, wides, sems)
    for n, out in enumerate(outs):
        trace_ref[n] = jnp.sum(sums[n : n + 1, :]) / math.sqrt(out.shape[0] * out.shape[1])


def shaped(dtype, *shape):
    return jax.ShapeDtypeStruct(shape, dtype)


def held(*arrays):
    buffers = [pltpu.VMEM(array.shape, array.dtype) for array in arrays]
    return buffers + [pltpu.SemaphoreType.DMA((len(arrays),))]


def call(kernel, outs, spaces, scratch, operands, places, name, limit, aliases=None):
    kinds = {"s": pltpu.SMEM, "v": pltpu.VMEM, "h": pltpu.HBM}
    pinned = [
        pltpu.with_memory_space_constraint(operand, pltpu.HBM) if place == "h" else operand
        for operand, place in zip(operands, places)
    ]
    return pl.pallas_call(
        kernel,
        out_shape=[
            pltpu.HBM(out.shape, out.dtype) if space == "h" else out
            for out, space in zip(outs, spaces)
        ],
        in_specs=[pl.BlockSpec(memory_space=kinds[place]) for place in places],
        out_specs=[pl.BlockSpec(memory_space=kinds[space]) for space in spaces],
        scratch_shapes=scratch,
        input_output_aliases=aliases or {},
        compiler_params=pltpu.CompilerParams(vmem_limit_bytes=limit * 2**20),
        name=name,
    )(*pinned)


MASKS = [pltpu.VMEM((256, 256), BF16), pltpu.VMEM((256, GROUP), BF16)]


def stage_forward(core, tokens, target, weight_qkv, weight_out, words_qkv, words_out, peers):
    count = tokens.shape[0] * tokens.shape[1]
    sources = (words_qkv, tokens, weight_qkv, words_out, weight_out, target)
    late = [
        shaped(BF16, count, 256),
        shaped(BF16, count, 256),
        shaped(BF16, count, 256),
        shaped(BF16, 256, 768),
        shaped(BF16, 256, 256),
    ]
    return call(
        block_forward_kernel,
        [
            shaped(BF16, peers, 16, 384),
            shaped(BF16, count, 768),
            shaped(BF16, count, 768),
            shaped(BF16, count, 512),
            shaped(BF16, count, 512),
        ]
        + late,
        "v" * 5 + "h" * 5,
        held(*sources) + held(*late) + [pltpu.VMEM((count, 256), F32)] + MASKS,
        (core, *sources),
        "shhhhhh",
        "block_forward",
        24,
    )


def stage_middle(core, pack, factor, sources):
    peers = pack.shape[0]
    count = peers * 8
    signs = [shaped(BF16, *weight.shape) for weight in sources[1::2]]
    return call(
        functools.partial(middle_kernel, factor),
        [shaped(BF16, peers, 16, 256), shaped(BF16, 1536, 256), shaped(BF16, 1536, 256)] + signs,
        "vvvhhhh",
        held(*signs)
        + MASKS
        + [pltpu.VMEM((2, count, 128), F32)] * 3
        + [pltpu.VMEM((count, 256), F32)] * 2
        + [
            pltpu.VMEM((count, 256), BF16),
            pltpu.VMEM((2 * count, 256), BF16),
            pltpu.VMEM((2 * count, 256), BF16),
            pltpu.VMEM((count, 768), BF16),
            pltpu.VMEM((count, 768), BF16),
            pltpu.VMEM((count, 512), BF16),
            pltpu.VMEM((count, 512), BF16),
            pltpu.VMEM((2 * count, 256), BF16),
            pltpu.VMEM((count, 1024), BF16),
            pltpu.VMEM((2 * count, 1024), BF16),
            pltpu.VMEM((count, 256), F32),
            pltpu.VMEM((count, 256), F32),
            pltpu.VMEM((2 * count, 256), BF16),
            pltpu.VMEM((count, 256), BF16),
            pltpu.VMEM((count, 256), BF16),
            pltpu.VMEM((2 * count, 768), BF16),
            pltpu.VMEM((12, 256, 256), BF16),
        ],
        (core, pack, *sources),
        "s" + "v" * 9,
        "middle",
        40,
    )


def stage_back(core, back, saved, weight_out):
    qkv, qkvd, a, ad, h, o, od, _, so = saved
    count = qkv.shape[0]
    late = (weight_out, so, o, od, h)
    return call(
        block_back_kernel,
        [shaped(BF16, 512, 256), shaped(BF16, 512, 256)],
        "vv",
        MASKS
        + [
            pltpu.VMEM((count, 256), BF16),
            pltpu.VMEM((count, 256), BF16),
            pltpu.VMEM((count, 768), BF16),
            pltpu.VMEM((4, 256, 256), BF16),
        ],
        (core, back, qkv, qkvd, a, ad, *late),
        "s" + "v" * 10,
        "block_back",
        20,
    )


def body(
    tokens, target, block_qkv, block_out, grid_qkv, grid_out, mlp_in, mlp_out,
    probe_block_qkv, probe_block_out, probe_grid_qkv, probe_grid_out, probe_mlp_in, probe_mlp_out,
):
    peers = lax.axis_size(PEERS)
    count = tokens.shape[0] * tokens.shape[1]
    factor = 1.0 / math.sqrt(count * peers * lax.axis_size("core"))
    core = lax.axis_index("core").astype(jnp.int32).reshape(1)
    swap = [(0, 1), (1, 0)]

    def exchange(values):
        return lax.all_to_all(values, PEERS, 0, 0, tiled=True)

    pack, *saved = stage_forward(
        core, tokens, target, block_qkv, block_out, probe_block_qkv, probe_block_out, peers
    )
    sources = (
        probe_grid_qkv, grid_qkv, probe_grid_out, grid_out,
        probe_mlp_in, mlp_in, probe_mlp_out, mlp_out,
    )
    back, mid_keep, mid_send, *signs = stage_middle(core, exchange(pack), factor, sources)
    back, mid_send = lax.optimization_barrier((exchange(back), mid_send))
    mid_got = lax.ppermute(mid_send, "core", swap)
    keep, send = stage_back(core, back, saved, block_out)
    got = lax.ppermute(send, "core", swap)
    (parts,) = call(
        pair_sum_kernel,
        [shaped(BF16, peers, 1024 // peers, 512)],
        "v",
        [],
        (mid_keep, mid_got, keep, got),
        "vvvv",
        "pair_sum",
        8,
    )
    parts = exchange(parts)
    (copies,) = call(
        peer_sum_kernel,
        [shaped(BF16, peers, 1024 // peers, 512)],
        "v",
        [],
        (parts,),
        "v",
        "peer_sum",
        8,
    )
    mine = exchange(copies).reshape(1024, 512)
    other = lax.ppermute(mine, "core", swap)
    weights = (block_qkv, block_out, grid_qkv, grid_out, mlp_in, mlp_out)
    signs = (*saved[7:9], *signs)
    outs = [shaped(F32, *weight.shape) for weight in weights]
    wides = [pltpu.VMEM((out.shape[0] // 2, out.shape[1]), F32) for out in outs]
    wides.append(pltpu.SemaphoreType.DMA((9,)))
    *halves, sums = call(
        finish_mine_kernel,
        outs + [shaped(F32, 8, 256)],
        "hhhhhhv",
        wides,
        (core, mine, *signs),
        "s" + "v" * 7,
        "finish_mine",
        16,
    )
    return call(
        finish_other_kernel,
        outs + [shaped(F32, 6)],
        "hhhhhhs",
        wides,
        (core, other, sums, *signs, *halves),
        "s" + "v" * 8 + "h" * 6,
        "finish_other",
        16,
        {9 + n: n for n in range(6)},
    )


def solution(mesh):
    fine = Mesh(mesh.devices.reshape(2, 4, 4, 2, 2), ("y_lo", "x", "z", "y_hi", "core"))
    placed = P(("y_lo", "x"), ("z", "y_hi", "core"), None)
    return jax.shard_map(
        body,
        mesh=fine,
        in_specs=(placed, placed) + (P(),) * 12,
        out_specs=(P(),) * 7,
        check_vma=False,
    )
```
